32 devices in a mesh: row: 8 (over z, x), col: 4 (over y, core).
Axes of the slice: x: 2, y: 2, z: 4, core: 2. Of those that a mesh axis runs over, the one named last changes fastest.
Arguments:
- cam_jac: float32 [128, 18, 512], P(('row', 'col')), may hold values from -1 to 1
- land_jac: float32 [128, 6, 512], P(('row', 'col')), may hold values from -5 to 5
- resid: float32 [128, 2, 512], P(('row', 'col')), may hold values from -20 to 20
- obs_cam: int32 [128, 512], P(('row', 'col')), may hold values from 0 to 127
- obs_land: int32 [128, 512], P(('row', 'col')), may hold values from 0 to 127
- pairs: int32 [128, 2], P(('row', 'col')), may hold values from 0 to 31, as said below
- cam_damp: float32 [18432], P(('row', 'col')), may hold values from 1 to 10
Outputs:
- cam_step: float32 [18432], P(('row', 'col'))
- land_step: float32 [128, 3, 128], P(('row', 'col'))
The draws below stay inside these ranges and needn't reach their ends.
Inputs may be any that keep to these rules, and one draw needn't show every extreme that they name: `pairs`: clusters are laid out device by device, 4 a device, devices in order of row, then col. A cluster held at grid row r and grid column c is seen by a first group in [r * 4, (r + 1) * 4) and a different second group in [c * 8, (c + 1) * 8).
All inputs are finite; a program needn't handle non-finite values.
Results may differ from the reference program's by a relative error of at most 0.0003.
Values sent between devices are 32-bit elements; how exact they have to be, the bound alone decides.
No kernel may reach another device: no remote copies, remote signals or barrier semaphores. Data moves between devices by JAX's collectives and lax.ppermute only.
A program may use at most 384 MiB of HBM per device.

```python
import math
import jax
import jax.numpy as jnp
from jax import lax

G = 32
CAM = 64
LM = 128
CL_DEV = 4
ITERS = 2
GW = 576
NS = 18432
OBS = 512
CL = 128
GROW = 4
GCOL = 8


def draw_pairs(key, part):
    cluster = jnp.arange(CL, dtype=jnp.int32)
    cols_count = G // GCOL
    grid_row = cluster // (CL_DEV * cols_count)
    grid_col = cluster // CL_DEV % cols_count
    key_first, key_free, key_skip = jax.random.split(key, 3)
    first = grid_row * GROW + jax.random.randint(key_first, (CL,), 0, GROW, dtype=jnp.int32)
    free_pick = jax.random.randint(key_free, (CL,), 0, GCOL, dtype=jnp.int32)
    skip_pick = jax.random.randint(key_skip, (CL,), 0, GCOL - 1, dtype=jnp.int32)
    within = first - grid_col * GCOL
    inside = (within >= 0) & (within < GCOL)
    skip_pick = skip_pick + (skip_pick >= within).astype(jnp.int32)
    second = grid_col * GCOL + jnp.where(inside, skip_pick, free_pick)
    return jnp.stack([first, second], axis=1).astype(jnp.int32)


def observe_indices(key):
    base_key = jax.random.fold_in(key, 101)
    key_landmark, key_offset = jax.random.split(base_key)
    landmark = jax.random.randint(key_landmark, (CL, OBS), 0, LM, dtype=jnp.int32)
    offset = jax.random.randint(key_offset, (CL, OBS), -3, 4, dtype=jnp.int32)
    center = landmark * (2 * CAM) // LM
    position = (center + offset) % (2 * CAM)
    camera = position % 2 * CAM + position // 2
    return (camera.astype(jnp.int32), landmark.astype(jnp.int32))


def signed_uniform(key, shape, lower, upper):
    key_signs, key_sizes = jax.random.split(key)
    signs = (jax.random.randint(key_signs, shape, 0, 2, dtype=jnp.int32) * 2 - 1).astype(jnp.float32)
    return signs * jax.random.uniform(key_sizes, shape, jnp.float32, lower, upper)


def cluster_floats(key):
    camera, landmark = observe_indices(key)
    subkeys = jax.random.split(jax.random.fold_in(key, 202), 9)
    cam_noise = jax.random.normal(subkeys[0], (CL, 18, OBS), jnp.float32)
    land_noise = jax.random.normal(subkeys[1], (CL, 6, OBS), jnp.float32)
    obs_noise = jax.random.normal(subkeys[2], (CL, 2, OBS), jnp.float32)
    amplitude = jax.random.uniform(subkeys[3], (CL, 9, 1), jnp.float32, 0.5, 1.5)
    cam_base = signed_uniform(subkeys[4], (CL, 18, 1), 0.2, 0.4)
    cam_jac = jnp.clip(cam_base + 0.06 * cam_noise, -1.0, 1.0)
    land_base = signed_uniform(subkeys[5], (CL, 6, 1), 1.5, 3.0)
    land_jac = jnp.clip(land_base + 0.3 * land_noise, -5.0, 5.0)
    angle_shift = jax.random.uniform(subkeys[6], (CL, 9, 1), jnp.float32, -math.pi, math.pi)
    place = (camera % CAM).astype(jnp.float32)[:, None, :]
    smooth_error = amplitude * jnp.cos(2.0 * math.pi * place / CAM + angle_shift)
    rough_table = 0.3 * jax.random.normal(subkeys[7], (CL, 9, 2 * CAM), jnp.float32)
    rough_error = jnp.take_along_axis(rough_table, jnp.broadcast_to(camera[:, None, :], (CL, 9, OBS)), axis=2)
    camera_error = smooth_error + rough_error
    point_table = 0.5 * jax.random.normal(subkeys[8], (CL, 3, LM), jnp.float32)
    point_error = jnp.take_along_axis(point_table, jnp.broadcast_to(landmark[:, None, :], (CL, 3, OBS)), axis=2)
    residual_rows = []
    for row_index in range(2):
        total_value = 0.3 * obs_noise[:, row_index]
        for param_index in range(9):
            total_value = total_value + cam_jac[:, row_index * 9 + param_index] * camera_error[:, param_index]
        for point_index in range(3):
            total_value = total_value + land_jac[:, row_index * 3 + point_index] * point_error[:, point_index]
        residual_rows.append(total_value)
    resid = jnp.clip(jnp.stack(residual_rows, axis=1), -20.0, 20.0)
    return (cam_jac, land_jac, resid)


def draw_obs_cam(key, part):
    return observe_indices(key)[0]


def draw_obs_land(key, part):
    return observe_indices(key)[1]


def draw_cam_jac(key, part):
    return cluster_floats(key)[0]


def draw_land_jac(key, part):
    return cluster_floats(key)[1]


def draw_resid(key, part):
    return cluster_floats(key)[2]


def levels(own_key, extent, cuts, least, top_value):
    def one(dim, parts):
        steps = jax.random.uniform(jax.random.fold_in(jax.random.fold_in(own_key, 6), dim), (parts,), jnp.float32, least / len(cuts), top_value / len(cuts))
        return jnp.repeat(jnp.exp(steps), extent[dim] // parts).reshape((-1,) + (1,) * (len(extent) - dim - 1))

    level = one(*cuts[0])
    for cut in cuts[1:]:
        level = level * one(*cut)
    return level


def setup_inputs(seed: int = 0) -> dict:
    streams_of = jax.random.split(jax.random.key(seed), 8)
    return {
        "cam_jac": draw_cam_jac(jax.random.fold_in(streams_of[7], 71), 0),
        "land_jac": draw_land_jac(jax.random.fold_in(streams_of[7], 71), 0),
        "resid": draw_resid(jax.random.fold_in(streams_of[7], 71), 0),
        "obs_cam": draw_obs_cam(jax.random.fold_in(streams_of[7], 71), 0),
        "obs_land": draw_obs_land(jax.random.fold_in(streams_of[7], 71), 0),
        "pairs": draw_pairs(jax.random.fold_in(streams_of[7], 71), 0),
        "cam_damp": jnp.clip(jnp.exp(math.log(10.0) - 2.3025851 * jax.random.uniform(streams_of[6], (NS,), jnp.float32) ** levels(streams_of[6], (NS,), ((0, 32),), -0.2, 0.2)), 1.0, 10.0),
    }


DAMPING = 1.0
HIGHEST = lax.Precision.HIGHEST

def cholesky_three(normal):
    root_first = jnp.sqrt(normal[0])
    inv_first = 1.0 / root_first
    low_one = normal[1] * inv_first
    low_two = normal[2] * inv_first
    inv_second = 1.0 / jnp.sqrt(normal[4] - low_one * low_one)
    low_three = (normal[5] - low_two * low_one) * inv_second
    inv_third = 1.0 / jnp.sqrt(normal[8] - low_two * low_two - low_three * low_three)
    return jnp.stack([inv_first, low_one, low_two, inv_second, low_three, inv_third])

def lower_solve(factor, first, second, third):
    out_one = first * factor[0]
    out_two = (second - factor[1] * out_one) * factor[3]
    out_three = (third - factor[2] * out_one - factor[4] * out_two) * factor[5]
    return jnp.stack([out_one, out_two, out_three])

def upper_solve(factor, first, second, third):
    out_three = third * factor[5]
    out_two = (second - factor[4] * out_three) * factor[3]
    out_one = (first - factor[1] * out_two - factor[2] * out_three) * factor[0]
    return jnp.stack([out_one, out_two, out_three])

def cluster_schur(cam_jac, land_jac, resid, obs_cam, obs_land):
    count = obs_cam.shape[0]
    width = CAM * 9
    cam_rows = cam_jac.reshape(2, 9, count)
    land_rows = land_jac.reshape(2, 3, count)
    coupled = cam_rows[0][:, None, :] * land_rows[0][None] + cam_rows[1][:, None, :] * land_rows[1][None]
    land_outer = (land_rows[0][:, None, :] * land_rows[0][None] + land_rows[1][:, None, :] * land_rows[1][None]).reshape(9, count)
    cam_outer = (cam_rows[0][:, None, :] * cam_rows[0][None] + cam_rows[1][:, None, :] * cam_rows[1][None]).reshape(81, count)
    cam_grad = cam_rows[0] * resid[0] + cam_rows[1] * resid[1]
    land_grad = land_rows[0] * resid[0] + land_rows[1] * resid[1]
    land_onehot = (obs_land[None, :] == jnp.arange(LM, dtype=jnp.int32)[:, None]).astype(jnp.float32)
    cam_onehot = (obs_cam[None, :] == jnp.arange(2 * CAM, dtype=jnp.int32)[:, None]).astype(jnp.float32)
    land_normal = jnp.dot(land_outer, land_onehot.T, precision=HIGHEST) + DAMPING * jnp.eye(3, dtype=jnp.float32).reshape(9, 1)
    land_total = jnp.dot(land_grad, land_onehot.T, precision=HIGHEST)
    cam_normal = jnp.dot(cam_outer, cam_onehot.T, precision=HIGHEST)
    cam_total = jnp.dot(cam_grad, cam_onehot.T, precision=HIGHEST)
    factor = cholesky_three(land_normal)
    obs_factor = jnp.take(factor, obs_land, axis=1)
    solved = jnp.stack([lower_solve(obs_factor, coupled[param, 0], coupled[param, 1], coupled[param, 2]) for param in range(9)])
    row_index = obs_cam[None, None, :] * 9 + jnp.arange(9, dtype=jnp.int32)[:, None, None]
    col_index = jnp.arange(3, dtype=jnp.int32)[None, :, None] * LM + obs_land[None, None, :]
    coupling = jnp.zeros((2 * width, 3 * LM), jnp.float32).at[row_index, col_index].add(solved)
    tvector = lower_solve(factor, land_total[0], land_total[1], land_total[2]).reshape(3 * LM)
    blocks = cam_normal.T.reshape(2, CAM, 9, 9)
    eye_cam = jnp.eye(CAM, dtype=jnp.float32)
    upper_first = (eye_cam[:, None, :, None] * blocks[0][:, :, None, :]).reshape(width, width)
    upper_second = (eye_cam[:, None, :, None] * blocks[1][:, :, None, :]).reshape(width, width)
    coupling_first = coupling[:width]
    coupling_second = coupling[width:]
    diag_first = upper_first - jnp.dot(coupling_first, coupling_first.T, precision=HIGHEST)
    cross = -jnp.dot(coupling_first, coupling_second.T, precision=HIGHEST)
    diag_second = upper_second - jnp.dot(coupling_second, coupling_second.T, precision=HIGHEST)
    right = -cam_total.T.reshape(2 * width) + jnp.dot(coupling, tvector, precision=HIGHEST)
    return (diag_first, cross, diag_second, right[:width], right[width:], coupling, tvector, factor)

def reference(cam_jac, land_jac, resid, obs_cam, obs_land, pairs, cam_damp):
    width = GW

    def accumulate(carry, items):
        diag_blocks, right_groups = carry
        jac_cam, jac_land, residual, cams, lands, pair = items
        diag_first, cross, diag_second, right_first, right_second, coupling, tvector, factor = cluster_schur(jac_cam, jac_land, residual, cams, lands)
        diag_blocks = diag_blocks.at[pair[0]].add(diag_first).at[pair[1]].add(diag_second)
        right_groups = right_groups.at[pair[0]].add(right_first).at[pair[1]].add(right_second)
        return ((diag_blocks, right_groups), cross)
    start = (jnp.zeros((G, width, width), jnp.float32), jnp.zeros((G, width), jnp.float32))
    (diag_blocks, right_groups), cross_blocks = lax.scan(accumulate, start, (cam_jac, land_jac, resid, obs_cam, obs_land, pairs))
    precond = 1.0 / (jnp.diagonal(diag_blocks, axis1=1, axis2=2).reshape(NS) + cam_damp)

    def apply_system(vector):
        groups = vector.reshape(G, width)
        image = jnp.einsum('gij,gj->gi', diag_blocks, groups, precision=HIGHEST)

        def add_pair(total, items):
            block, pair = items
            total = total.at[pair[0]].add(jnp.dot(block, groups[pair[1]], precision=HIGHEST))
            total = total.at[pair[1]].add(jnp.dot(groups[pair[0]], block, precision=HIGHEST))
            return (total, None)
        image, unused = lax.scan(add_pair, image, (cross_blocks, pairs))
        return image.reshape(NS) + cam_damp * vector
    solution = jnp.zeros((NS,), jnp.float32)
    residual = right_groups.reshape(NS)
    precon_res = precond * residual
    direction = precon_res
    norm_now = jnp.sum(residual * precon_res)
    for step in range(ITERS):
        image = apply_system(direction)
        alpha = norm_now / jnp.sum(direction * image)
        solution = solution + alpha * direction
        residual = residual - alpha * image
        if step + 1 < ITERS:
            precon_res = precond * residual
            norm_next = jnp.sum(residual * precon_res)
            direction = precon_res + norm_next / norm_now * direction
            norm_now = norm_next

    def landmark(items):
        jac_cam, jac_land, residual_obs, cams, lands, pair = items
        outputs = cluster_schur(jac_cam, jac_land, residual_obs, cams, lands)
        coupling, tvector, factor = (outputs[5], outputs[6], outputs[7])
        first_part = lax.dynamic_slice_in_dim(solution, (pair[0] * width).astype(jnp.int32), width)
        second_part = lax.dynamic_slice_in_dim(solution, (pair[1] * width).astype(jnp.int32), width)
        camera_part = jnp.concatenate([first_part, second_part])
        summed = (tvector + jnp.dot(camera_part, coupling, precision=HIGHEST)).reshape(3, LM)
        return -upper_solve(factor, summed[0], summed[1], summed[2])
    land_step = lax.map(landmark, (cam_jac, land_jac, resid, obs_cam, obs_land, pairs))
    return (solution, land_step)
```

```python
import functools

import jax
import jax.numpy as jnp
from jax import lax
from jax.experimental import pallas as pl
from jax.experimental.pallas import tpu as pltpu
from jax.sharding import PartitionSpec as P

CAM = 64
LM = 128
LANES = 128
AXES = ("row", "col")
DAMPING = 1.0

NN = (((1,), (0,)), ((), ()))
NT = (((1,), (1,)), ((), ()))


def split3(x):
    hi = x.astype(jnp.bfloat16)
    rest = x - hi.astype(jnp.float32)
    mid = rest.astype(jnp.bfloat16)
    low = (rest - mid.astype(jnp.float32)).astype(jnp.bfloat16)
    return jnp.concatenate([hi, mid, low], axis=0)


def dot3(x, exact, dims):
    n = x.shape[0]
    y = lax.dot_general(split3(x), exact, dims, preferred_element_type=jnp.float32)
    return (y[2 * n :] + y[n : 2 * n]) + y[:n]


def onehot(index_row, size):
    ids = lax.broadcasted_iota(jnp.int32, (size, index_row.shape[1]), 0)
    return jnp.where(ids == index_row, 1.0, 0.0).astype(jnp.bfloat16)


def pad_rows(x, rows):
    return jnp.concatenate([x, jnp.zeros((rows - x.shape[0], x.shape[1]), x.dtype)], axis=0)


def stack_rows(rows, total):
    rows = list(rows)
    rows.append(jnp.zeros((total - len(rows), rows[0].shape[1]), jnp.float32))
    return jnp.concatenate(rows, axis=0)


def cholesky_three(v00, v01, v02, v11, v12, v22):
    inv_first = 1.0 / jnp.sqrt(v00)
    low_one = v01 * inv_first
    low_two = v02 * inv_first
    inv_second = 1.0 / jnp.sqrt(v11 - low_one * low_one)
    low_three = (v12 - low_two * low_one) * inv_second
    inv_third = 1.0 / jnp.sqrt(v22 - low_two * low_two - low_three * low_three)
    return (inv_first, low_one, low_two, inv_second, low_three, inv_third)


def lower_solve(factor, first, second, third):
    out_one = first * factor[0]
    out_two = (second - factor[1] * out_one) * factor[3]
    out_three = (third - factor[2] * out_one - factor[4] * out_two) * factor[5]
    return (out_one, out_two, out_three)


def upper_solve(factor, first, second, third):
    out_three = third * factor[5]
    out_two = (second - factor[4] * out_three) * factor[3]
    out_one = (first - factor[1] * out_two - factor[2] * out_three) * factor[0]
    return (out_one, out_two, out_three)


def row_list(x, count):
    return [x[i : i + 1] for i in range(count)]


def lane_ids(rows):
    return lax.broadcasted_iota(jnp.int32, (rows, LANES), 1)


def to_first(x, half):
    return pltpu.roll(x, half * CAM, 1)


def to_second(x, half):
    return pltpu.roll(x, (1 - half) * CAM, 1)


def load_tile(ref, tiles, t):
    ninth = ref[tiles + t // 8, pl.ds(t % 8, 1), :]
    return jnp.concatenate([ref[t], ninth, jnp.zeros((7, LANES), jnp.float32)], axis=0)


def add_tile(ref, tiles, t, value):
    ref[t] += value[:8]
    ref[tiles + t // 8, pl.ds(t % 8, 1), :] += value[8:9]


def shard_select(shard, lane_offset):
    entry = lax.broadcasted_iota(jnp.int32, (shard, LANES), 0)
    start = 9 * (lax.broadcasted_iota(jnp.int32, (shard, LANES), 1) - lane_offset)
    inside = (entry >= start) & (entry < start + 9)
    return jnp.where(inside, 1.0, 0.0).astype(jnp.bfloat16)


def param_mask(shard):
    entry = lax.broadcasted_iota(jnp.int32, (16, shard), 1).astype(jnp.float32)
    camera = jnp.floor((entry + 0.5) * (1.0 / 9.0))
    param = entry - 9.0 * camera
    return param == lax.broadcasted_iota(jnp.int32, (16, shard), 0).astype(jnp.float32)


def place(pairs_ref, k, n_row, n_col, groups):
    first = pairs_ref[k, 0] - lax.axis_index("row") * (groups // n_row)
    second = pairs_ref[k, 1] - lax.axis_index("col") * (groups // n_col)
    return first // 2, first % 2, second // 2, second % 2


def scatter_pair(value, ref, tiles, row_tiles, spot):
    t_first, h_first, t_second, h_second = spot
    lower = lane_ids(value.shape[0]) < CAM
    add_tile(ref, tiles, t_first, to_first(jnp.where(lower, value, 0.0), h_first))
    add_tile(ref, tiles, row_tiles + t_second, to_second(jnp.where(lower, 0.0, value), h_second))


def own_place(n_row, n_col, cams):
    shard_cams = cams // (n_row * n_col)
    start = lax.axis_index("col") * shard_cams
    return start // LANES, start % LANES


def build_kernel(n_row, n_col, cams, pairs_ref, cam_ref, land_ref, resid_ref, ocam_ref, oland_ref, damp_ref, part_ref, m_ref, fac_ref, damp_tile_ref):
    groups = cams // CAM
    row_tiles = cams // n_row // LANES
    tiles = row_tiles + cams // n_col // LANES
    count = cam_ref.shape[0]
    obs = cam_ref.shape[2]
    shard = damp_ref.shape[1]
    part_ref[...] = jnp.zeros(part_ref.shape, jnp.float32)
    rhs_ref, diag_ref = part_ref.at[0], part_ref.at[1]

    own_tile, own_lane = own_place(n_row, n_col, cams)
    spread = jnp.where(param_mask(shard), damp_ref[...], 0.0)
    damp_tile = dot3(spread, shard_select(shard, own_lane), NN)
    damp_tile_ref[...] = damp_tile
    add_tile(diag_ref, tiles, own_tile, damp_tile)

    key = ocam_ref[...] * LM + oland_ref[...]
    key = jnp.concatenate([key.astype(jnp.float32), jnp.full((8 - count, obs), -1.0, jnp.float32)], axis=0)
    key_t = jnp.transpose(key)

    for k in range(count):
        cam_hot = onehot(ocam_ref[k : k + 1, :], 2 * CAM)
        land_hot = onehot(oland_ref[k : k + 1, :], LM)
        lj = [land_ref[k, i : i + 1, :] for i in range(6)]
        e0, e1 = resid_ref[k, 0:1, :], resid_ref[k, 1:2, :]

        def outer(i, j):
            return lj[i] * lj[j] + lj[3 + i] * lj[3 + j]

        entries = [outer(0, 0), outer(0, 1), outer(0, 2), outer(1, 1), outer(1, 2), outer(2, 2)]
        entries += [lj[b] * e0 + lj[3 + b] * e1 for b in range(3)]
        sums = row_list(dot3(stack_rows(entries, 16), land_hot, NT), 9)
        factor = cholesky_three(
            sums[0] + DAMPING, sums[1], sums[2], sums[3] + DAMPING, sums[4], sums[5] + DAMPING
        )
        tvec = lower_solve(factor, sums[6], sums[7], sums[8])
        land_values = stack_rows(list(factor) + list(tvec), 16)
        fac_ref[k] = land_values
        at_obs = row_list(dot3(land_values, land_hot, NN), 9)
        m0 = lower_solve(at_obs, lj[0], lj[1], lj[2])
        m1 = lower_solve(at_obs, lj[3], lj[4], lj[5])
        m_ref[k] = stack_rows(m0 + m1, 8)
        w0 = m0[0] * at_obs[6] + m0[1] * at_obs[7] + m0[2] * at_obs[8] - e0
        w1 = m1[0] * at_obs[6] + m1[1] * at_obs[7] + m1[2] * at_obs[8] - e1
        j0 = pad_rows(cam_ref[k, 0:9, :], 16)
        j1 = pad_rows(cam_ref[k, 9:18, :], 16)
        rhs = j0 * w0 + j1 * w1
        coupled = jnp.concatenate([j0 * m0[b] + j1 * m1[b] for b in range(3)], axis=0)
        same = jnp.where(key_t[:, k : k + 1] == key[k : k + 1, :], 1.0, 0.0).astype(jnp.bfloat16)
        prod = coupled * dot3(coupled, same, NN)
        diag = j0 * j0 + j1 * j1 - (prod[0:16] + prod[16:32] + prod[32:48])
        both = dot3(jnp.concatenate([rhs, diag], axis=0), cam_hot, NT)
        spot = place(pairs_ref, k, n_row, n_col, groups)
        scatter_pair(both[:16], rhs_ref, tiles, row_tiles, spot)
        scatter_pair(both[16:], diag_ref, tiles, row_tiles, spot)


def half_product(k, p_ref, pairs_ref, cam_ref, ocam_ref, oland_ref, m_ref):
    cams_tiles = p_ref.shape[0] * 8 // 9
    first, second = pairs_ref[k, 0], pairs_ref[k, 1]
    p_first = to_first(load_tile(p_ref, cams_tiles, first // 2), first % 2)
    p_second = to_second(load_tile(p_ref, cams_tiles, second // 2), second % 2)
    p_here = jnp.where(lane_ids(16) < CAM, p_first, p_second)
    cam_hot = onehot(ocam_ref[k : k + 1, :], 2 * CAM)
    land_hot = onehot(oland_ref[k : k + 1, :], LM)
    at_obs = dot3(p_here, cam_hot, NN)[:9]
    u0 = jnp.sum(cam_ref[k, 0:9, :] * at_obs, axis=0, keepdims=True)
    u1 = jnp.sum(cam_ref[k, 9:18, :] * at_obs, axis=0, keepdims=True)
    m = [m_ref[k, i : i + 1, :] for i in range(6)]
    y = [m[b] * u0 + m[3 + b] * u1 for b in range(3)]
    y_land = dot3(stack_rows(y, 16), land_hot, NT)
    return cam_hot, land_hot, u0, u1, m, y_land


def first_kernel(n_row, n_col, cams, pairs_ref, sums_ref, cam_ref, ocam_ref, oland_ref, m_ref, fac_ref, damp_tile_ref, part_ref, back_ref, p_ref):
    groups = cams // CAM
    row_tiles = cams // n_row // LANES
    tiles = row_tiles + cams // n_col // LANES
    count = cam_ref.shape[0]
    p_ref[...] = sums_ref[0] * (1.0 / sums_ref[1])
    part_ref[...] = jnp.zeros(part_ref.shape, jnp.float32)
    own_tile, _ = own_place(n_row, n_col, cams)
    whole_tile = lax.axis_index("row") * row_tiles + own_tile
    own = load_tile(p_ref, cams // LANES, whole_tile)
    add_tile(part_ref, tiles, own_tile, own * damp_tile_ref[...])
    for k in range(count):
        cam_hot, land_hot, u0, u1, m, y_land = half_product(k, p_ref, pairs_ref, cam_ref, ocam_ref, oland_ref, m_ref)
        factor = row_list(fac_ref[k], 9)
        solved = upper_solve(factor, y_land[0:1], y_land[1:2], y_land[2:3])
        from_t = upper_solve(factor, factor[6], factor[7], factor[8])
        back_ref[k] = stack_rows(solved + from_t, 8)
        y_obs = row_list(dot3(y_land, land_hot, NN), 3)
        v0 = u0 - (m[0] * y_obs[0] + m[1] * y_obs[1] + m[2] * y_obs[2])
        v1 = u1 - (m[3] * y_obs[0] + m[4] * y_obs[1] + m[5] * y_obs[2])
        image = pad_rows(cam_ref[k, 0:9, :] * v0 + cam_ref[k, 9:18, :] * v1, 16)
        image = dot3(image, cam_hot, NT)
        scatter_pair(image, part_ref, tiles, row_tiles, place(pairs_ref, k, n_row, n_col, groups))


def total_sum(x):
    x = jnp.sum(x, axis=0)
    return jnp.sum(jnp.sum(x, axis=0, keepdims=True), axis=1, keepdims=True)


def second_kernel(n_row, n_col, cams, pairs_ref, sums_ref, image_ref, cam_ref, ocam_ref, oland_ref, m_ref, fac_ref, damp_tile_ref, back_ref, energy_ref, cam_out_ref, land_base_ref, land_slope_ref, p_ref, d_ref):
    row_tiles = cams // n_row // LANES
    count = cam_ref.shape[0]
    shard = cam_out_ref.shape[1]
    right, image = sums_ref[0], image_ref[...]
    precond = 1.0 / sums_ref[1]
    start = right * precond
    norm_now = total_sum(right * start)
    alpha = norm_now / total_sum(start * image)
    residual = right - alpha * image
    precon_res = precond * residual
    norm_next = total_sum(residual * precon_res)
    p_ref[...] = start
    d_ref[...] = precon_res + norm_next / norm_now * start

    own_tile, own_lane = own_place(n_row, n_col, cams)
    whole_tile = lax.axis_index("row") * row_tiles + own_tile
    own_first = load_tile(p_ref, cams // LANES, whole_tile)
    own_second = load_tile(d_ref, cams // LANES, whole_tile)
    energy = own_second * own_second * damp_tile_ref[...]
    energy = jnp.sum(jnp.sum(energy, axis=0, keepdims=True), axis=1, keepdims=True)

    select = shard_select(shard, own_lane)
    mask = param_mask(shard)
    flat = dot3(jnp.concatenate([own_first, own_second], axis=0), select, NT)
    flat_first = jnp.sum(jnp.where(mask, flat[:16], 0.0), axis=0, keepdims=True)
    flat_second = jnp.sum(jnp.where(mask, flat[16:], 0.0), axis=0, keepdims=True)
    cam_out_ref[0:1, :] = alpha * flat_first
    cam_out_ref[1:2, :] = norm_next * flat_second

    for k in range(count):
        _, land_hot, u0, u1, m, y_land = half_product(k, d_ref, pairs_ref, cam_ref, ocam_ref, oland_ref, m_ref)
        factor = row_list(fac_ref[k], 9)
        solved = upper_solve(factor, y_land[0:1], y_land[1:2], y_land[2:3])
        for b in range(3):
            land_base_ref[k, b : b + 1, :] = -(back_ref[k, 3 + b : 4 + b, :] + alpha * back_ref[k, b : b + 1, :])
            land_slope_ref[k, b : b + 1, :] = -norm_next * solved[b]
        y_obs = row_list(dot3(y_land, land_hot, NN), 3)
        v0 = u0 - (m[0] * y_obs[0] + m[1] * y_obs[1] + m[2] * y_obs[2])
        v1 = u1 - (m[3] * y_obs[0] + m[4] * y_obs[1] + m[5] * y_obs[2])
        energy = energy + jnp.sum(u0 * v0 + u1 * v1, axis=1, keepdims=True)
    energy_ref[...] = jnp.broadcast_to(energy, energy_ref.shape)


def hyper(x, n_row, n_col):
    n = n_row * n_col
    bit = 1
    while bit < n:
        x = x + lax.ppermute(x, AXES, [(i, i ^ bit) for i in range(n)])
        bit *= 2
    return x


def per_device(n_row, n_col, cam_jac, land_jac, resid, obs_cam, obs_land, pairs, cam_damp):
    f32 = jnp.float32
    count, _, obs = cam_jac.shape
    shard = cam_damp.shape[0]
    n_dev = n_row * n_col
    cams = shard * n_dev // 9
    row_tiles = cams // n_row // LANES
    tiles = row_tiles + cams // n_col // LANES
    part_tiles = tiles + (tiles + 7) // 8
    whole_tiles = cams // LANES
    whole_packed = whole_tiles + (whole_tiles + 7) // 8
    vmem = pl.BlockSpec(memory_space=pltpu.VMEM)
    smem = pl.BlockSpec(memory_space=pltpu.SMEM)

    def shape(*dims):
        return jax.ShapeDtypeStruct(dims, f32)

    part, m, fac, damp_tile = pl.pallas_call(
        functools.partial(build_kernel, n_row, n_col, cams),
        out_shape=(shape(2, part_tiles, 8, LANES), shape(count, 8, obs), shape(count, 16, LM), shape(16, LANES)),
        in_specs=[smem] + [vmem] * 6,
        out_specs=(vmem,) * 4,
    )(pairs, cam_jac, land_jac, resid, obs_cam, obs_land, cam_damp.reshape(1, shard))

    def expand(x):
        whole = jnp.zeros((whole_packed, 8, LANES), f32)

        def put(whole, lo, hi, start):
            old = lax.dynamic_slice_in_dim(whole, start, hi - lo, 0)
            return lax.dynamic_update_slice_in_dim(whole, old + x[lo:hi], start, 0)

        whole = put(whole, 0, row_tiles, lax.axis_index("row") * row_tiles)
        whole = put(whole, row_tiles, tiles, lax.axis_index("col") * (tiles - row_tiles))
        ninth = jnp.zeros((whole_tiles, LANES), f32)
        flat = x[tiles:].reshape(-1, LANES)
        for lo, hi, start in (
            (0, row_tiles, lax.axis_index("row") * row_tiles),
            (row_tiles, tiles, lax.axis_index("col") * (tiles - row_tiles)),
        ):
            old = lax.dynamic_slice_in_dim(ninth, start, hi - lo, 0)
            ninth = lax.dynamic_update_slice_in_dim(ninth, old + flat[lo:hi], start, 0)
        ninth = ninth.reshape(-1, 8, LANES)
        return lax.dynamic_update_slice_in_dim(whole, ninth, whole_tiles, 0)

    sums = hyper(jnp.stack([expand(part[0]), expand(part[1])]), n_row, n_col)

    image, back = pl.pallas_call(
        functools.partial(first_kernel, n_row, n_col, cams),
        out_shape=(shape(part_tiles, 8, LANES), shape(count, 8, LM)),
        in_specs=[smem] + [vmem] * 7,
        out_specs=(vmem,) * 2,
        scratch_shapes=[pltpu.VMEM((whole_packed, 8, LANES), f32)],
    )(pairs, sums, cam_jac, obs_cam, obs_land, m, fac, damp_tile)

    image = hyper(expand(image), n_row, n_col)

    energy, cam_out, land_base, land_slope = pl.pallas_call(
        functools.partial(second_kernel, n_row, n_col, cams),
        out_shape=(shape(8, LANES), shape(2, shard), shape(count, 3, LM), shape(count, 3, LM)),
        in_specs=[smem] + [vmem] * 9,
        out_specs=(vmem,) * 4,
        scratch_shapes=[pltpu.VMEM((whole_packed, 8, LANES), f32)] * 2,
    )(pairs, sums, image, cam_jac, obs_cam, obs_land, m, fac, damp_tile, back)

    spread = jnp.broadcast_to(energy[0:1][None], (n_dev, 1, LANES))
    gathered = lax.all_to_all(spread, AXES, 0, 0, tiled=True)
    inverse = 1.0 / jnp.sum(gathered, axis=0)[0, 0]
    return cam_out[0] + inverse * cam_out[1], land_base + inverse * land_slope


def solution(mesh):
    n_row, n_col = mesh.shape["row"], mesh.shape["col"]
    both = P(AXES)
    in_specs = (P(AXES, None, None),) * 3 + (P(AXES, None),) * 3 + (both,)
    out_specs = (both, P(AXES, None, None))
    return jax.shard_map(
        functools.partial(per_device, n_row, n_col),
        mesh=mesh,
        in_specs=in_specs,
        out_specs=out_specs,
        check_vma=False,
    )
```

```python
import functools

import jax
import jax.numpy as jnp
from jax import lax
from jax.experimental import pallas as pl
from jax.experimental.pallas import tpu as pltpu
from jax.sharding import PartitionSpec as P

CAM = 64
LM = 128
LANES = 128
AXES = ("row", "col")
DAMPING = 1.0

NN = (((1,), (0,)), ((), ()))
NT = (((1,), (1,)), ((), ()))


def split3(x):
    hi = x.astype(jnp.bfloat16)
    rest = x - hi.astype(jnp.float32)
    mid = rest.astype(jnp.bfloat16)
    low = (rest - mid.astype(jnp.float32)).astype(jnp.bfloat16)
    return jnp.concatenate([hi, mid, low], axis=0)


def dot3(x, exact, dims):
    n = x.shape[0]
    y = lax.dot_general(split3(x), exact, dims, preferred_element_type=jnp.float32)
    return (y[2 * n :] + y[n : 2 * n]) + y[:n]


def onehot(index_row, size):
    ids = lax.broadcasted_iota(jnp.int32, (size, index_row.shape[1]), 0)
    return jnp.where(ids == index_row, 1.0, 0.0).astype(jnp.bfloat16)


def pad_rows(x, rows):
    return jnp.concatenate([x, jnp.zeros((rows - x.shape[0], x.shape[1]), x.dtype)], axis=0)


def stack_rows(rows, total):
    rows = list(rows)
    rows.append(jnp.zeros((total - len(rows), rows[0].shape[1]), jnp.float32))
    return jnp.concatenate(rows, axis=0)


def cholesky_three(v00, v01, v02, v11, v12, v22):
    inv_first = 1.0 / jnp.sqrt(v00)
    low_one = v01 * inv_first
    low_two = v02 * inv_first
    inv_second = 1.0 / jnp.sqrt(v11 - low_one * low_one)
    low_three = (v12 - low_two * low_one) * inv_second
    inv_third = 1.0 / jnp.sqrt(v22 - low_two * low_two - low_three * low_three)
    return (inv_first, low_one, low_two, inv_second, low_three, inv_third)


def lower_solve(factor, first, second, third):
    out_one = first * factor[0]
    out_two = (second - factor[1] * out_one) * factor[3]
    out_three = (third - factor[2] * out_one - factor[4] * out_two) * factor[5]
    return (out_one, out_two, out_three)


def upper_solve(factor, first, second, third):
    out_three = third * factor[5]
    out_two = (second - factor[4] * out_three) * factor[3]
    out_one = (first - factor[1] * out_two - factor[2] * out_three) * factor[0]
    return (out_one, out_two, out_three)


def row_list(x, count):
    return [x[i : i + 1] for i in range(count)]


def lane_ids(rows):
    return lax.broadcasted_iota(jnp.int32, (rows, LANES), 1)


def to_first(x, half):
    return pltpu.roll(x, half * CAM, 1)


def to_second(x, half):
    return pltpu.roll(x, (1 - half) * CAM, 1)


def load_tile(ref, tiles, t):
    ninth = ref[tiles + t // 8, pl.ds(t % 8, 1), :]
    return jnp.concatenate([ref[t], ninth, jnp.zeros((7, LANES), jnp.float32)], axis=0)


def add_tile(ref, tiles, t, value):
    ref[t] += value[:8]
    ref[tiles + t // 8, pl.ds(t % 8, 1), :] += value[8:9]


def shard_select(shard, lane_offset):
    entry = lax.broadcasted_iota(jnp.int32, (shard, LANES), 0)
    start = 9 * (lax.broadcasted_iota(jnp.int32, (shard, LANES), 1) - lane_offset)
    inside = (entry >= start) & (entry < start + 9)
    return jnp.where(inside, 1.0, 0.0).astype(jnp.bfloat16)


def param_mask(shard):
    entry = lax.broadcasted_iota(jnp.int32, (16, shard), 1).astype(jnp.float32)
    camera = jnp.floor((entry + 0.5) * (1.0 / 9.0))
    param = entry - 9.0 * camera
    return param == lax.broadcasted_iota(jnp.int32, (16, shard), 0).astype(jnp.float32)


def place(pairs_ref, k, n_row, n_col, groups):
    first = pairs_ref[0, k] - lax.axis_index("row") * (groups // n_row)
    second = pairs_ref[1, k] - lax.axis_index("col") * (groups // n_col)
    return first // 2, first % 2, second // 2, second % 2


def scatter_pair(value, ref, tiles, row_tiles, spot):
    t_first, h_first, t_second, h_second = spot
    lower = lane_ids(value.shape[0]) < CAM
    add_tile(ref, tiles, t_first, to_first(jnp.where(lower, value, 0.0), h_first))
    add_tile(ref, tiles, row_tiles + t_second, to_second(jnp.where(lower, 0.0, value), h_second))


def own_place(n_row, n_col, cams):
    shard_cams = cams // (n_row * n_col)
    start = lax.axis_index("col") * shard_cams
    return start // LANES, start % LANES


def build_kernel(n_row, n_col, cams, pairs_ref, cam_ref, land_ref, resid_ref, ocam_ref, oland_ref, damp_ref, part_ref, jac_ref, m_ref, fac_ref, damp_tile_ref):
    groups = cams // CAM
    row_tiles = cams // n_row // LANES
    tiles = row_tiles + cams // n_col // LANES
    count, obs = ocam_ref.shape
    shard = damp_ref.shape[1]
    part_ref[...] = jnp.zeros(part_ref.shape, jnp.float32)
    rhs_ref, diag_ref = part_ref.at[0], part_ref.at[1]

    own_tile, own_lane = own_place(n_row, n_col, cams)
    spread = jnp.where(param_mask(shard), damp_ref[...], 0.0)
    damp_tile = dot3(spread, shard_select(shard, own_lane), NN)
    damp_tile_ref[...] = damp_tile
    add_tile(diag_ref, tiles, own_tile, damp_tile)

    key = ocam_ref[...] * LM + oland_ref[...]
    key = jnp.concatenate([key.astype(jnp.float32), jnp.full((8 - count, obs), -1.0, jnp.float32)], axis=0)
    key_t = jnp.transpose(key)

    for k in range(count):
        cam_hot = onehot(ocam_ref[k : k + 1, :], 2 * CAM)
        land_hot = onehot(oland_ref[k : k + 1, :], LM)
        lj = [land_ref[i, k : k + 1, :] for i in range(6)]
        e0, e1 = resid_ref[0, k : k + 1, :], resid_ref[1, k : k + 1, :]

        def outer(i, j):
            return lj[i] * lj[j] + lj[3 + i] * lj[3 + j]

        entries = [outer(0, 0), outer(0, 1), outer(0, 2), outer(1, 1), outer(1, 2), outer(2, 2)]
        entries += [lj[b] * e0 + lj[3 + b] * e1 for b in range(3)]
        sums = row_list(dot3(stack_rows(entries, 16), land_hot, NT), 9)
        factor = cholesky_three(
            sums[0] + DAMPING, sums[1], sums[2], sums[3] + DAMPING, sums[4], sums[5] + DAMPING
        )
        tvec = lower_solve(factor, sums[6], sums[7], sums[8])
        land_values = stack_rows(list(factor) + list(tvec), 16)
        fac_ref[k] = land_values
        at_obs = row_list(dot3(land_values, land_hot, NN), 9)
        m0 = lower_solve(at_obs, lj[0], lj[1], lj[2])
        m1 = lower_solve(at_obs, lj[3], lj[4], lj[5])
        m_ref[k] = stack_rows(m0 + m1, 8)
        w0 = m0[0] * at_obs[6] + m0[1] * at_obs[7] + m0[2] * at_obs[8] - e0
        w1 = m1[0] * at_obs[6] + m1[1] * at_obs[7] + m1[2] * at_obs[8] - e1
        j0 = pad_rows(cam_ref[0:9, k, :], 16)
        j1 = pad_rows(cam_ref[9:18, k, :], 16)
        jac_ref[k, 0] = j0
        jac_ref[k, 1] = j1
        rhs = j0 * w0 + j1 * w1
        coupled = jnp.concatenate([j0 * m0[b] + j1 * m1[b] for b in range(3)], axis=0)
        same = jnp.where(key_t[:, k : k + 1] == key[k : k + 1, :], 1.0, 0.0).astype(jnp.bfloat16)
        prod = coupled * dot3(coupled, same, NN)
        diag = j0 * j0 + j1 * j1 - (prod[0:16] + prod[16:32] + prod[32:48])
        both = dot3(jnp.concatenate([rhs, diag], axis=0), cam_hot, NT)
        spot = place(pairs_ref, k, n_row, n_col, groups)
        scatter_pair(both[:16], rhs_ref, tiles, row_tiles, spot)
        scatter_pair(both[16:], diag_ref, tiles, row_tiles, spot)


def half_product(k, p_ref, pairs_ref, jac_ref, ocam_ref, oland_ref, m_ref):
    cams_tiles = p_ref.shape[0] * 8 // 9
    first, second = pairs_ref[0, k], pairs_ref[1, k]
    p_first = to_first(load_tile(p_ref, cams_tiles, first // 2), first % 2)
    p_second = to_second(load_tile(p_ref, cams_tiles, second // 2), second % 2)
    p_here = jnp.where(lane_ids(16) < CAM, p_first, p_second)
    cam_hot = onehot(ocam_ref[k : k + 1, :], 2 * CAM)
    land_hot = onehot(oland_ref[k : k + 1, :], LM)
    at_obs = dot3(p_here, cam_hot, NN)
    u0 = jnp.sum(jac_ref[k, 0] * at_obs, axis=0, keepdims=True)
    u1 = jnp.sum(jac_ref[k, 1] * at_obs, axis=0, keepdims=True)
    m = [m_ref[k, i : i + 1, :] for i in range(6)]
    y = [m[b] * u0 + m[3 + b] * u1 for b in range(3)]
    y_land = dot3(stack_rows(y, 16), land_hot, NT)
    return cam_hot, land_hot, u0, u1, m, y_land


def first_kernel(n_row, n_col, cams, pairs_ref, sums_ref, jac_ref, ocam_ref, oland_ref, m_ref, fac_ref, damp_tile_ref, parts_ref, back_ref, p_ref):
    part_ref = parts_ref.at[0]
    groups = cams // CAM
    row_tiles = cams // n_row // LANES
    tiles = row_tiles + cams // n_col // LANES
    count = jac_ref.shape[0]
    p_ref[...] = sums_ref[0] * (1.0 / sums_ref[1])
    part_ref[...] = jnp.zeros(part_ref.shape, jnp.float32)
    own_tile, _ = own_place(n_row, n_col, cams)
    whole_tile = lax.axis_index("row") * row_tiles + own_tile
    own = load_tile(p_ref, cams // LANES, whole_tile)
    add_tile(part_ref, tiles, own_tile, own * damp_tile_ref[...])
    for k in range(count):
        cam_hot, land_hot, u0, u1, m, y_land = half_product(k, p_ref, pairs_ref, jac_ref, ocam_ref, oland_ref, m_ref)
        factor = row_list(fac_ref[k], 9)
        solved = upper_solve(factor, y_land[0:1], y_land[1:2], y_land[2:3])
        from_t = upper_solve(factor, factor[6], factor[7], factor[8])
        back_ref[k] = stack_rows(solved + from_t, 8)
        y_obs = row_list(dot3(y_land, land_hot, NN), 3)
        v0 = u0 - (m[0] * y_obs[0] + m[1] * y_obs[1] + m[2] * y_obs[2])
        v1 = u1 - (m[3] * y_obs[0] + m[4] * y_obs[1] + m[5] * y_obs[2])
        image = jac_ref[k, 0] * v0 + jac_ref[k, 1] * v1
        image = dot3(image, cam_hot, NT)
        scatter_pair(image, part_ref, tiles, row_tiles, place(pairs_ref, k, n_row, n_col, groups))


def total_sum(x):
    x = jnp.sum(x, axis=0)
    return jnp.sum(jnp.sum(x, axis=0, keepdims=True), axis=1, keepdims=True)


def second_kernel(n_row, n_col, cams, pairs_ref, sums_ref, image_ref, jac_ref, ocam_ref, oland_ref, m_ref, fac_ref, damp_tile_ref, back_ref, energy_ref, cam_out_ref, land_base_ref, land_slope_ref, p_ref, d_ref):
    row_tiles = cams // n_row // LANES
    count = jac_ref.shape[0]
    shard = cam_out_ref.shape[1]
    right, image = sums_ref[0], image_ref[0]
    precond = 1.0 / sums_ref[1]
    start = right * precond
    norm_now = total_sum(right * start)
    alpha = norm_now / total_sum(start * image)
    residual = right - alpha * image
    precon_res = precond * residual
    norm_next = total_sum(residual * precon_res)
    p_ref[...] = start
    d_ref[...] = precon_res + norm_next / norm_now * start

    own_tile, own_lane = own_place(n_row, n_col, cams)
    whole_tile = lax.axis_index("row") * row_tiles + own_tile
    own_first = load_tile(p_ref, cams // LANES, whole_tile)
    own_second = load_tile(d_ref, cams // LANES, whole_tile)
    energy = own_second * own_second * damp_tile_ref[...]
    energy = jnp.sum(jnp.sum(energy, axis=0, keepdims=True), axis=1, keepdims=True)

    select = shard_select(shard, own_lane)
    mask = param_mask(shard)
    flat = dot3(jnp.concatenate([own_first, own_second], axis=0), select, NT)
    flat_first = jnp.sum(jnp.where(mask, flat[:16], 0.0), axis=0, keepdims=True)
    flat_second = jnp.sum(jnp.where(mask, flat[16:], 0.0), axis=0, keepdims=True)
    cam_out_ref[0:1, :] = alpha * flat_first
    cam_out_ref[1:2, :] = norm_next * flat_second

    for k in range(count):
        _, land_hot, u0, u1, m, y_land = half_product(k, d_ref, pairs_ref, jac_ref, ocam_ref, oland_ref, m_ref)
        factor = row_list(fac_ref[k], 9)
        solved = upper_solve(factor, y_land[0:1], y_land[1:2], y_land[2:3])
        for b in range(3):
            land_base_ref[b, k : k + 1, :] = -(back_ref[k, 3 + b : 4 + b, :] + alpha * back_ref[k, b : b + 1, :])
            land_slope_ref[b, k : k + 1, :] = -norm_next * solved[b]
        y_obs = row_list(dot3(y_land, land_hot, NN), 3)
        v0 = u0 - (m[0] * y_obs[0] + m[1] * y_obs[1] + m[2] * y_obs[2])
        v1 = u1 - (m[3] * y_obs[0] + m[4] * y_obs[1] + m[5] * y_obs[2])
        energy = energy + jnp.sum(u0 * v0 + u1 * v1, axis=1, keepdims=True)
    energy_ref[...] = jnp.broadcast_to(energy, energy_ref.shape)


def merge_kernel(n_row, n_col, cams, radix, *refs):
    *part_refs, whole_ref = refs
    row_tiles = cams // n_row // LANES
    col_tiles = cams // n_col // LANES
    tiles = row_tiles + col_tiles
    whole_tiles = cams // LANES
    row, col = lax.axis_index("row"), lax.axis_index("col")
    whole_ref[...] = jnp.zeros(whole_ref.shape, jnp.float32)
    for v in range(whole_ref.shape[0]):

        def add(t, local, x):
            whole_ref[v, t] += x[local]
            ninth = x[tiles + local // 8, local % 8 : local % 8 + 1]
            whole_ref[v, whole_tiles + t // 8, pl.ds(t % 8, 1), :] += ninth

        parts = [ref[v] for ref in part_refs]
        for digit, part in enumerate(parts):
            start = (row ^ (digit * (n_row // radix))) * row_tiles
            for i in range(row_tiles):
                add(start + i, i, part)
        total = parts[0]
        for part in parts[1:]:
            total = total + part
        for i in range(col_tiles):
            add(col * col_tiles + i, row_tiles + i, total)


def exchange(x, masks, n_dev):
    return [lax.ppermute(x, AXES, [(i, i ^ mask) for i in range(n_dev)]) for mask in masks]


def in_vmem(x):
    return pltpu.with_memory_space_constraint(x, pltpu.VMEM)


def per_device(n_row, n_col, cam_jac, land_jac, resid, obs_cam, obs_land, pairs, cam_damp):
    f32 = jnp.float32
    count, _, obs = cam_jac.shape
    shard = cam_damp.shape[0]
    n_dev = n_row * n_col
    cams = shard * n_dev // 9
    row_tiles = cams // n_row // LANES
    tiles = row_tiles + cams // n_col // LANES
    part_tiles = tiles + (tiles + 7) // 8
    whole_tiles = cams // LANES
    whole_packed = whole_tiles + (whole_tiles + 7) // 8
    vmem = pl.BlockSpec(memory_space=pltpu.VMEM)
    smem = pl.BlockSpec(memory_space=pltpu.SMEM)

    def shape(*dims):
        return pltpu.VMEM(dims, f32)

    radix = min(n_row, 4)
    low = n_row // radix
    lead = [digit * low * n_col for digit in range(1, radix)]
    ones = [digit * n_col for digit in range(1, low)]
    twos = [digit * 2 for digit in range(1, n_col // 2)]
    if len(ones) == 1 and len(twos) == 1:
        rounds = [[ones[0], twos[0], ones[0] + twos[0]], [1]]
    else:
        rounds = [ones, twos, [1]]

    def all_reduce(part):
        pieces = [part] + exchange(part, lead, n_dev)
        x = pl.pallas_call(
            functools.partial(merge_kernel, n_row, n_col, cams, radix),
            out_shape=shape(part.shape[0], whole_packed, 8, LANES),
            in_specs=[vmem] * radix,
            out_specs=vmem,
        )(*map(in_vmem, pieces))
        for masks in rounds:
            for y in exchange(x, masks, n_dev):
                x = x + y
        return x

    part, jac, m, fac, damp_tile = pl.pallas_call(
        functools.partial(build_kernel, n_row, n_col, cams),
        out_shape=(shape(2, part_tiles, 8, LANES), shape(count, 2, 16, obs), shape(count, 8, obs), shape(count, 16, LM), shape(16, LANES)),
        in_specs=[smem] + [vmem] * 6,
        out_specs=(vmem,) * 5,
    )(
        pairs.T,
        jnp.transpose(cam_jac, (1, 0, 2)),
        jnp.transpose(land_jac, (1, 0, 2)),
        jnp.transpose(resid, (1, 0, 2)),
        obs_cam,
        obs_land,
        cam_damp.reshape(1, shard),
    )
    sums = all_reduce(part)

    image, back = pl.pallas_call(
        functools.partial(first_kernel, n_row, n_col, cams),
        out_shape=(shape(1, part_tiles, 8, LANES), shape(count, 8, LM)),
        in_specs=[smem] + [vmem] * 7,
        out_specs=(vmem,) * 2,
        scratch_shapes=[pltpu.VMEM((whole_packed, 8, LANES), f32)],
    )(pairs.T, *map(in_vmem, (sums, jac, obs_cam, obs_land, m, fac, damp_tile)))

    image = all_reduce(image)

    energy, cam_out, land_base, land_slope = pl.pallas_call(
        functools.partial(second_kernel, n_row, n_col, cams),
        out_shape=(shape(8, LANES), shape(2, shard), shape(3, count, LM), shape(3, count, LM)),
        in_specs=[smem] + [vmem] * 9,
        out_specs=(vmem,) * 4,
        scratch_shapes=[pltpu.VMEM((whole_packed, 8, LANES), f32)] * 2,
    )(pairs.T, *map(in_vmem, (sums, image, jac, obs_cam, obs_land, m, fac, damp_tile, back)))

    spread = jnp.broadcast_to(energy[0:1][None], (n_dev, 1, LANES))
    gathered = lax.all_to_all(spread, AXES, 0, 0, tiled=True)
    inverse = 1.0 / jnp.sum(gathered, axis=0)[0, 0]
    land = land_base + inverse * land_slope
    return cam_out[0] + inverse * cam_out[1], jnp.transpose(land, (1, 0, 2))


def solution(mesh):
    n_row, n_col = mesh.shape["row"], mesh.shape["col"]
    both = P(AXES)
    in_specs = (P(AXES, None, None),) * 3 + (P(AXES, None),) * 3 + (both,)
    out_specs = (both, P(AXES, None, None))
    return jax.shard_map(
        functools.partial(per_device, n_row, n_col),
        mesh=mesh,
        in_specs=in_specs,
        out_specs=out_specs,
        check_vma=False,
    )
```

```python
import functools

import jax
import jax.numpy as jnp
from jax import lax
from jax.experimental import pallas as pl
from jax.experimental.pallas import tpu as pltpu
from jax.sharding import PartitionSpec as P

CAM = 64
LM = 128
LANES = 128
AXES = ("row", "col")
DAMPING = 1.0

NN = (((1,), (0,)), ((), ()))
NT = (((1,), (1,)), ((), ()))


def split3(x):
    hi = x.astype(jnp.bfloat16)
    rest = x - hi.astype(jnp.float32)
    mid = rest.astype(jnp.bfloat16)
    low = (rest - mid.astype(jnp.float32)).astype(jnp.bfloat16)
    return jnp.concatenate([hi, mid, low], axis=0)


def dot3(x, exact, dims):
    n = x.shape[0]
    y = lax.dot_general(split3(x), exact, dims, preferred_element_type=jnp.float32)
    return (y[2 * n :] + y[n : 2 * n]) + y[:n]


def onehot(index_column, lanes):
    return jnp.where(index_column == lanes, 1.0, 0.0).astype(jnp.bfloat16)


def take_lanes(x, index_row):
    pieces = []
    for start in range(0, index_row.shape[1], LANES):
        index = jnp.broadcast_to(index_row[:, start : start + LANES], x.shape)
        pieces.append(jnp.take_along_axis(x, index, axis=1, mode="promise_in_bounds"))
    return jnp.concatenate(pieces, axis=1)


def pad_rows(x, rows):
    if x.shape[0] == rows:
        return x
    return jnp.concatenate([x, jnp.zeros((rows - x.shape[0], x.shape[1]), x.dtype)], axis=0)


def stack_rows(rows, total):
    rows = list(rows)
    rows.append(jnp.zeros((total - len(rows), rows[0].shape[1]), jnp.float32))
    return jnp.concatenate(rows, axis=0)


def cholesky_three(v00, v01, v02, v11, v12, v22):
    inv_first = 1.0 / jnp.sqrt(v00)
    low_one = v01 * inv_first
    low_two = v02 * inv_first
    inv_second = 1.0 / jnp.sqrt(v11 - low_one * low_one)
    low_three = (v12 - low_two * low_one) * inv_second
    inv_third = 1.0 / jnp.sqrt(v22 - low_two * low_two - low_three * low_three)
    return (inv_first, low_one, low_two, inv_second, low_three, inv_third)


def lower_solve(factor, first, second, third):
    out_one = first * factor[0]
    out_two = (second - factor[1] * out_one) * factor[3]
    out_three = (third - factor[2] * out_one - factor[4] * out_two) * factor[5]
    return (out_one, out_two, out_three)


def upper_solve(factor, first, second, third):
    out_three = third * factor[5]
    out_two = (second - factor[4] * out_three) * factor[3]
    out_one = (first - factor[1] * out_two - factor[2] * out_three) * factor[0]
    return (out_one, out_two, out_three)


def row_list(x, count):
    return [x[i : i + 1] for i in range(count)]


def lane_ids(rows):
    return lax.broadcasted_iota(jnp.int32, (rows, LANES), 1)


def to_first(x, half):
    return pltpu.roll(x, half * CAM, 1)


def to_second(x, half):
    return pltpu.roll(x, (1 - half) * CAM, 1)


def load_tile(ref, tiles, t):
    ninth = ref[tiles + t // 8, pl.ds(t % 8, 1), :]
    return jnp.concatenate([ref[t], ninth, jnp.zeros((7, LANES), jnp.float32)], axis=0)


def add_tile(ref, tiles, t, value):
    ref[t] += value[:8]
    ref[tiles + t // 8, pl.ds(t % 8, 1), :] += value[8:9]


def shard_select(shard, lane_offset):
    entry = lax.broadcasted_iota(jnp.int32, (shard, LANES), 0)
    start = 9 * (lax.broadcasted_iota(jnp.int32, (shard, LANES), 1) - lane_offset)
    inside = (entry >= start) & (entry < start + 9)
    return jnp.where(inside, 1.0, 0.0).astype(jnp.bfloat16)


def param_mask(shard):
    entry = lax.broadcasted_iota(jnp.int32, (16, shard), 1).astype(jnp.float32)
    camera = jnp.floor((entry + 0.5) * (1.0 / 9.0))
    param = entry - 9.0 * camera
    return param == lax.broadcasted_iota(jnp.int32, (16, shard), 0).astype(jnp.float32)


def place(pairs_ref, k, n_row, n_col, groups):
    first = pairs_ref[0, k] - lax.axis_index("row") * (groups // n_row)
    second = pairs_ref[1, k] - lax.axis_index("col") * (groups // n_col)
    return first // 2, first % 2, second // 2, second % 2


def scatter_pair(value, ref, tiles, row_tiles, spot):
    t_first, h_first, t_second, h_second = spot
    lower = lane_ids(value.shape[0]) < CAM
    add_tile(ref, tiles, t_first, to_first(jnp.where(lower, value, 0.0), h_first))
    add_tile(ref, tiles, row_tiles + t_second, to_second(jnp.where(lower, 0.0, value), h_second))


def own_place(n_row, n_col, cams):
    shard_cams = cams // (n_row * n_col)
    start = lax.axis_index("col") * shard_cams
    return start // LANES, start % LANES


def build_kernel(n_row, n_col, cams, pairs_ref, cam_ref, land_ref, resid_ref, ocam_ref, oland_ref, damp_ref, part_ref, jac_ref, cam_hot_ref, land_hot_ref, index_ref, m_ref, fac_ref, damp_tile_ref):
    groups = cams // CAM
    row_tiles = cams // n_row // LANES
    tiles = row_tiles + cams // n_col // LANES
    count, obs = ocam_ref.shape
    shard = damp_ref.shape[0]
    part_ref[...] = jnp.zeros(part_ref.shape, jnp.float32)
    rhs_ref, diag_ref = part_ref.at[0], part_ref.at[1]

    own_tile, own_lane = own_place(n_row, n_col, cams)
    spread = jnp.where(param_mask(shard), damp_ref[...].reshape(1, shard), 0.0)
    damp_tile = dot3(spread, shard_select(shard, own_lane), NN)
    damp_tile_ref[...] = damp_tile
    add_tile(diag_ref, tiles, own_tile, damp_tile)

    index_ref[0] = ocam_ref[...]
    index_ref[1] = oland_ref[...]
    rows = jnp.concatenate([ocam_ref[...], oland_ref[...]], axis=0).astype(jnp.float32)
    columns = jnp.transpose(pad_rows(rows, (2 * count + 7) // 8 * 8))
    key = rows[:count] * float(LM) + rows[count:]
    lanes = lax.broadcasted_iota(jnp.int32, (obs, LANES), 1).astype(jnp.float32)

    for k in range(count):
        cam_column, land_column = columns[:, k : k + 1], columns[:, count + k : count + k + 1]
        cam_hot, land_hot = onehot(cam_column, lanes), onehot(land_column, lanes)
        cam_hot_ref[k] = cam_hot
        land_hot_ref[k] = land_hot
        lj = [land_ref[i, k : k + 1, :] for i in range(6)]
        e0, e1 = resid_ref[k, 0:1, :], resid_ref[k, 1:2, :]

        def outer(i, j):
            return lj[i] * lj[j] + lj[3 + i] * lj[3 + j]

        entries = [outer(0, 0), outer(0, 1), outer(0, 2), outer(1, 1), outer(1, 2), outer(2, 2)]
        entries += [lj[b] * e0 + lj[3 + b] * e1 for b in range(3)]
        sums = row_list(dot3(stack_rows(entries, 16), land_hot, NN), 9)
        factor = cholesky_three(
            sums[0] + DAMPING, sums[1], sums[2], sums[3] + DAMPING, sums[4], sums[5] + DAMPING
        )
        tvec = lower_solve(factor, sums[6], sums[7], sums[8])
        land_values = stack_rows(list(factor) + list(tvec), 16)
        fac_ref[k] = land_values
        at_obs = row_list(take_lanes(land_values, oland_ref[k : k + 1, :]), 9)
        m0 = lower_solve(at_obs, lj[0], lj[1], lj[2])
        m1 = lower_solve(at_obs, lj[3], lj[4], lj[5])
        m_ref[k] = stack_rows(m0 + m1, 8)
        w0 = m0[0] * at_obs[6] + m0[1] * at_obs[7] + m0[2] * at_obs[8] - e0
        w1 = m1[0] * at_obs[6] + m1[1] * at_obs[7] + m1[2] * at_obs[8] - e1
        j0 = pad_rows(cam_ref[0:9, k, :], 16)
        j1 = pad_rows(cam_ref[9:18, k, :], 16)
        jac_ref[k, 0] = j0
        jac_ref[k, 1] = j1
        rhs = j0 * w0 + j1 * w1
        coupled = jnp.concatenate([j0 * m0[b] + j1 * m1[b] for b in range(3)], axis=0)
        same = onehot(cam_column * float(LM) + land_column, key[k : k + 1, :])
        prod = coupled * dot3(coupled, same, NN)
        diag = j0 * j0 + j1 * j1 - (prod[0:16] + prod[16:32] + prod[32:48])
        both = dot3(jnp.concatenate([rhs, diag], axis=0), cam_hot, NN)
        spot = place(pairs_ref, k, n_row, n_col, groups)
        scatter_pair(both[:16], rhs_ref, tiles, row_tiles, spot)
        scatter_pair(both[16:], diag_ref, tiles, row_tiles, spot)


def half_product(k, p_ref, pairs_ref, jac_ref, land_hot_ref, index_ref, m_ref):
    cams_tiles = p_ref.shape[0] * 8 // 9
    first, second = pairs_ref[0, k], pairs_ref[1, k]
    p_first = to_first(load_tile(p_ref, cams_tiles, first // 2), first % 2)
    p_second = to_second(load_tile(p_ref, cams_tiles, second // 2), second % 2)
    p_here = jnp.where(lane_ids(16) < CAM, p_first, p_second)
    at_obs = take_lanes(p_here, index_ref[0, k : k + 1, :])
    u0 = jnp.sum(jac_ref[k, 0] * at_obs, axis=0, keepdims=True)
    u1 = jnp.sum(jac_ref[k, 1] * at_obs, axis=0, keepdims=True)
    m = [m_ref[k, i : i + 1, :] for i in range(6)]
    y = [m[b] * u0 + m[3 + b] * u1 for b in range(3)]
    y_land = dot3(stack_rows(y, 16), land_hot_ref[k], NN)
    return u0, u1, m, y_land


def first_kernel(n_row, n_col, cams, pairs_ref, sums_ref, jac_ref, cam_hot_ref, land_hot_ref, index_ref, m_ref, fac_ref, damp_tile_ref, parts_ref, back_ref, p_ref):
    part_ref = parts_ref.at[0]
    groups = cams // CAM
    row_tiles = cams // n_row // LANES
    tiles = row_tiles + cams // n_col // LANES
    count = jac_ref.shape[0]
    p_ref[...] = sums_ref[0] * (1.0 / sums_ref[1])
    part_ref[...] = jnp.zeros(part_ref.shape, jnp.float32)
    own_tile, _ = own_place(n_row, n_col, cams)
    whole_tile = lax.axis_index("row") * row_tiles + own_tile
    own = load_tile(p_ref, cams // LANES, whole_tile)
    add_tile(part_ref, tiles, own_tile, own * damp_tile_ref[...])
    for k in range(count):
        u0, u1, m, y_land = half_product(k, p_ref, pairs_ref, jac_ref, land_hot_ref, index_ref, m_ref)
        factor = row_list(fac_ref[k], 9)
        solved = upper_solve(factor, y_land[0:1], y_land[1:2], y_land[2:3])
        from_t = upper_solve(factor, factor[6], factor[7], factor[8])
        back_ref[k] = stack_rows(solved + from_t, 8)
        y_obs = row_list(take_lanes(y_land[:8], index_ref[1, k : k + 1, :]), 3)
        v0 = u0 - (m[0] * y_obs[0] + m[1] * y_obs[1] + m[2] * y_obs[2])
        v1 = u1 - (m[3] * y_obs[0] + m[4] * y_obs[1] + m[5] * y_obs[2])
        image = jac_ref[k, 0] * v0 + jac_ref[k, 1] * v1
        image = dot3(image, cam_hot_ref[k], NN)
        scatter_pair(image, part_ref, tiles, row_tiles, place(pairs_ref, k, n_row, n_col, groups))


def total_sum(x):
    x = jnp.sum(x, axis=0)
    return jnp.sum(jnp.sum(x, axis=0, keepdims=True), axis=1, keepdims=True)


def second_kernel(n_row, n_col, cams, pairs_ref, sums_ref, image_ref, jac_ref, land_hot_ref, index_ref, m_ref, fac_ref, damp_tile_ref, back_ref, energy_ref, cam_out_ref, land_base_ref, land_slope_ref, p_ref, d_ref):
    row_tiles = cams // n_row // LANES
    count = jac_ref.shape[0]
    shard = cam_out_ref.shape[1]
    right, image = sums_ref[0], image_ref[0]
    precond = 1.0 / sums_ref[1]
    start = right * precond
    norm_now = total_sum(right * start)
    alpha = norm_now / total_sum(start * image)
    residual = right - alpha * image
    precon_res = precond * residual
    norm_next = total_sum(residual * precon_res)
    p_ref[...] = start
    d_ref[...] = precon_res + norm_next / norm_now * start

    own_tile, own_lane = own_place(n_row, n_col, cams)
    whole_tile = lax.axis_index("row") * row_tiles + own_tile
    own_first = load_tile(p_ref, cams // LANES, whole_tile)
    own_second = load_tile(d_ref, cams // LANES, whole_tile)
    energy = own_second * own_second * damp_tile_ref[...]
    energy = jnp.sum(jnp.sum(energy, axis=0, keepdims=True), axis=1, keepdims=True)

    select = shard_select(shard, own_lane)
    mask = param_mask(shard)
    flat = dot3(jnp.concatenate([own_first, own_second], axis=0), select, NT)
    flat_first = jnp.sum(jnp.where(mask, flat[:16], 0.0), axis=0, keepdims=True)
    flat_second = jnp.sum(jnp.where(mask, flat[16:], 0.0), axis=0, keepdims=True)
    cam_out_ref[0:1, :] = alpha * flat_first
    cam_out_ref[1:2, :] = norm_next * flat_second

    for k in range(count):
        u0, u1, m, y_land = half_product(k, d_ref, pairs_ref, jac_ref, land_hot_ref, index_ref, m_ref)
        factor = row_list(fac_ref[k], 9)
        solved = upper_solve(factor, y_land[0:1], y_land[1:2], y_land[2:3])
        for b in range(3):
            land_base_ref[b, k : k + 1, :] = -(back_ref[k, 3 + b : 4 + b, :] + alpha * back_ref[k, b : b + 1, :])
            land_slope_ref[b, k : k + 1, :] = -norm_next * solved[b]
        y_obs = row_list(take_lanes(y_land[:8], index_ref[1, k : k + 1, :]), 3)
        v0 = u0 - (m[0] * y_obs[0] + m[1] * y_obs[1] + m[2] * y_obs[2])
        v1 = u1 - (m[3] * y_obs[0] + m[4] * y_obs[1] + m[5] * y_obs[2])
        energy = energy + jnp.sum(u0 * v0 + u1 * v1, axis=1, keepdims=True)
    energy_ref[...] = jnp.broadcast_to(energy, energy_ref.shape)


def merge_kernel(n_row, n_col, cams, radix, *refs):
    *part_refs, whole_ref = refs
    row_tiles = cams // n_row // LANES
    col_tiles = cams // n_col // LANES
    tiles = row_tiles + col_tiles
    whole_tiles = cams // LANES
    row, col = lax.axis_index("row"), lax.axis_index("col")
    whole_ref[...] = jnp.zeros(whole_ref.shape, jnp.float32)
    for v in range(whole_ref.shape[0]):

        def add(t, local, x):
            whole_ref[v, t] += x[local]
            ninth = x[tiles + local // 8, local % 8 : local % 8 + 1]
            whole_ref[v, whole_tiles + t // 8, pl.ds(t % 8, 1), :] += ninth

        parts = [ref[v] for ref in part_refs]
        for digit, part in enumerate(parts):
            start = (row ^ (digit * (n_row // radix))) * row_tiles
            for i in range(row_tiles):
                add(start + i, i, part)
        total = parts[0]
        for part in parts[1:]:
            total = total + part
        for i in range(col_tiles):
            add(col * col_tiles + i, row_tiles + i, total)


def last_kernel(energy_ref, cam_ref, land_base_ref, land_slope_ref, cam_out_ref, land_out_ref):
    inverse = 1.0 / jnp.sum(energy_ref[...], axis=0)[:, 0:1]
    cam_out_ref[...] = (cam_ref[0:1, :] + inverse * cam_ref[1:2, :]).reshape(cam_out_ref.shape)
    land_out_ref[...] = land_base_ref[...] + inverse[None] * land_slope_ref[...]


def exchange(x, masks, n_dev):
    return [lax.ppermute(x, AXES, [(i, i ^ mask) for i in range(n_dev)]) for mask in masks]


def in_vmem(x):
    return pltpu.with_memory_space_constraint(x, pltpu.VMEM)


def per_device(n_row, n_col, cam_jac, land_jac, resid, obs_cam, obs_land, pairs, cam_damp):
    f32 = jnp.float32
    count, _, obs = cam_jac.shape
    shard = cam_damp.shape[0]
    n_dev = n_row * n_col
    cams = shard * n_dev // 9
    row_tiles = cams // n_row // LANES
    tiles = row_tiles + cams // n_col // LANES
    part_tiles = tiles + (tiles + 7) // 8
    whole_tiles = cams // LANES
    whole_packed = whole_tiles + (whole_tiles + 7) // 8
    vmem = pl.BlockSpec(memory_space=pltpu.VMEM)
    smem = pl.BlockSpec(memory_space=pltpu.SMEM)

    def shape(*dims):
        return pltpu.VMEM(dims, f32)

    radix = min(n_row, 4)
    low = n_row // radix
    lead = [digit * low * n_col for digit in range(1, radix)]
    ones = [digit * n_col for digit in range(1, low)]
    twos = [digit * 2 for digit in range(1, n_col // 2)]
    if len(ones) == 1 and len(twos) == 1:
        rounds = [[ones[0], twos[0], ones[0] + twos[0]], [1]]
    else:
        rounds = [ones, twos, [1]]

    def all_reduce(part):
        pieces = [part] + exchange(part, lead, n_dev)
        x = pl.pallas_call(
            functools.partial(merge_kernel, n_row, n_col, cams, radix),
            out_shape=shape(part.shape[0], whole_packed, 8, LANES),
            in_specs=[vmem] * radix,
            out_specs=vmem,
        )(*map(in_vmem, pieces))
        for masks in rounds:
            for y in exchange(x, masks, n_dev):
                x = x + y
        return x

    hot = pltpu.VMEM((count, obs, LANES), jnp.bfloat16)
    part, jac, cam_hot, land_hot, index, m, fac, damp_tile = pl.pallas_call(
        functools.partial(build_kernel, n_row, n_col, cams),
        out_shape=(shape(2, part_tiles, 8, LANES), shape(count, 2, 16, obs), hot, hot, pltpu.VMEM((2, count, obs), jnp.int32), shape(count, 8, obs), shape(count, 16, LM), shape(16, LANES)),
        in_specs=[smem] + [vmem] * 6,
        out_specs=(vmem,) * 8,
    )(
        pairs.T,
        jnp.transpose(cam_jac, (1, 0, 2)),
        jnp.transpose(land_jac, (1, 0, 2)),
        resid,
        obs_cam,
        obs_land,
        cam_damp,
    )
    sums = all_reduce(part)

    image, back = pl.pallas_call(
        functools.partial(first_kernel, n_row, n_col, cams),
        out_shape=(shape(1, part_tiles, 8, LANES), shape(count, 8, LM)),
        in_specs=[smem] + [vmem] * 8,
        out_specs=(vmem,) * 2,
        scratch_shapes=[pltpu.VMEM((whole_packed, 8, LANES), f32)],
    )(pairs.T, *map(in_vmem, (sums, jac, cam_hot, land_hot, index, m, fac, damp_tile)))

    image = all_reduce(image)

    energy, cam_out, land_base, land_slope = pl.pallas_call(
        functools.partial(second_kernel, n_row, n_col, cams),
        out_shape=(shape(n_dev, 1, LANES), shape(2, shard), shape(3, count, LM), shape(3, count, LM)),
        in_specs=[smem] + [vmem] * 9,
        out_specs=(vmem,) * 4,
        scratch_shapes=[pltpu.VMEM((whole_packed, 8, LANES), f32)] * 2,
    )(pairs.T, *map(in_vmem, (sums, image, jac, land_hot, index, m, fac, damp_tile, back)))

    gathered = lax.all_to_all(energy, AXES, 0, 0, tiled=True)
    cam_step, land_step = pl.pallas_call(
        last_kernel,
        out_shape=(jax.ShapeDtypeStruct((shard,), f32), jax.ShapeDtypeStruct((3, count, LM), f32)),
        in_specs=[vmem] * 4,
        out_specs=(vmem,) * 2,
    )(*map(in_vmem, (gathered, cam_out, land_base, land_slope)))
    return cam_step, jnp.transpose(land_step, (1, 0, 2))


def solution(mesh):
    n_row, n_col = mesh.shape["row"], mesh.shape["col"]
    both = P(AXES)
    in_specs = (P(AXES, None, None),) * 3 + (P(AXES, None),) * 3 + (both,)
    out_specs = (both, P(AXES, None, None))
    return jax.shard_map(
        functools.partial(per_device, n_row, n_col),
        mesh=mesh,
        in_specs=in_specs,
        out_specs=out_specs,
        check_vma=False,
    )
```

```python
import functools

import jax
import jax.numpy as jnp
from jax import lax
from jax.experimental import pallas as pl
from jax.experimental.pallas import tpu as pltpu
from jax.sharding import PartitionSpec as P

CAM = 64
LM = 128
LANES = 128
AXES = ("row", "col")
DAMPING = 1.0

NN = (((1,), (0,)), ((), ()))
NT = (((1,), (1,)), ((), ()))


def split3(x):
    hi = x.astype(jnp.bfloat16)
    rest = x - hi.astype(jnp.float32)
    mid = rest.astype(jnp.bfloat16)
    low = (rest - mid.astype(jnp.float32)).astype(jnp.bfloat16)
    return jnp.concatenate([hi, mid, low], axis=0)


def dot3(x, exact, dims):
    n = x.shape[0]
    y = lax.dot_general(split3(x), exact, dims, preferred_element_type=jnp.float32)
    return (y[2 * n :] + y[n : 2 * n]) + y[:n]


def onehot(index_column, lanes):
    return jnp.where(index_column == lanes, 1.0, 0.0).astype(jnp.bfloat16)


def take_lanes(x, index_row):
    pieces = []
    for start in range(0, index_row.shape[1], LANES):
        index = jnp.broadcast_to(index_row[:, start : start + LANES], x.shape)
        pieces.append(jnp.take_along_axis(x, index, axis=1, mode="promise_in_bounds"))
    return jnp.concatenate(pieces, axis=1)


def pad_rows(x, rows):
    if x.shape[0] == rows:
        return x
    return jnp.concatenate([x, jnp.zeros((rows - x.shape[0], x.shape[1]), x.dtype)], axis=0)


def stack_rows(rows, total):
    rows = list(rows)
    if len(rows) == total:
        return jnp.concatenate(rows, axis=0)
    rows.append(jnp.zeros((total - len(rows), rows[0].shape[1]), jnp.float32))
    return jnp.concatenate(rows, axis=0)


def cholesky_three(v00, v01, v02, v11, v12, v22):
    inv_first = 1.0 / jnp.sqrt(v00)
    low_one = v01 * inv_first
    low_two = v02 * inv_first
    inv_second = 1.0 / jnp.sqrt(v11 - low_one * low_one)
    low_three = (v12 - low_two * low_one) * inv_second
    inv_third = 1.0 / jnp.sqrt(v22 - low_two * low_two - low_three * low_three)
    return (inv_first, low_one, low_two, inv_second, low_three, inv_third)


def lower_solve(factor, first, second, third):
    out_one = first * factor[0]
    out_two = (second - factor[1] * out_one) * factor[3]
    out_three = (third - factor[2] * out_one - factor[4] * out_two) * factor[5]
    return (out_one, out_two, out_three)


def upper_solve(factor, first, second, third):
    out_three = third * factor[5]
    out_two = (second - factor[4] * out_three) * factor[3]
    out_one = (first - factor[1] * out_two - factor[2] * out_three) * factor[0]
    return (out_one, out_two, out_three)


def row_list(x, count):
    return [x[i : i + 1] for i in range(count)]


def lane_ids(rows):
    return lax.broadcasted_iota(jnp.int32, (rows, LANES), 1)


def to_first(x, half):
    return pltpu.roll(x, half * CAM, 1)


def to_second(x, half):
    return pltpu.roll(x, (1 - half) * CAM, 1)


def load_tile(ref, tiles, t):
    ninth = ref[tiles + t // 8, pl.ds(t % 8, 1), :]
    return jnp.concatenate([ref[t], ninth, jnp.zeros((7, LANES), jnp.float32)], axis=0)


def shard_select(shard, lane_offset):
    entry = lax.broadcasted_iota(jnp.int32, (shard, LANES), 0)
    start = 9 * (lax.broadcasted_iota(jnp.int32, (shard, LANES), 1) - lane_offset)
    inside = (entry >= start) & (entry < start + 9)
    return jnp.where(inside, 1.0, 0.0).astype(jnp.bfloat16)


def param_mask(shard):
    entry = lax.broadcasted_iota(jnp.int32, (16, shard), 1).astype(jnp.float32)
    camera = jnp.floor((entry + 0.5) * (1.0 / 9.0))
    param = entry - 9.0 * camera
    return param == lax.broadcasted_iota(jnp.int32, (16, shard), 0).astype(jnp.float32)


def place(pairs_ref, k, n_row, n_col, groups):
    first = pairs_ref[0, k] - lax.axis_index("row") * (groups // n_row)
    second = pairs_ref[1, k] - lax.axis_index("col") * (groups // n_col)
    return first // 2, first % 2, second // 2, second % 2


def write_parts(ref, row_tiles, tiles, spots, values, extra=None):
    rows = values[0].shape[0]
    lower = lane_ids(rows) < CAM
    firsts = [to_first(jnp.where(lower, v, 0.0), spot[1]) for v, spot in zip(values, spots)]
    seconds = [to_second(jnp.where(lower, 0.0, v), spot[3]) for v, spot in zip(values, spots)]
    ninths = []
    for t in range(tiles):
        if t < row_tiles:
            items = [(spot[0] == t, v) for v, spot in zip(firsts, spots)]
            if extra is not None:
                items.append((extra[0] == t, extra[1]))
        else:
            items = [(spot[2] == t - row_tiles, v) for v, spot in zip(seconds, spots)]
        total = sum(jnp.where(here, v, 0.0) for here, v in items)
        ref[t] = total[:8]
        ninths.append(total[8:9])
    for start in range(0, tiles, 8):
        ref[tiles + start // 8] = stack_rows(ninths[start : start + 8], 8)


def own_place(n_row, n_col, cams):
    shard_cams = cams // (n_row * n_col)
    start = lax.axis_index("col") * shard_cams
    return start // LANES, start % LANES


def build_kernel(n_row, n_col, cams, pairs_ref, cam_ref, land_ref, resid_ref, ocam_ref, oland_ref, damp_ref, part_ref, jac_ref, cam_hot_ref, land_hot_ref, index_ref, m_ref, fac_ref, damp_tile_ref):
    groups = cams // CAM
    row_tiles = cams // n_row // LANES
    tiles = row_tiles + cams // n_col // LANES
    count, obs = ocam_ref.shape
    each = range(count)
    shard = damp_ref.shape[0]

    index_ref[0] = ocam_ref[...]
    index_ref[1] = oland_ref[...]
    rows = jnp.concatenate([ocam_ref[...], oland_ref[...]], axis=0).astype(jnp.float32)
    columns = jnp.transpose(pad_rows(rows, (2 * count + 7) // 8 * 8))
    key = rows[:count] * float(LM) + rows[count:]
    lanes = lax.broadcasted_iota(jnp.int32, (obs, LANES), 1).astype(jnp.float32)
    cam_columns = [columns[:, k : k + 1] for k in each]
    land_columns = [columns[:, count + k : count + k + 1] for k in each]
    for k in each:
        land_hot_ref[k] = onehot(land_columns[k], lanes)

    lj = [[land_ref[i, k : k + 1, :] for i in range(6)] for k in each]
    e0 = [resid_ref[k, 0:1, :] for k in each]
    e1 = [resid_ref[k, 1:2, :] for k in each]
    sums = []
    for k in each:

        def outer(i, j):
            return lj[k][i] * lj[k][j] + lj[k][3 + i] * lj[k][3 + j]

        entries = [outer(0, 0), outer(0, 1), outer(0, 2), outer(1, 1), outer(1, 2), outer(2, 2)]
        entries += [lj[k][b] * e0[k] + lj[k][3 + b] * e1[k] for b in range(3)]
        sums.append(dot3(stack_rows(entries, 16), land_hot_ref[k], NN))
    total = [jnp.concatenate([sums[k][i : i + 1] for k in each], axis=0) for i in range(9)]
    factor = cholesky_three(
        total[0] + DAMPING, total[1], total[2], total[3] + DAMPING, total[4], total[5] + DAMPING
    )
    land_rows = list(factor) + list(lower_solve(factor, total[6], total[7], total[8]))
    for k in each:
        cam_hot_ref[k] = onehot(cam_columns[k], lanes)
        jac_ref[k, 0] = pad_rows(cam_ref[0:9, k, :], 16)
        jac_ref[k, 1] = pad_rows(cam_ref[9:18, k, :], 16)
    ms, ws = [], []
    for k in each:
        land_values = stack_rows([row[k : k + 1] for row in land_rows], 16)
        fac_ref[k] = land_values
        at_obs = row_list(take_lanes(land_values, oland_ref[k : k + 1, :]), 9)
        m0 = lower_solve(at_obs, lj[k][0], lj[k][1], lj[k][2])
        m1 = lower_solve(at_obs, lj[k][3], lj[k][4], lj[k][5])
        m_ref[k] = stack_rows(m0 + m1, 8)
        ms.append((m0, m1))
        w0 = m0[0] * at_obs[6] + m0[1] * at_obs[7] + m0[2] * at_obs[8] - e0[k]
        w1 = m1[0] * at_obs[6] + m1[1] * at_obs[7] + m1[2] * at_obs[8] - e1[k]
        ws.append((w0, w1))
    both = []
    for k in each:
        j0, j1 = jac_ref[k, 0], jac_ref[k, 1]
        m0, m1 = ms[k]
        coupled = jnp.concatenate([j0 * m0[b] + j1 * m1[b] for b in range(3)], axis=0)
        same = onehot(cam_columns[k] * float(LM) + land_columns[k], key[k : k + 1, :])
        prod = coupled * dot3(coupled, same, NN)
        diag = j0 * j0 + j1 * j1 - (prod[0:16] + prod[16:32] + prod[32:48])
        rhs = j0 * ws[k][0] + j1 * ws[k][1]
        both.append(dot3(jnp.concatenate([rhs, diag], axis=0), cam_hot_ref[k], NN))

    own_tile, own_lane = own_place(n_row, n_col, cams)
    spread = jnp.where(param_mask(shard), damp_ref[...].reshape(1, shard), 0.0)
    damp_tile = dot3(spread, shard_select(shard, own_lane), NN)
    damp_tile_ref[...] = damp_tile
    spots = [place(pairs_ref, k, n_row, n_col, groups) for k in each]
    write_parts(part_ref.at[0], row_tiles, tiles, spots, [x[:16] for x in both])
    write_parts(part_ref.at[1], row_tiles, tiles, spots, [x[16:] for x in both], (own_tile, damp_tile))


def half_product(p_ref, pairs_ref, jac_ref, land_hot_ref, index_ref, m_ref):
    each = range(jac_ref.shape[0])
    cams_tiles = p_ref.shape[0] * 8 // 9
    lower = lane_ids(16) < CAM
    u, m, y_land = [], [], []
    for k in each:
        first, second = pairs_ref[0, k], pairs_ref[1, k]
        p_first = to_first(load_tile(p_ref, cams_tiles, first // 2), first % 2)
        p_second = to_second(load_tile(p_ref, cams_tiles, second // 2), second % 2)
        at_obs = take_lanes(jnp.where(lower, p_first, p_second), index_ref[0, k : k + 1, :])
        u.append([jnp.sum(jac_ref[k, r] * at_obs, axis=0, keepdims=True) for r in range(2)])
    for k in each:
        m.append([m_ref[k, i : i + 1, :] for i in range(6)])
        y = [m[k][b] * u[k][0] + m[k][3 + b] * u[k][1] for b in range(3)]
        y_land.append(dot3(stack_rows(y, 16), land_hot_ref[k], NN)[:8])
    return u, m, y_land


def reduced_rows(u, m, y_land, index_ref):
    out = []
    for k in range(len(u)):
        y = row_list(take_lanes(y_land[k], index_ref[1, k : k + 1, :]), 3)
        out.append([u[k][r] - (m[k][3 * r] * y[0] + m[k][3 * r + 1] * y[1] + m[k][3 * r + 2] * y[2]) for r in range(2)])
    return out


def back_solve(fac_ref, k, rows):
    factor = row_list(fac_ref[k], 9)
    return upper_solve(factor, *rows), factor


def first_kernel(n_row, n_col, cams, pairs_ref, sums_ref, jac_ref, cam_hot_ref, land_hot_ref, index_ref, m_ref, fac_ref, damp_tile_ref, part_ref, back_ref, p_ref):
    groups = cams // CAM
    row_tiles = cams // n_row // LANES
    tiles = row_tiles + cams // n_col // LANES
    each = range(jac_ref.shape[0])
    p_ref[...] = sums_ref[0] * (1.0 / sums_ref[1])
    own_tile, _ = own_place(n_row, n_col, cams)
    whole_tile = lax.axis_index("row") * row_tiles + own_tile
    own = load_tile(p_ref, cams // LANES, whole_tile) * damp_tile_ref[...]
    u, m, y_land = half_product(p_ref, pairs_ref, jac_ref, land_hot_ref, index_ref, m_ref)
    v = reduced_rows(u, m, y_land, index_ref)
    images = [dot3(jac_ref[k, 0] * v[k][0] + jac_ref[k, 1] * v[k][1], cam_hot_ref[k], NN) for k in each]
    for k in each:
        solved, factor = back_solve(fac_ref, k, row_list(y_land[k], 3))
        from_t = upper_solve(factor, factor[6], factor[7], factor[8])
        back_ref[k] = stack_rows(solved + from_t, 8)
    spots = [place(pairs_ref, k, n_row, n_col, groups) for k in each]
    write_parts(part_ref.at[0], row_tiles, tiles, spots, images, (own_tile, own))


def total_sum(x):
    x = jnp.sum(x, axis=0)
    return jnp.sum(jnp.sum(x, axis=0, keepdims=True), axis=1, keepdims=True)


def second_kernel(n_row, n_col, cams, pairs_ref, sums_ref, image_ref, jac_ref, land_hot_ref, index_ref, m_ref, fac_ref, damp_tile_ref, back_ref, energy_ref, cam_out_ref, land_base_ref, land_slope_ref, p_ref, d_ref):
    row_tiles = cams // n_row // LANES
    count = jac_ref.shape[0]
    shard = cam_out_ref.shape[1]
    right, image = sums_ref[0], image_ref[0]
    precond = 1.0 / sums_ref[1]
    start = right * precond
    norm_now = total_sum(right * start)
    alpha = norm_now / total_sum(start * image)
    residual = right - alpha * image
    precon_res = precond * residual
    norm_next = total_sum(residual * precon_res)
    p_ref[...] = start
    d_ref[...] = precon_res + norm_next / norm_now * start

    own_tile, own_lane = own_place(n_row, n_col, cams)
    whole_tile = lax.axis_index("row") * row_tiles + own_tile
    own_first = load_tile(p_ref, cams // LANES, whole_tile)
    own_second = load_tile(d_ref, cams // LANES, whole_tile)
    energy = own_second * own_second * damp_tile_ref[...]
    energy = jnp.sum(jnp.sum(energy, axis=0, keepdims=True), axis=1, keepdims=True)

    select = shard_select(shard, own_lane)
    mask = param_mask(shard)
    flat = dot3(jnp.concatenate([own_first, own_second], axis=0), select, NT)
    flat_first = jnp.sum(jnp.where(mask, flat[:16], 0.0), axis=0, keepdims=True)
    flat_second = jnp.sum(jnp.where(mask, flat[16:], 0.0), axis=0, keepdims=True)
    cam_out_ref[0:1, :] = alpha * flat_first
    cam_out_ref[1:2, :] = norm_next * flat_second

    u, m, y_land = half_product(d_ref, pairs_ref, jac_ref, land_hot_ref, index_ref, m_ref)
    v = reduced_rows(u, m, y_land, index_ref)
    by_obs = sum(u[k][0] * v[k][0] + u[k][1] * v[k][1] for k in range(count))
    energy = energy + jnp.sum(by_obs, axis=1, keepdims=True)
    for k in range(count):
        solved, _ = back_solve(fac_ref, k, row_list(y_land[k], 3))
        for b in range(3):
            land_base_ref[b, k : k + 1, :] = -(back_ref[k, 3 + b : 4 + b, :] + alpha * back_ref[k, b : b + 1, :])
            land_slope_ref[b, k : k + 1, :] = -norm_next * solved[b]
    energy_ref[...] = jnp.broadcast_to(energy, energy_ref.shape)


def merge_kernel(n_row, n_col, cams, radix, *refs):
    *part_refs, whole_ref = refs
    row_tiles = cams // n_row // LANES
    col_tiles = cams // n_col // LANES
    tiles = row_tiles + col_tiles
    whole_tiles = cams // LANES
    row, col = lax.axis_index("row"), lax.axis_index("col")
    whole_ref[...] = jnp.zeros(whole_ref.shape, jnp.float32)
    for v in range(whole_ref.shape[0]):

        def add(t, local, x):
            whole_ref[v, t] += x[local]
            ninth = x[tiles + local // 8, local % 8 : local % 8 + 1]
            whole_ref[v, whole_tiles + t // 8, pl.ds(t % 8, 1), :] += ninth

        parts = [ref[v] for ref in part_refs]
        for digit, part in enumerate(parts):
            start = (row ^ (digit * (n_row // radix))) * row_tiles
            for i in range(row_tiles):
                add(start + i, i, part)
        total = parts[0]
        for part in parts[1:]:
            total = total + part
        for i in range(col_tiles):
            add(col * col_tiles + i, row_tiles + i, total)


def last_kernel(energy_ref, cam_ref, land_base_ref, land_slope_ref, cam_out_ref, land_out_ref):
    inverse = 1.0 / jnp.sum(energy_ref[...], axis=0)[:, 0:1]
    cam_out_ref[...] = (cam_ref[0:1, :] + inverse * cam_ref[1:2, :]).reshape(cam_out_ref.shape)
    land_out_ref[...] = land_base_ref[...] + inverse[None] * land_slope_ref[...]


def exchange(x, masks, n_dev):
    return [lax.ppermute(x, AXES, [(i, i ^ mask) for i in range(n_dev)]) for mask in masks]


def in_vmem(x):
    return pltpu.with_memory_space_constraint(x, pltpu.VMEM)


def per_device(n_row, n_col, cam_jac, land_jac, resid, obs_cam, obs_land, pairs, cam_damp):
    f32 = jnp.float32
    count, _, obs = cam_jac.shape
    shard = cam_damp.shape[0]
    n_dev = n_row * n_col
    cams = shard * n_dev // 9
    row_tiles = cams // n_row // LANES
    tiles = row_tiles + cams // n_col // LANES
    part_tiles = tiles + (tiles + 7) // 8
    whole_tiles = cams // LANES
    whole_packed = whole_tiles + (whole_tiles + 7) // 8
    vmem = pl.BlockSpec(memory_space=pltpu.VMEM)
    smem = pl.BlockSpec(memory_space=pltpu.SMEM)

    def shape(*dims):
        return pltpu.VMEM(dims, f32)

    radix = min(n_row, 4)
    low = n_row // radix
    lead = [digit * low * n_col for digit in range(1, radix)]
    ones = [digit * n_col for digit in range(1, low)]
    twos = [digit * 2 for digit in range(1, n_col // 2)]
    if len(ones) == 1 and len(twos) == 1:
        rounds = [[ones[0], twos[0], ones[0] + twos[0]], [1]]
    else:
        rounds = [ones, twos, [1]]

    def all_reduce(part):
        pieces = [part] + exchange(part, lead, n_dev)
        x = pl.pallas_call(
            functools.partial(merge_kernel, n_row, n_col, cams, radix),
            out_shape=shape(part.shape[0], whole_packed, 8, LANES),
            in_specs=[vmem] * radix,
            out_specs=vmem,
        )(*map(in_vmem, pieces))
        for masks in rounds:
            for y in exchange(x, masks, n_dev):
                x = x + y
        return x

    hot = pltpu.VMEM((count, obs, LANES), jnp.bfloat16)
    part, jac, cam_hot, land_hot, index, m, fac, damp_tile = pl.pallas_call(
        functools.partial(build_kernel, n_row, n_col, cams),
        out_shape=(shape(2, part_tiles, 8, LANES), shape(count, 2, 16, obs), hot, hot, pltpu.VMEM((2, count, obs), jnp.int32), shape(count, 8, obs), shape(count, 16, LM), shape(16, LANES)),
        in_specs=[smem] + [vmem] * 6,
        out_specs=(vmem,) * 8,
    )(
        pairs.T,
        jnp.transpose(cam_jac, (1, 0, 2)),
        jnp.transpose(land_jac, (1, 0, 2)),
        resid,
        obs_cam,
        obs_land,
        cam_damp,
    )
    sums = all_reduce(part)

    image, back = pl.pallas_call(
        functools.partial(first_kernel, n_row, n_col, cams),
        out_shape=(shape(1, part_tiles, 8, LANES), shape(count, 8, LM)),
        in_specs=[smem] + [vmem] * 8,
        out_specs=(vmem,) * 2,
        scratch_shapes=[pltpu.VMEM((whole_packed, 8, LANES), f32)],
    )(pairs.T, *map(in_vmem, (sums, jac, cam_hot, land_hot, index, m, fac, damp_tile)))

    image = all_reduce(image)

    energy, cam_out, land_base, land_slope = pl.pallas_call(
        functools.partial(second_kernel, n_row, n_col, cams),
        out_shape=(shape(n_dev, 1, LANES), shape(2, shard), shape(3, count, LM), shape(3, count, LM)),
        in_specs=[smem] + [vmem] * 9,
        out_specs=(vmem,) * 4,
        scratch_shapes=[pltpu.VMEM((whole_packed, 8, LANES), f32)] * 2,
    )(pairs.T, *map(in_vmem, (sums, image, jac, land_hot, index, m, fac, damp_tile, back)))

    gathered = lax.all_to_all(energy, AXES, 0, 0, tiled=True)
    cam_step, land_step = pl.pallas_call(
        last_kernel,
        out_shape=(jax.ShapeDtypeStruct((shard,), f32), jax.ShapeDtypeStruct((3, count, LM), f32)),
        in_specs=[vmem] * 4,
        out_specs=(vmem,) * 2,
    )(*map(in_vmem, (gathered, cam_out, land_base, land_slope)))
    return cam_step, jnp.transpose(land_step, (1, 0, 2))


def solution(mesh):
    n_row, n_col = mesh.shape["row"], mesh.shape["col"]
    both = P(AXES)
    in_specs = (P(AXES, None, None),) * 3 + (P(AXES, None),) * 3 + (both,)
    out_specs = (both, P(AXES, None, None))
    return jax.shard_map(
        functools.partial(per_device, n_row, n_col),
        mesh=mesh,
        in_specs=in_specs,
        out_specs=out_specs,
        check_vma=False,
    )
```

```python
import functools

import jax
import jax.numpy as jnp
from jax import lax
from jax.experimental import pallas as pl
from jax.experimental.pallas import tpu as pltpu
from jax.sharding import PartitionSpec as P

CAM = 64
LM = 128
LANES = 128
AXES = ("row", "col")
DAMPING = 1.0

NN = (((1,), (0,)), ((), ()))
NT = (((1,), (1,)), ((), ()))


def split3(x):
    hi = x.astype(jnp.bfloat16)
    rest = x - hi.astype(jnp.float32)
    mid = rest.astype(jnp.bfloat16)
    low = (rest - mid.astype(jnp.float32)).astype(jnp.bfloat16)
    return jnp.concatenate([hi, mid, low], axis=0)


def dot3(x, exact, dims):
    n = x.shape[0]
    y = lax.dot_general(split3(x), exact, dims, preferred_element_type=jnp.float32)
    return (y[2 * n :] + y[n : 2 * n]) + y[:n]


def onehot(index_column, lanes):
    return jnp.where(index_column == lanes, jnp.bfloat16(1), jnp.bfloat16(0))


def take_lanes(x, index_row):
    pieces = []
    for start in range(0, index_row.shape[1], LANES):
        index = jnp.broadcast_to(index_row[:, start : start + LANES], x.shape)
        pieces.append(jnp.take_along_axis(x, index, axis=1, mode="promise_in_bounds"))
    return jnp.concatenate(pieces, axis=1)


def pad_rows(x, rows):
    if x.shape[0] == rows:
        return x
    return jnp.concatenate([x, jnp.zeros((rows - x.shape[0], x.shape[1]), x.dtype)], axis=0)


def stack_rows(rows, total):
    rows = list(rows)
    if len(rows) == total:
        return jnp.concatenate(rows, axis=0)
    rows.append(jnp.zeros((total - len(rows), rows[0].shape[1]), jnp.float32))
    return jnp.concatenate(rows, axis=0)


def cholesky_three(v00, v01, v02, v11, v12, v22):
    inv_first = 1.0 / jnp.sqrt(v00)
    low_one = v01 * inv_first
    low_two = v02 * inv_first
    inv_second = 1.0 / jnp.sqrt(v11 - low_one * low_one)
    low_three = (v12 - low_two * low_one) * inv_second
    inv_third = 1.0 / jnp.sqrt(v22 - low_two * low_two - low_three * low_three)
    return (inv_first, low_one, low_two, inv_second, low_three, inv_third)


def lower_solve(factor, first, second, third):
    out_one = first * factor[0]
    out_two = (second - factor[1] * out_one) * factor[3]
    out_three = (third - factor[2] * out_one - factor[4] * out_two) * factor[5]
    return (out_one, out_two, out_three)


def upper_solve(factor, first, second, third):
    out_three = third * factor[5]
    out_two = (second - factor[4] * out_three) * factor[3]
    out_one = (first - factor[1] * out_two - factor[2] * out_three) * factor[0]
    return (out_one, out_two, out_three)


def row_list(x, count):
    return [x[i : i + 1] for i in range(count)]


def lane_ids(rows):
    return lax.broadcasted_iota(jnp.int32, (rows, LANES), 1)


def to_first(x, half):
    return pltpu.roll(x, half * CAM, 1)


def to_second(x, half):
    return pltpu.roll(x, (1 - half) * CAM, 1)


def packed(tiles):
    return tiles + tiles // 8 + 1


def load_tile(ref, tiles, t):
    ninth = ref[tiles + t // 8, pl.ds(t % 8, 1), :]
    return jnp.concatenate([ref[t], ninth, jnp.zeros((7, LANES), jnp.float32)], axis=0)


def write_ninths(ref, tiles, rows, sums=None):
    rows = list(rows) + [jnp.zeros((1, LANES), jnp.float32) if sums is None else sums]
    for start in range(0, len(rows), 8):
        ref[tiles + start // 8] = stack_rows(rows[start : start + 8], 8)


def shard_select(shard, lane_offset):
    entry = lax.broadcasted_iota(jnp.int32, (shard, LANES), 0)
    start = 9 * (lax.broadcasted_iota(jnp.int32, (shard, LANES), 1) - lane_offset)
    inside = (entry >= start) & (entry < start + 9)
    return jnp.where(inside, 1.0, 0.0).astype(jnp.bfloat16)


def param_mask(shard):
    entry = lax.broadcasted_iota(jnp.int32, (16, shard), 1).astype(jnp.float32)
    camera = jnp.floor((entry + 0.5) * (1.0 / 9.0))
    param = entry - 9.0 * camera
    return param == lax.broadcasted_iota(jnp.int32, (16, shard), 0).astype(jnp.float32)


def place(pairs_ref, k, n_row, n_col, groups):
    first = pairs_ref[0, k] - lax.axis_index("row") * (groups // n_row)
    second = pairs_ref[1, k] - lax.axis_index("col") * (groups // n_col)
    return first // 2, first % 2, second // 2, second % 2


def read_spots(spots_ref):
    return [[spots_ref[i, k] for i in range(4)] for k in range(spots_ref.shape[1])]


def write_parts(ref, row_tiles, tiles, spots, values, extra=None, sums=None):
    lower = lane_ids(values[0].shape[0]) < CAM
    firsts = [to_first(jnp.where(lower, v, 0.0), spot[1]) for v, spot in zip(values, spots)]
    seconds = [to_second(jnp.where(lower, 0.0, v), spot[3]) for v, spot in zip(values, spots)]
    ninths = []
    for t in range(tiles):
        if t < row_tiles:
            items = [(spot[0] == t, v) for v, spot in zip(firsts, spots)]
            if extra is not None:
                items.append((extra[0] == t, extra[1]))
        else:
            items = [(spot[2] == t - row_tiles, v) for v, spot in zip(seconds, spots)]
        total = sum(jnp.where(here, v, 0.0) for here, v in items)
        ref[t] = total[:8]
        ninths.append(total[8:9])
    write_ninths(ref, tiles, ninths, sums)


def own_place(n_row, n_col, cams):
    shard_cams = cams // (n_row * n_col)
    start = lax.axis_index("col") * shard_cams
    return start // LANES, start % LANES


def build_kernel(n_row, n_col, cams, pairs_ref, cam_ref, land_ref, resid_ref, ocam_ref, oland_ref, damp_ref, part_ref, jac_ref, cam_hot_ref, land_hot_ref, index_ref, m_ref, fac_ref, damp_tile_ref, select_ref, spots_ref):
    groups = cams // CAM
    row_tiles = cams // n_row // LANES
    tiles = row_tiles + cams // n_col // LANES
    count, obs = ocam_ref.shape
    each = range(count)
    shard = damp_ref.shape[0]

    index_ref[0] = ocam_ref[...]
    index_ref[1] = oland_ref[...]
    rows = jnp.concatenate([ocam_ref[...], oland_ref[...]], axis=0).astype(jnp.float32)
    columns = jnp.transpose(pad_rows(rows, (2 * count + 7) // 8 * 8)).astype(jnp.int32)
    key = (ocam_ref[...] * LM + oland_ref[...]).astype(jnp.int16)
    lanes = lax.broadcasted_iota(jnp.int32, (obs, LANES), 1).astype(jnp.int16)
    cam_columns = [columns[:, k : k + 1] for k in each]
    land_columns = [columns[:, count + k : count + k + 1] for k in each]
    for k in each:
        land_hot_ref[k] = onehot(land_columns[k].astype(jnp.int16), lanes)

    lj = [[land_ref[i, k : k + 1, :] for i in range(6)] for k in each]
    e0 = [resid_ref[k, 0:1, :] for k in each]
    e1 = [resid_ref[k, 1:2, :] for k in each]
    sums = []
    for k in each:

        def outer(i, j):
            return lj[k][i] * lj[k][j] + lj[k][3 + i] * lj[k][3 + j]

        entries = [outer(0, 0), outer(0, 1), outer(0, 2), outer(1, 1), outer(1, 2), outer(2, 2)]
        entries += [lj[k][b] * e0[k] + lj[k][3 + b] * e1[k] for b in range(3)]
        sums.append(dot3(stack_rows(entries, 16), land_hot_ref[k], NN))
    total = [jnp.concatenate([sums[k][i : i + 1] for k in each], axis=0) for i in range(9)]
    factor = cholesky_three(
        total[0] + DAMPING, total[1], total[2], total[3] + DAMPING, total[4], total[5] + DAMPING
    )
    land_rows = list(factor) + list(lower_solve(factor, total[6], total[7], total[8]))
    for k in each:
        cam_hot_ref[k] = onehot(cam_columns[k].astype(jnp.int16), lanes)
        jac_ref[k, 0] = pad_rows(cam_ref[0:9, k, :], 16)
        jac_ref[k, 1] = pad_rows(cam_ref[9:18, k, :], 16)
    ms, ws = [], []
    for k in each:
        land_values = stack_rows([row[k : k + 1] for row in land_rows], 16)
        fac_ref[k] = land_values
        at_obs = row_list(take_lanes(land_values, oland_ref[k : k + 1, :]), 9)
        m0 = lower_solve(at_obs, lj[k][0], lj[k][1], lj[k][2])
        m1 = lower_solve(at_obs, lj[k][3], lj[k][4], lj[k][5])
        m_ref[k] = stack_rows(m0 + m1, 8)
        ms.append((m0, m1))
        w0 = m0[0] * at_obs[6] + m0[1] * at_obs[7] + m0[2] * at_obs[8] - e0[k]
        w1 = m1[0] * at_obs[6] + m1[1] * at_obs[7] + m1[2] * at_obs[8] - e1[k]
        ws.append((w0, w1))
    both = []
    for k in each:
        j0, j1 = jac_ref[k, 0], jac_ref[k, 1]
        m0, m1 = ms[k]
        coupled = jnp.concatenate([j0 * m0[b] + j1 * m1[b] for b in range(3)], axis=0)
        same = onehot((cam_columns[k] * LM + land_columns[k]).astype(jnp.int16), key[k : k + 1, :])
        prod = coupled * dot3(coupled, same, NN)
        diag = j0 * j0 + j1 * j1 - (prod[0:16] + prod[16:32] + prod[32:48])
        rhs = j0 * ws[k][0] + j1 * ws[k][1]
        both.append(dot3(jnp.concatenate([rhs, diag], axis=0), cam_hot_ref[k], NN))

    own_tile, own_lane = own_place(n_row, n_col, cams)
    spread = jnp.where(param_mask(shard), damp_ref[...].reshape(1, shard), 0.0)
    select = shard_select(shard, own_lane)
    select_ref[...] = select
    damp_tile = dot3(spread, select, NN)
    damp_tile_ref[...] = damp_tile
    spots = [place(pairs_ref, k, n_row, n_col, groups) for k in each]
    for k in each:
        for i in range(4):
            spots_ref[i, k] = spots[k][i]
    write_parts(part_ref.at[0], row_tiles, tiles, spots, [x[:16] for x in both])
    write_parts(part_ref.at[1], row_tiles, tiles, spots, [x[16:] for x in both], (own_tile, damp_tile))


def half_product(p_ref, row_tiles, tiles, spots, jac_ref, land_hot_ref, index_ref, m_ref):
    each = range(jac_ref.shape[0])
    lower = lane_ids(16) < CAM
    u, m, y_land = [], [], []
    for k in each:
        t_first, h_first, t_second, h_second = spots[k]
        p_first = to_first(load_tile(p_ref, tiles, t_first), h_first)
        p_second = to_second(load_tile(p_ref, tiles, row_tiles + t_second), h_second)
        at_obs = take_lanes(jnp.where(lower, p_first, p_second), index_ref[0, k : k + 1, :])
        u.append([jnp.sum(jac_ref[k, r] * at_obs, axis=0, keepdims=True) for r in range(2)])
    for k in each:
        m.append([m_ref[k, i : i + 1, :] for i in range(6)])
        y = [m[k][b] * u[k][0] + m[k][3 + b] * u[k][1] for b in range(3)]
        y_land.append(dot3(stack_rows(y, 16), land_hot_ref[k], NN)[:8])
    return u, m, y_land


def reduced_rows(u, m, y_land, index_ref):
    out = []
    for k in range(len(u)):
        y = row_list(take_lanes(y_land[k], index_ref[1, k : k + 1, :]), 3)
        out.append([u[k][r] - (m[k][3 * r] * y[0] + m[k][3 * r + 1] * y[1] + m[k][3 * r + 2] * y[2]) for r in range(2)])
    return out


def back_solve(fac_ref, k, rows):
    factor = row_list(fac_ref[k], 9)
    return upper_solve(factor, *rows), factor


def total_sum(x):
    return jnp.sum(jnp.sum(x, axis=0, keepdims=True), axis=1, keepdims=True)


def own_lanes(own_lane, shard_cams):
    ids = lane_ids(16)
    return (ids >= own_lane) & (ids < own_lane + shard_cams)


def in_lanes(values):
    ids = lane_ids(1)
    row = jnp.zeros((1, LANES), jnp.float32)
    for lane, value in enumerate(values):
        row = jnp.where(ids == lane, value, row)
    return row


def energy_sum(u, v):
    return total_sum(sum(u[k][r] * v[k][r] for k in range(len(u)) for r in range(2)))


def first_kernel(n_row, n_col, cams, spots_ref, mine_ref, other_ref, jac_ref, cam_hot_ref, land_hot_ref, index_ref, m_ref, fac_ref, damp_tile_ref, part_ref, back_ref, p_ref, right_ref):
    row_tiles = cams // n_row // LANES
    tiles = row_tiles + cams // n_col // LANES
    each = range(jac_ref.shape[0])
    right = mine_ref[0] + other_ref[0]
    right_ref[...] = right
    p_ref[...] = right * (1.0 / (mine_ref[1] + other_ref[1]))
    spots = read_spots(spots_ref)
    u, m, y_land = half_product(p_ref, row_tiles, tiles, spots, jac_ref, land_hot_ref, index_ref, m_ref)
    v = reduced_rows(u, m, y_land, index_ref)
    images = [dot3(jac_ref[k, 0] * v[k][0] + jac_ref[k, 1] * v[k][1], cam_hot_ref[k], NN) for k in each]
    own_tile, own_lane = own_place(n_row, n_col, cams)
    own = load_tile(p_ref, tiles, own_tile)
    damped = own * damp_tile_ref[...]
    mask = own_lanes(own_lane, cams // (n_row * n_col))
    norm_now = total_sum(jnp.where(mask, own * load_tile(right_ref, tiles, own_tile), 0.0))
    energy = energy_sum(u, v) + total_sum(own * damped)
    for k in each:
        solved, factor = back_solve(fac_ref, k, row_list(y_land[k], 3))
        from_t = upper_solve(factor, factor[6], factor[7], factor[8])
        for b in range(3):
            back_ref[0, b, k : k + 1, :] = from_t[b]
            back_ref[1, b, k : k + 1, :] = solved[b]
    write_parts(part_ref.at[0], row_tiles, tiles, spots, images, (own_tile, damped), in_lanes([norm_now, energy]))


def second_kernel(n_row, n_col, cams, spots_ref, mine_ref, other_ref, image_mine_ref, image_other_ref, jac_ref, land_hot_ref, index_ref, m_ref, fac_ref, damp_tile_ref, select_ref, sums_ref, known_ref, cam_ref, solved_ref, p_ref, scratch_ref):
    row_tiles = cams // n_row // LANES
    tiles = row_tiles + cams // n_col // LANES
    each = range(jac_ref.shape[0])
    shard = cam_ref.shape[1]
    image = image_mine_ref[0] + image_other_ref[0]
    sums = image[tiles + tiles // 8, tiles % 8 : tiles % 8 + 1]
    norm_now, energy_now = sums[:, 0:1], sums[:, 1:2]
    alpha = norm_now / energy_now
    for i, value in enumerate((1.0 / norm_now, energy_now, alpha)):
        known_ref[i : i + 1, :] = jnp.broadcast_to(value, (1, LANES))
    right = mine_ref[0] + other_ref[0]
    precond = 1.0 / (mine_ref[1] + other_ref[1])
    residual = right - alpha * image
    p_ref[...] = precond * residual
    scratch_ref[0] = right * precond
    scratch_ref[1] = residual
    scratch_ref[2] = image
    spots = read_spots(spots_ref)
    u, m, y_land = half_product(p_ref, row_tiles, tiles, spots, jac_ref, land_hot_ref, index_ref, m_ref)
    v = reduced_rows(u, m, y_land, index_ref)

    own_tile, own_lane = own_place(n_row, n_col, cams)
    own = load_tile(p_ref, tiles, own_tile)
    own_start, own_residual, own_image = [load_tile(scratch_ref.at[i], tiles, own_tile) for i in range(3)]
    flat = dot3(jnp.concatenate([own_start, own], axis=0), select_ref[...], NT)
    params = param_mask(shard)
    for i in range(2):
        cam_ref[i : i + 1, :] = jnp.sum(jnp.where(params, flat[16 * i : 16 * i + 16], 0.0), axis=0, keepdims=True)
    mask = own_lanes(own_lane, cams // (n_row * n_col))
    norm_next = total_sum(jnp.where(mask, own * own_residual, 0.0))
    cross = total_sum(jnp.where(mask, own * own_image, 0.0))
    energy = energy_sum(u, v) + total_sum(own * own * damp_tile_ref[...])
    sums_ref[...] = jnp.broadcast_to(in_lanes([energy, norm_next, cross])[None], sums_ref.shape)
    for k in each:
        solved, _ = back_solve(fac_ref, k, row_list(y_land[k], 3))
        for b in range(3):
            solved_ref[b, k : k + 1, :] = solved[b]


def last_kernel(sums_ref, known_ref, cam_ref, back_ref, solved_ref, cam_out_ref, land_out_ref):
    sums = jnp.sum(sums_ref[...], axis=0)
    energy, norm_next, cross = [jnp.broadcast_to(sums[:, i : i + 1], (1, LANES)) for i in range(3)]
    inverse_now, energy_now, alpha = [known_ref[i : i + 1, :] for i in range(3)]
    beta = norm_next * inverse_now
    slope = norm_next / (energy + beta * (2.0 * cross + beta * energy_now))
    first = alpha + slope * beta
    shard = cam_ref.shape[1]
    repeats = (shard + LANES - 1) // LANES
    first_wide, slope_wide = [jnp.concatenate([x] * repeats, axis=1)[:, :shard] for x in (first, slope)]
    cam_step = first_wide * cam_ref[0:1, :] + slope_wide * cam_ref[1:2, :]
    cam_out_ref[...] = cam_step.reshape(cam_out_ref.shape)
    land_out_ref[...] = -(back_ref[0] + first[None] * back_ref[1] + slope[None] * solved_ref[...])


def spread_kernel(n_row, n_col, cams, radix, masks, *refs):
    part_refs, out_refs, (whole_ref, ninth_ref) = refs[:radix], refs[radix:-2], refs[-2:]
    row_tiles = cams // n_row // LANES
    col_tiles = cams // n_col // LANES
    tiles = row_tiles + col_tiles
    sent = row_tiles + 2 * col_tiles
    row, col = lax.axis_index("row"), lax.axis_index("col")
    for v in range(whole_ref.shape[0]):
        parts = [ref[v] for ref in part_refs]
        total = parts[0]
        for part in parts[1:]:
            total = total + part
        sums = total[tiles + tiles // 8, tiles % 8 : tiles % 8 + 1]
        whole_ref[v] = jnp.zeros(whole_ref.shape[1:], jnp.float32)
        ninth_ref[v] = jnp.zeros(ninth_ref.shape[1:], jnp.float32)
        for i in range(col_tiles):
            t = row_tiles + i
            whole_ref[v, col * col_tiles + i] = total[t]
            ninth_ref[v, pl.ds(col * col_tiles + i, 1), :] = total[tiles + t // 8, t % 8 : t % 8 + 1]
        for digit, part in enumerate(parts):
            start = (row ^ (digit * (n_row // radix))) * row_tiles
            for i in range(row_tiles):
                whole_ref[v, start + i] += part[i]
                ninth_ref[v, pl.ds(start + i, 1), :] += part[tiles + i // 8, i % 8 : i % 8 + 1]
        for mask, out_ref in zip(masks, out_refs):
            col_start = ((col ^ (mask % n_col)) // 2) * (2 * col_tiles)
            row_start = (row ^ (mask // n_col)) * row_tiles
            places = [col_start + i for i in range(2 * col_tiles)] + [row_start + i for i in range(row_tiles)]
            for i, t in enumerate(places):
                out_ref[v, i] = whole_ref[v, t]
            write_ninths(out_ref.at[v], sent, [ninth_ref[v, pl.ds(t, 1), :] for t in places], sums)


def pair_kernel(n_row, n_col, cams, *refs):
    in_refs, (mine_ref, other_ref) = refs[:-2], refs[-2:]
    row_tiles = cams // n_row // LANES
    col_tiles = cams // n_col // LANES
    tiles = row_tiles + col_tiles
    sent = row_tiles + 2 * col_tiles
    core = lax.axis_index("col") % 2
    for v in range(mine_ref.shape[0]):
        total = in_refs[0][v]
        for ref in in_refs[1:]:
            total = total + ref[v]

        def ninth(i):
            return total[sent + i // 8, i % 8 : i % 8 + 1]

        sums = ninth(sent)
        rows = range(2 * col_tiles, sent)
        lower = [(total[i], ninth(i)) for i in range(col_tiles)]
        upper = [(total[i], ninth(i)) for i in range(col_tiles, 2 * col_tiles)]
        for out_ref, first in ((mine_ref, core == 0), (other_ref, core == 1)):
            ninths = []
            for i, t in enumerate(rows):
                out_ref[v, i] = total[t]
                ninths.append(ninth(t))
            for i in range(col_tiles):
                out_ref[v, row_tiles + i] = jnp.where(first, lower[i][0], upper[i][0])
                ninths.append(jnp.where(first, lower[i][1], upper[i][1]))
            write_ninths(out_ref.at[v], tiles, ninths, sums)


def exchange(x, masks, n_dev):
    return [lax.ppermute(x, AXES, [(i, i ^ mask) for i in range(n_dev)]) for mask in masks]


def in_vmem(x):
    return pltpu.with_memory_space_constraint(x, pltpu.VMEM)


def per_device(n_row, n_col, cam_jac, land_jac, resid, obs_cam, obs_land, pairs, cam_damp):
    f32 = jnp.float32
    count, _, obs = cam_jac.shape
    shard = cam_damp.shape[0]
    n_dev = n_row * n_col
    cams = shard * n_dev // 9
    row_tiles = cams // n_row // LANES
    col_tiles = cams // n_col // LANES
    tiles = row_tiles + col_tiles
    sent = row_tiles + 2 * col_tiles
    vmem = pl.BlockSpec(memory_space=pltpu.VMEM)
    smem = pl.BlockSpec(memory_space=pltpu.SMEM)

    def shape(*dims):
        return pltpu.VMEM(dims, f32)

    radix = min(n_row, 4)
    low = n_row // radix
    lead = [digit * low * n_col for digit in range(1, radix)]
    middle = [x * n_col + y * 2 for x in range(low) for y in range(n_col // 2)]
    middle = middle[:1] + middle[:0:-1]

    def call(kernel, operands, out_shape, scratch=(), whole=(n_row, n_col, cams), specs=None, out_specs=None):
        return pl.pallas_call(
            functools.partial(kernel, *whole),
            out_shape=out_shape,
            in_specs=specs or [vmem] * len(operands),
            out_specs=out_specs or jax.tree.map(lambda _: vmem, out_shape),
            scratch_shapes=scratch,
        )(*operands)

    def all_reduce(part):
        vectors = part.shape[0]
        pieces = [part] + exchange(part, lead, n_dev)
        to_send = call(
            spread_kernel,
            tuple(map(in_vmem, pieces)),
            (shape(vectors, packed(sent), 8, LANES),) * len(middle),
            (pltpu.VMEM((vectors, cams // LANES, 8, LANES), f32), pltpu.VMEM((vectors, cams // LANES, LANES), f32)),
            (n_row, n_col, cams, radix, tuple(middle)),
        )
        got = [to_send[0]] + [exchange(x, [mask], n_dev)[0] for x, mask in zip(to_send[1:], middle[1:])]
        mine, other = call(pair_kernel, tuple(map(in_vmem, got)), (shape(vectors, packed(tiles), 8, LANES),) * 2)
        return in_vmem(mine), in_vmem(exchange(other, [1], n_dev)[0])

    hot = pltpu.VMEM((count, obs, LANES), jnp.bfloat16)
    part, jac, cam_hot, land_hot, index, m, fac, damp_tile, select, spots = call(
        build_kernel,
        (
            pairs.T,
            jnp.transpose(cam_jac, (1, 0, 2)),
            jnp.transpose(land_jac, (1, 0, 2)),
            resid,
            obs_cam,
            obs_land,
            cam_damp,
        ),
        (
            shape(2, packed(tiles), 8, LANES),
            shape(count, 2, 16, obs),
            hot,
            hot,
            pltpu.VMEM((2, count, obs), jnp.int32),
            shape(count, 8, obs),
            shape(count, 16, LM),
            shape(16, LANES),
            pltpu.VMEM((shard, LANES), jnp.bfloat16),
            pltpu.SMEM((4, count), jnp.int32),
        ),
        specs=[smem] + [vmem] * 6,
        out_specs=(vmem,) * 9 + (smem,),
    )
    sums = all_reduce(part)
    jac, cam_hot, land_hot, index, m, fac, damp_tile, select = map(
        in_vmem, (jac, cam_hot, land_hot, index, m, fac, damp_tile, select)
    )
    spots = pltpu.with_memory_space_constraint(spots, pltpu.SMEM)
    vector = pltpu.VMEM((packed(tiles), 8, LANES), f32)
    part, back = call(
        first_kernel,
        (spots, *sums, jac, cam_hot, land_hot, index, m, fac, damp_tile),
        (shape(1, packed(tiles), 8, LANES), shape(2, 3, count, LM)),
        (vector, vector),
        specs=[smem] + [vmem] * 9,
    )
    image = all_reduce(part)
    partial, known, cam_flat, solved = call(
        second_kernel,
        (spots, *sums, *image, jac, land_hot, index, m, fac, damp_tile, select),
        (shape(n_dev, 1, LANES), shape(8, LANES), shape(2, shard), shape(3, count, LM)),
        (vector, pltpu.VMEM((3, packed(tiles), 8, LANES), f32)),
        specs=[smem] + [vmem] * 11,
    )
    gathered = lax.all_to_all(partial, AXES, 0, 0, tiled=True)
    cam_step, land_step = call(
        last_kernel,
        tuple(map(in_vmem, (gathered, known, cam_flat, back, solved))),
        (jax.ShapeDtypeStruct((shard,), f32), jax.ShapeDtypeStruct((3, count, LM), f32)),
        whole=(),
    )
    return cam_step, jnp.transpose(land_step, (1, 0, 2))


def solution(mesh):
    n_row, n_col = mesh.shape["row"], mesh.shape["col"]
    both = P(AXES)
    in_specs = (P(AXES, None, None),) * 3 + (P(AXES, None),) * 3 + (both,)
    out_specs = (both, P(AXES, None, None))
    return jax.shard_map(
        functools.partial(per_device, n_row, n_col),
        mesh=mesh,
        in_specs=in_specs,
        out_specs=out_specs,
        check_vma=False,
    )
```

```python
import functools

import jax
import jax.numpy as jnp
from jax import lax
from jax.experimental import pallas as pl
from jax.experimental.pallas import tpu as pltpu
from jax.sharding import PartitionSpec as P

CAM = 64
LM = 128
LANES = 128
AXES = ("row", "col")
DAMPING = 1.0

NN = (((1,), (0,)), ((), ()))
NT = (((1,), (1,)), ((), ()))


def split3(x):
    hi = x.astype(jnp.bfloat16)
    rest = x - hi.astype(jnp.float32)
    mid = rest.astype(jnp.bfloat16)
    low = (rest - mid.astype(jnp.float32)).astype(jnp.bfloat16)
    return jnp.concatenate([hi, mid, low], axis=0)


def dot3(x, exact, dims):
    n = x.shape[0]
    y = lax.dot_general(split3(x), exact, dims, preferred_element_type=jnp.float32)
    return (y[2 * n :] + y[n : 2 * n]) + y[:n]


def onehot(index_column, lanes):
    return jnp.where(index_column == lanes, jnp.bfloat16(1), jnp.bfloat16(0))


def take_lanes(x, index_row):
    pieces = []
    for start in range(0, index_row.shape[1], LANES):
        index = jnp.broadcast_to(index_row[:, start : start + LANES], x.shape)
        pieces.append(jnp.take_along_axis(x, index, axis=1, mode="promise_in_bounds"))
    return jnp.concatenate(pieces, axis=1)


def pad_rows(x, rows):
    if x.shape[0] == rows:
        return x
    return jnp.concatenate([x, jnp.zeros((rows - x.shape[0], x.shape[1]), x.dtype)], axis=0)


def stack_rows(rows, total):
    rows = list(rows)
    if len(rows) == total:
        return jnp.concatenate(rows, axis=0)
    rows.append(jnp.zeros((total - len(rows), rows[0].shape[1]), jnp.float32))
    return jnp.concatenate(rows, axis=0)


def cholesky_three(v00, v01, v02, v11, v12, v22):
    inv_first = 1.0 / jnp.sqrt(v00)
    low_one = v01 * inv_first
    low_two = v02 * inv_first
    inv_second = 1.0 / jnp.sqrt(v11 - low_one * low_one)
    low_three = (v12 - low_two * low_one) * inv_second
    inv_third = 1.0 / jnp.sqrt(v22 - low_two * low_two - low_three * low_three)
    return (inv_first, low_one, low_two, inv_second, low_three, inv_third)


def lower_solve(factor, first, second, third):
    out_one = first * factor[0]
    out_two = (second - factor[1] * out_one) * factor[3]
    out_three = (third - factor[2] * out_one - factor[4] * out_two) * factor[5]
    return (out_one, out_two, out_three)


def upper_solve(factor, first, second, third):
    out_three = third * factor[5]
    out_two = (second - factor[4] * out_three) * factor[3]
    out_one = (first - factor[1] * out_two - factor[2] * out_three) * factor[0]
    return (out_one, out_two, out_three)


def row_list(x, count):
    return [x[i : i + 1] for i in range(count)]


def lane_ids(rows):
    return lax.broadcasted_iota(jnp.int32, (rows, LANES), 1)


def to_first(x, half):
    return pltpu.roll(x, half * CAM, 1)


def to_second(x, half):
    return pltpu.roll(x, (1 - half) * CAM, 1)


def packed(tiles):
    return tiles + tiles // 8 + 1


def load_tile(ref, tiles, t):
    ninth = ref[tiles + t // 8, pl.ds(t % 8, 1), :]
    return jnp.concatenate([ref[t], ninth, jnp.zeros((7, LANES), jnp.float32)], axis=0)


def write_ninths(ref, tiles, rows, sums=None):
    rows = list(rows) + [jnp.zeros((1, LANES), jnp.float32) if sums is None else sums]
    for start in range(0, len(rows), 8):
        ref[tiles + start // 8] = stack_rows(rows[start : start + 8], 8)


def shard_select(shard, lane_offset):
    entry = lax.broadcasted_iota(jnp.int32, (shard, LANES), 0)
    start = 9 * (lax.broadcasted_iota(jnp.int32, (shard, LANES), 1) - lane_offset)
    inside = (entry >= start) & (entry < start + 9)
    return jnp.where(inside, 1.0, 0.0).astype(jnp.bfloat16)


def param_mask(shard):
    entry = lax.broadcasted_iota(jnp.int32, (16, shard), 1).astype(jnp.float32)
    camera = jnp.floor((entry + 0.5) * (1.0 / 9.0))
    param = entry - 9.0 * camera
    return param == lax.broadcasted_iota(jnp.int32, (16, shard), 0).astype(jnp.float32)


def place(pairs_ref, k, n_row, n_col, groups):
    first = pairs_ref[0, k] - lax.axis_index("row") * (groups // n_row)
    second = pairs_ref[1, k] - lax.axis_index("col") * (groups // n_col)
    return first // 2, first % 2, second // 2, second % 2


def read_spots(spots_ref):
    return [[spots_ref[i, k] for i in range(4)] for k in range(spots_ref.shape[1])]


def write_parts(ref, row_tiles, tiles, spots, values, extra=None, sums=None):
    lower = lane_ids(values[0].shape[0]) < CAM
    firsts = [to_first(jnp.where(lower, v, 0.0), spot[1]) for v, spot in zip(values, spots)]
    seconds = [to_second(jnp.where(lower, 0.0, v), spot[3]) for v, spot in zip(values, spots)]
    ninths = []
    for t in range(tiles):
        if t < row_tiles:
            items = [(spot[0] == t, v) for v, spot in zip(firsts, spots)]
            if extra is not None:
                items.append((extra[0] == t, extra[1]))
        else:
            items = [(spot[2] == t - row_tiles, v) for v, spot in zip(seconds, spots)]
        total = sum(jnp.where(here, v, 0.0) for here, v in items)
        ref[t] = total[:8]
        ninths.append(total[8:9])
    write_ninths(ref, tiles, ninths, sums)


def own_place(n_row, n_col, cams):
    shard_cams = cams // (n_row * n_col)
    start = lax.axis_index("col") * shard_cams
    return start // LANES, start % LANES


def build_kernel(n_row, n_col, cams, pairs_ref, cam_ref, land_ref, resid_ref, ocam_ref, oland_ref, damp_ref, part_ref, jac_ref, cam_hot_ref, land_hot_ref, index_ref, m_ref, fac_ref, damp_tile_ref, select_ref, spots_ref):
    groups = cams // CAM
    row_tiles = cams // n_row // LANES
    tiles = row_tiles + cams // n_col // LANES
    count, obs = ocam_ref.shape
    each = range(count)
    shard = damp_ref.shape[0]

    index_ref[0] = ocam_ref[...]
    index_ref[1] = oland_ref[...]
    rows = jnp.concatenate([ocam_ref[...], oland_ref[...]], axis=0).astype(jnp.float32)
    columns = jnp.transpose(pad_rows(rows, (2 * count + 7) // 8 * 8)).astype(jnp.int32)
    key = (ocam_ref[...] * LM + oland_ref[...]).astype(jnp.int16)
    lanes = lax.broadcasted_iota(jnp.int32, (obs, LANES), 1).astype(jnp.int16)
    cam_columns = [columns[:, k : k + 1] for k in each]
    land_columns = [columns[:, count + k : count + k + 1] for k in each]
    for k in each:
        land_hot_ref[k] = onehot(land_columns[k].astype(jnp.int16), lanes)

    lj = [[land_ref[i, k : k + 1, :] for i in range(6)] for k in each]
    e0 = [resid_ref[k, 0:1, :] for k in each]
    e1 = [resid_ref[k, 1:2, :] for k in each]
    sums = []
    for k in each:

        def outer(i, j):
            return lj[k][i] * lj[k][j] + lj[k][3 + i] * lj[k][3 + j]

        entries = [outer(0, 0), outer(0, 1), outer(0, 2), outer(1, 1), outer(1, 2), outer(2, 2)]
        entries += [lj[k][b] * e0[k] + lj[k][3 + b] * e1[k] for b in range(3)]
        sums.append(dot3(stack_rows(entries, 16), land_hot_ref[k], NN))
    alike = []
    for k in each:
        for r in range(2):
            jac_ref[k, r, 0:8, :] = cam_ref[9 * r : 9 * r + 8, k, :]
            jac_ref[k, r, 8:16, :] = pad_rows(cam_ref[9 * r + 8 : 9 * r + 9, k, :], 8)
        j0, j1 = jac_ref[k, 0], jac_ref[k, 1]
        coupled = [j0[:8] * lj[k][b] + j1[:8] * lj[k][3 + b] for b in range(3)]
        coupled.append(stack_rows([j0[8:9] * lj[k][b] + j1[8:9] * lj[k][3 + b] for b in range(3)], 8))
        same = onehot((cam_columns[k] * LM + land_columns[k]).astype(jnp.int16), key[k : k + 1, :])
        alike.append(dot3(jnp.concatenate(coupled, axis=0), same, NN))
    total = [jnp.concatenate([sums[k][i : i + 1] for k in each], axis=0) for i in range(9)]
    factor = cholesky_three(
        total[0] + DAMPING, total[1], total[2], total[3] + DAMPING, total[4], total[5] + DAMPING
    )
    land_rows = list(factor) + list(lower_solve(factor, total[6], total[7], total[8]))
    for k in each:
        cam_hot_ref[k] = onehot(cam_columns[k].astype(jnp.int16), lanes)
    ms, ws = [], []
    for k in each:
        land_values = stack_rows([row[k : k + 1] for row in land_rows], 16)
        fac_ref[k] = land_values
        at_obs = row_list(take_lanes(land_values, oland_ref[k : k + 1, :]), 9)
        m0 = lower_solve(at_obs, lj[k][0], lj[k][1], lj[k][2])
        m1 = lower_solve(at_obs, lj[k][3], lj[k][4], lj[k][5])
        m_ref[k] = stack_rows(m0 + m1, 8)
        ms.append((at_obs, m0, m1))
        w0 = m0[0] * at_obs[6] + m0[1] * at_obs[7] + m0[2] * at_obs[8] - e0[k]
        w1 = m1[0] * at_obs[6] + m1[1] * at_obs[7] + m1[2] * at_obs[8] - e1[k]
        ws.append((w0, w1))
    both = []
    for k in each:
        j0, j1 = jac_ref[k, 0], jac_ref[k, 1]
        at_obs, m0, m1 = ms[k]
        squares = []
        for jr0, jr1, products in (
            (j0[:8], j1[:8], [alike[k][8 * b : 8 * b + 8] for b in range(3)]),
            (j0[8:9], j1[8:9], [alike[k][24 + b : 25 + b] for b in range(3)]),
        ):
            solved = lower_solve(at_obs, *products)
            squares.append(sum((jr0 * m0[b] + jr1 * m1[b]) * solved[b] for b in range(3)))
        diag = j0 * j0 + j1 * j1 - jnp.concatenate([squares[0], pad_rows(squares[1], 8)], axis=0)
        rhs = j0 * ws[k][0] + j1 * ws[k][1]
        both.append(dot3(jnp.concatenate([rhs, diag], axis=0), cam_hot_ref[k], NN))

    own_tile, own_lane = own_place(n_row, n_col, cams)
    spread = jnp.where(param_mask(shard), damp_ref[...].reshape(1, shard), 0.0)
    select = shard_select(shard, own_lane)
    select_ref[...] = select
    damp_tile = dot3(spread, select, NN)
    damp_tile_ref[...] = damp_tile
    spots = [place(pairs_ref, k, n_row, n_col, groups) for k in each]
    for k in each:
        for i in range(4):
            spots_ref[i, k] = spots[k][i]
    write_parts(part_ref.at[0], row_tiles, tiles, spots, [x[:16] for x in both])
    write_parts(part_ref.at[1], row_tiles, tiles, spots, [x[16:] for x in both], (own_tile, damp_tile))


def half_product(p_ref, row_tiles, tiles, spots, jac_ref, land_hot_ref, index_ref, m_ref):
    each = range(jac_ref.shape[0])
    lower = lane_ids(16) < CAM
    u, m, y_land = [], [], []
    for k in each:
        t_first, h_first, t_second, h_second = spots[k]
        p_first = to_first(load_tile(p_ref, tiles, t_first), h_first)
        p_second = to_second(load_tile(p_ref, tiles, row_tiles + t_second), h_second)
        at_obs = take_lanes(jnp.where(lower, p_first, p_second), index_ref[0, k : k + 1, :])
        u.append([jnp.sum(jac_ref[k, r] * at_obs, axis=0, keepdims=True) for r in range(2)])
    for k in each:
        m.append([m_ref[k, i : i + 1, :] for i in range(6)])
        y = [m[k][b] * u[k][0] + m[k][3 + b] * u[k][1] for b in range(3)]
        y_land.append(dot3(stack_rows(y, 16), land_hot_ref[k], NN)[:8])
    return u, m, y_land


def reduced_rows(u, m, y_land, index_ref):
    out = []
    for k in range(len(u)):
        y = row_list(take_lanes(y_land[k], index_ref[1, k : k + 1, :]), 3)
        out.append([u[k][r] - (m[k][3 * r] * y[0] + m[k][3 * r + 1] * y[1] + m[k][3 * r + 2] * y[2]) for r in range(2)])
    return out


def back_solve(fac_ref, k, rows):
    factor = row_list(fac_ref[k], 9)
    return upper_solve(factor, *rows), factor


def total_sum(x):
    return jnp.sum(jnp.sum(x, axis=0, keepdims=True), axis=1, keepdims=True)


def own_lanes(own_lane, shard_cams):
    ids = lane_ids(16)
    return (ids >= own_lane) & (ids < own_lane + shard_cams)


def in_lanes(values):
    ids = lane_ids(1)
    row = jnp.zeros((1, LANES), jnp.float32)
    for lane, value in enumerate(values):
        row = jnp.where(ids == lane, value, row)
    return row


def energy_sum(u, v):
    return total_sum(sum(u[k][r] * v[k][r] for k in range(len(u)) for r in range(2)))


def add_up(refs):
    total = refs[0][...]
    for ref in refs[1:]:
        total = total + ref[...]
    return total


def first_kernel(n_row, n_col, cams, pieces, spots_ref, jac_ref, cam_hot_ref, land_hot_ref, index_ref, m_ref, fac_ref, damp_tile_ref, *refs):
    part_ref, back_ref, right_ref, precond_ref, p_ref = refs[pieces:]
    row_tiles = cams // n_row // LANES
    tiles = row_tiles + cams // n_col // LANES
    each = range(jac_ref.shape[0])
    sums = add_up(refs[:pieces])
    right, precond = sums[0], 1.0 / sums[1]
    right_ref[...] = right
    precond_ref[...] = precond
    p_ref[...] = right * precond
    spots = read_spots(spots_ref)
    u, m, y_land = half_product(p_ref, row_tiles, tiles, spots, jac_ref, land_hot_ref, index_ref, m_ref)
    v = reduced_rows(u, m, y_land, index_ref)
    images = [dot3(jac_ref[k, 0] * v[k][0] + jac_ref[k, 1] * v[k][1], cam_hot_ref[k], NN) for k in each]
    own_tile, own_lane = own_place(n_row, n_col, cams)
    own = load_tile(p_ref, tiles, own_tile)
    damped = own * damp_tile_ref[...]
    mask = own_lanes(own_lane, cams // (n_row * n_col))
    norm_now = total_sum(jnp.where(mask, own * load_tile(right_ref, tiles, own_tile), 0.0))
    energy = energy_sum(u, v) + total_sum(own * damped)
    for k in each:
        solved, factor = back_solve(fac_ref, k, row_list(y_land[k], 3))
        from_t = upper_solve(factor, factor[6], factor[7], factor[8])
        for b in range(3):
            back_ref[0, b, k : k + 1, :] = from_t[b]
            back_ref[1, b, k : k + 1, :] = solved[b]
    write_parts(part_ref.at[0], row_tiles, tiles, spots, images, (own_tile, damped), in_lanes([norm_now, energy]))


def second_kernel(n_row, n_col, cams, pieces, spots_ref, jac_ref, land_hot_ref, index_ref, m_ref, fac_ref, damp_tile_ref, select_ref, right_ref, precond_ref, *refs):
    sums_ref, known_ref, cam_ref, solved_ref, p_ref, scratch_ref = refs[pieces:]
    row_tiles = cams // n_row // LANES
    tiles = row_tiles + cams // n_col // LANES
    each = range(jac_ref.shape[0])
    shard = cam_ref.shape[1]
    image = add_up(refs[:pieces])[0]
    sums = image[tiles + tiles // 8, tiles % 8 : tiles % 8 + 1]
    norm_now, energy_now = sums[:, 0:1], sums[:, 1:2]
    alpha = norm_now / energy_now
    for i, value in enumerate((1.0 / norm_now, energy_now, alpha)):
        known_ref[i : i + 1, :] = jnp.broadcast_to(value, (1, LANES))
    right, precond = right_ref[...], precond_ref[...]
    residual = right - alpha * image
    p_ref[...] = precond * residual
    scratch_ref[0] = right * precond
    scratch_ref[1] = residual
    scratch_ref[2] = image
    spots = read_spots(spots_ref)
    u, m, y_land = half_product(p_ref, row_tiles, tiles, spots, jac_ref, land_hot_ref, index_ref, m_ref)
    v = reduced_rows(u, m, y_land, index_ref)

    own_tile, own_lane = own_place(n_row, n_col, cams)
    own = load_tile(p_ref, tiles, own_tile)
    own_start, own_residual, own_image = [load_tile(scratch_ref.at[i], tiles, own_tile) for i in range(3)]
    flat = dot3(jnp.concatenate([own_start, own], axis=0), select_ref[...], NT)
    params = param_mask(shard)
    for i in range(2):
        cam_ref[i : i + 1, :] = jnp.sum(jnp.where(params, flat[16 * i : 16 * i + 16], 0.0), axis=0, keepdims=True)
    mask = own_lanes(own_lane, cams // (n_row * n_col))
    norm_next = total_sum(jnp.where(mask, own * own_residual, 0.0))
    cross = total_sum(jnp.where(mask, own * own_image, 0.0))
    energy = energy_sum(u, v) + total_sum(own * own * damp_tile_ref[...])
    sums_ref[...] = jnp.broadcast_to(in_lanes([energy, norm_next, cross])[None], sums_ref.shape)
    for k in each:
        solved, _ = back_solve(fac_ref, k, row_list(y_land[k], 3))
        for b in range(3):
            solved_ref[b, k : k + 1, :] = solved[b]


def last_kernel(sums_ref, known_ref, cam_ref, back_ref, solved_ref, cam_out_ref, land_out_ref):
    sums = jnp.sum(sums_ref[...], axis=0)
    energy, norm_next, cross = [jnp.broadcast_to(sums[:, i : i + 1], (1, LANES)) for i in range(3)]
    inverse_now, energy_now, alpha = [known_ref[i : i + 1, :] for i in range(3)]
    beta = norm_next * inverse_now
    slope = norm_next / (energy + beta * (2.0 * cross + beta * energy_now))
    first = alpha + slope * beta
    shard = cam_ref.shape[1]
    repeats = (shard + LANES - 1) // LANES
    first_wide, slope_wide = [jnp.concatenate([x] * repeats, axis=1)[:, :shard] for x in (first, slope)]
    cam_step = first_wide * cam_ref[0:1, :] + slope_wide * cam_ref[1:2, :]
    cam_out_ref[...] = cam_step.reshape(cam_out_ref.shape)
    land_out_ref[...] = -(back_ref[0] + first[None] * back_ref[1] + slope[None] * solved_ref[...])


def core_kernel(n_row, n_col, cams, radix, *refs):
    part_refs, out_refs, (whole_ref, ninth_ref) = refs[:radix], refs[radix:-2], refs[-2:]
    row_tiles = cams // n_row // LANES
    col_tiles = cams // n_col // LANES
    tiles = row_tiles + col_tiles
    low = n_row // radix
    row, col = lax.axis_index("row"), lax.axis_index("col")
    for v in range(whole_ref.shape[0]):
        parts = [ref[v] for ref in part_refs]
        received = parts[1]
        for part in parts[2:]:
            received = received + part
        row_sums = tiles + tiles // 8, tiles % 8
        sums = (parts[0] + received)[row_sums[0], row_sums[1] : row_sums[1] + 1]
        whole_ref[v] = jnp.zeros(whole_ref.shape[1:], jnp.float32)
        ninth_ref[v] = jnp.zeros(ninth_ref.shape[1:], jnp.float32)
        columns = [(col, parts[0]), (col ^ 1, received)]
        for column, total in columns:
            for i in range(col_tiles):
                t = row_tiles + i
                whole_ref[v, column * col_tiles + i] = total[t]
                ninth_ref[v, pl.ds(column * col_tiles + i, 1), :] = total[tiles + t // 8, t % 8 : t % 8 + 1]
        for digit, part in enumerate(parts):
            start = (row ^ (digit * low)) * row_tiles
            for i in range(row_tiles):
                whole_ref[v, start + i] += part[i]
                ninth_ref[v, pl.ds(start + i, 1), :] += part[tiles + i // 8, i % 8 : i % 8 + 1]
        for core, out_ref in zip((col % 2, 1 - col % 2), out_refs):
            places = [(2 * y + 1 - core) * col_tiles + i for y in range(n_col // 2) for i in range(col_tiles)]
            places += [(col // 2 * 2 + core) * col_tiles + i for i in range(col_tiles)]
            places += [row // low * (low * row_tiles) + i for i in range(low * row_tiles)]
            for i, t in enumerate(places):
                out_ref[v, i] = whole_ref[v, t]
            write_ninths(out_ref.at[v], len(places), [ninth_ref[v, pl.ds(t, 1), :] for t in places], sums)


def spread_kernel(n_row, n_col, cams, radix, masks, mine_ref, other_ref, *refs):
    out_refs, total_ref = refs[:-1], refs[-1]
    row_tiles = cams // n_row // LANES
    col_tiles = cams // n_col // LANES
    tiles = row_tiles + col_tiles
    low = n_row // radix
    col_sent = n_col // 2 * col_tiles
    sent = col_sent + col_tiles + low * row_tiles
    row, col = lax.axis_index("row") % low, lax.axis_index("col") // 2
    for v in range(total_ref.shape[0]):
        total = mine_ref[v] + other_ref[v]
        total_ref[v] = total
        sums = total[sent + sent // 8, sent % 8 : sent % 8 + 1]
        for mask, out_ref in zip(masks, out_refs):
            row_start = col_sent + col_tiles + (row ^ (mask // n_col)) * row_tiles
            col_start = (col ^ (mask % n_col // 2)) * col_tiles if mask else col_sent
            places = [row_start + i for i in range(row_tiles)] + [col_start + i for i in range(col_tiles)]
            for i, t in enumerate(places):
                out_ref[v, i] = total_ref[v, t]
            ninths = [total_ref[v, sent + t // 8, pl.ds(t % 8, 1), :] for t in places]
            write_ninths(out_ref.at[v], tiles, ninths, sums)


def exchange(x, masks, n_dev):
    return [lax.ppermute(x, AXES, [(i, i ^ mask) for i in range(n_dev)]) for mask in masks]


def in_vmem(x):
    return pltpu.with_memory_space_constraint(x, pltpu.VMEM)


def per_device(n_row, n_col, cam_jac, land_jac, resid, obs_cam, obs_land, pairs, cam_damp):
    f32 = jnp.float32
    count, _, obs = cam_jac.shape
    shard = cam_damp.shape[0]
    n_dev = n_row * n_col
    cams = shard * n_dev // 9
    row_tiles = cams // n_row // LANES
    col_tiles = cams // n_col // LANES
    tiles = row_tiles + col_tiles
    vmem = pl.BlockSpec(memory_space=pltpu.VMEM)
    smem = pl.BlockSpec(memory_space=pltpu.SMEM)

    def shape(*dims):
        return pltpu.VMEM(dims, f32)

    radix = min(n_row, 4)
    low = n_row // radix
    sent = n_col // 2 * col_tiles + col_tiles + low * row_tiles
    lead = [digit * low * n_col + 1 for digit in range(1, radix)]
    middle = [x * n_col + y * 2 for x in range(low) for y in range(n_col // 2)]
    middle = middle[:1] + [mask + 1 for mask in middle[:0:-1]]

    def call(kernel, operands, out_shape, scratch=(), whole=(n_row, n_col, cams), specs=None, out_specs=None):
        return pl.pallas_call(
            functools.partial(kernel, *whole),
            out_shape=out_shape,
            in_specs=specs or [vmem] * len(operands),
            out_specs=out_specs or jax.tree.map(lambda _: vmem, out_shape),
            scratch_shapes=scratch,
        )(*operands)

    def all_reduce(part):
        vectors = part.shape[0]
        pieces = [part] + exchange(part, lead, n_dev)
        mine, other = call(
            core_kernel,
            tuple(map(in_vmem, pieces)),
            (shape(vectors, packed(sent), 8, LANES),) * 2,
            (pltpu.VMEM((vectors, cams // LANES, 8, LANES), f32), pltpu.VMEM((vectors, cams // LANES, LANES), f32)),
            (n_row, n_col, cams, radix),
        )
        (other,) = exchange(other, [1], n_dev)
        to_send = call(
            spread_kernel,
            (in_vmem(mine), in_vmem(other)),
            (shape(vectors, packed(tiles), 8, LANES),) * len(middle),
            (pltpu.VMEM((vectors, packed(sent), 8, LANES), f32),),
            (n_row, n_col, cams, radix, tuple(middle)),
        )
        got = [to_send[0]] + [exchange(x, [mask], n_dev)[0] for x, mask in zip(to_send[1:], middle[1:])]
        return tuple(map(in_vmem, got))

    hot = pltpu.VMEM((count, obs, LANES), jnp.bfloat16)
    part, jac, cam_hot, land_hot, index, m, fac, damp_tile, select, spots = call(
        build_kernel,
        (
            pairs.T,
            jnp.transpose(cam_jac, (1, 0, 2)),
            jnp.transpose(land_jac, (1, 0, 2)),
            resid,
            obs_cam,
            obs_land,
            cam_damp,
        ),
        (
            shape(2, packed(tiles), 8, LANES),
            shape(count, 2, 16, obs),
            hot,
            hot,
            pltpu.VMEM((2, count, obs), jnp.int32),
            shape(count, 8, obs),
            shape(count, 16, LM),
            shape(16, LANES),
            pltpu.VMEM((shard, LANES), jnp.bfloat16),
            pltpu.SMEM((4, count), jnp.int32),
        ),
        specs=[smem] + [vmem] * 6,
        out_specs=(vmem,) * 9 + (smem,),
    )
    sums = all_reduce(part)
    jac, cam_hot, land_hot, index, m, fac, damp_tile, select = map(
        in_vmem, (jac, cam_hot, land_hot, index, m, fac, damp_tile, select)
    )
    spots = pltpu.with_memory_space_constraint(spots, pltpu.SMEM)
    pieces = len(middle)
    vector = pltpu.VMEM((packed(tiles), 8, LANES), f32)
    part, back, right, precond = call(
        first_kernel,
        (spots, jac, cam_hot, land_hot, index, m, fac, damp_tile, *sums),
        (shape(1, packed(tiles), 8, LANES), shape(2, 3, count, LM), vector, vector),
        (vector,),
        (n_row, n_col, cams, pieces),
        specs=[smem] + [vmem] * (7 + pieces),
    )
    image = all_reduce(part)
    partial, known, cam_flat, solved = call(
        second_kernel,
        (spots, jac, land_hot, index, m, fac, damp_tile, select, in_vmem(right), in_vmem(precond), *image),
        (shape(n_dev, 1, LANES), shape(8, LANES), shape(2, shard), shape(3, count, LM)),
        (vector, pltpu.VMEM((3, packed(tiles), 8, LANES), f32)),
        (n_row, n_col, cams, pieces),
        specs=[smem] + [vmem] * (9 + pieces),
    )
    gathered = lax.all_to_all(partial, AXES, 0, 0, tiled=True)
    cam_step, land_step = call(
        last_kernel,
        tuple(map(in_vmem, (gathered, known, cam_flat, back, solved))),
        (jax.ShapeDtypeStruct((shard,), f32), jax.ShapeDtypeStruct((3, count, LM), f32)),
        whole=(),
    )
    return cam_step, jnp.transpose(land_step, (1, 0, 2))


def solution(mesh):
    n_row, n_col = mesh.shape["row"], mesh.shape["col"]
    both = P(AXES)
    in_specs = (P(AXES, None, None),) * 3 + (P(AXES, None),) * 3 + (both,)
    out_specs = (both, P(AXES, None, None))
    return jax.shard_map(
        functools.partial(per_device, n_row, n_col),
        mesh=mesh,
        in_specs=in_specs,
        out_specs=out_specs,
        check_vma=False,
    )
```

```python
import functools

import jax
import jax.numpy as jnp
from jax import lax
from jax.experimental import pallas as pl
from jax.experimental.pallas import tpu as pltpu
from jax.sharding import PartitionSpec as P

CAM = 64
LM = 128
LANES = 128
AXES = ("row", "col")
DAMPING = 1.0

NN = (((1,), (0,)), ((), ()))
NT = (((1,), (1,)), ((), ()))


def split3(x):
    hi = x.astype(jnp.bfloat16)
    rest = x - hi.astype(jnp.float32)
    mid = rest.astype(jnp.bfloat16)
    low = (rest - mid.astype(jnp.float32)).astype(jnp.bfloat16)
    return jnp.concatenate([hi, mid, low], axis=0)


def dot3(x, exact, dims):
    n = x.shape[0]
    y = lax.dot_general(split3(x), exact, dims, preferred_element_type=jnp.float32)
    return (y[2 * n :] + y[n : 2 * n]) + y[:n]


def onehot(index_column, lanes):
    return jnp.where(index_column == lanes, jnp.bfloat16(1), jnp.bfloat16(0))


def take_lanes(x, index_row):
    pieces = []
    for start in range(0, index_row.shape[1], LANES):
        index = jnp.broadcast_to(index_row[:, start : start + LANES], x.shape)
        pieces.append(jnp.take_along_axis(x, index, axis=1, mode="promise_in_bounds"))
    return jnp.concatenate(pieces, axis=1)


def pad_rows(x, rows):
    if x.shape[0] == rows:
        return x
    return jnp.concatenate([x, jnp.zeros((rows - x.shape[0], x.shape[1]), x.dtype)], axis=0)


def stack_rows(rows, total):
    rows = list(rows)
    if len(rows) == total:
        return jnp.concatenate(rows, axis=0)
    rows.append(jnp.zeros((total - len(rows), rows[0].shape[1]), jnp.float32))
    return jnp.concatenate(rows, axis=0)


def cholesky_three(v00, v01, v02, v11, v12, v22):
    inv_first = 1.0 / jnp.sqrt(v00)
    low_one = v01 * inv_first
    low_two = v02 * inv_first
    inv_second = 1.0 / jnp.sqrt(v11 - low_one * low_one)
    low_three = (v12 - low_two * low_one) * inv_second
    inv_third = 1.0 / jnp.sqrt(v22 - low_two * low_two - low_three * low_three)
    return (inv_first, low_one, low_two, inv_second, low_three, inv_third)


def lower_solve(factor, first, second, third):
    out_one = first * factor[0]
    out_two = (second - factor[1] * out_one) * factor[3]
    out_three = (third - factor[2] * out_one - factor[4] * out_two) * factor[5]
    return (out_one, out_two, out_three)


def upper_solve(factor, first, second, third):
    out_three = third * factor[5]
    out_two = (second - factor[4] * out_three) * factor[3]
    out_one = (first - factor[1] * out_two - factor[2] * out_three) * factor[0]
    return (out_one, out_two, out_three)


def row_list(x, count):
    return [x[i : i + 1] for i in range(count)]


def lane_ids(rows):
    return lax.broadcasted_iota(jnp.int32, (rows, LANES), 1)


def to_first(x, half):
    return pltpu.roll(x, half * CAM, 1)


def to_second(x, half):
    return pltpu.roll(x, (1 - half) * CAM, 1)


def packed(tiles, more=0):
    return tiles + (tiles + more) // 8 + 1


def load_tile(ref, tiles, t):
    ninth = ref[tiles + t // 8, pl.ds(t % 8, 1), :]
    return jnp.concatenate([ref[t], ninth, jnp.zeros((7, LANES), jnp.float32)], axis=0)


def write_ninths(ref, tiles, rows, sums=None, more=()):
    rows = list(rows) + [jnp.zeros((1, LANES), jnp.float32) if sums is None else sums] + list(more)
    for start in range(0, len(rows), 8):
        ref[tiles + start // 8] = stack_rows(rows[start : start + 8], 8)


def shard_select(shard, lane_offset):
    entry = lax.broadcasted_iota(jnp.int32, (shard, LANES), 0)
    start = 9 * (lax.broadcasted_iota(jnp.int32, (shard, LANES), 1) - lane_offset)
    inside = (entry >= start) & (entry < start + 9)
    return jnp.where(inside, 1.0, 0.0).astype(jnp.bfloat16)


def param_mask(shard):
    entry = lax.broadcasted_iota(jnp.int32, (16, shard), 1).astype(jnp.float32)
    camera = jnp.floor((entry + 0.5) * (1.0 / 9.0))
    param = entry - 9.0 * camera
    return param == lax.broadcasted_iota(jnp.int32, (16, shard), 0).astype(jnp.float32)


def place(pairs_ref, k, n_row, n_col, groups):
    first = pairs_ref[0, k] - lax.axis_index("row") * (groups // n_row)
    second = pairs_ref[1, k] - lax.axis_index("col") * (groups // n_col)
    return first // 2, first % 2, second // 2, second % 2


def read_spots(spots_ref):
    return [[spots_ref[i, k] for i in range(4)] for k in range(spots_ref.shape[1])]


def write_parts(ref, row_tiles, spots, values, extra=None, sums=None):
    lower = lane_ids(values[0].shape[0]) < CAM
    firsts = [to_first(jnp.where(lower, v, 0.0), spot[1]) for v, spot in zip(values, spots)]
    tiles = []
    for t in range(row_tiles):
        items = [(spot[0] == t, v) for v, spot in zip(firsts, spots)]
        if extra is not None:
            items.append((extra[0] == t, extra[1]))
        tiles.append(sum(jnp.where(here, v, 0.0) for here, v in items))
    groups = []
    left = lane_ids(1) < CAM
    for k in range(0, len(values), 2):
        other = min(k + 1, len(values) - 1)
        second = values[other] if other > k else jnp.zeros_like(values[k])
        tiles.append(jnp.where(lower, pltpu.roll(values[k], CAM, 1), second))
        ids = [2 * spots[i][2] + spots[i][3] for i in (k, other)]
        groups.append(jnp.where(left, ids[0], ids[1]).astype(jnp.float32))
    for t, tile in enumerate(tiles):
        ref[t] = tile[:8]
    write_ninths(ref, len(tiles), [tile[8:9] for tile in tiles], sums, groups)


def own_place(n_row, n_col, cams):
    shard_cams = cams // (n_row * n_col)
    start = lax.axis_index("col") * shard_cams
    return start // LANES, start % LANES


def build_kernel(n_row, n_col, cams, pairs_ref, cam_ref, land_ref, resid_ref, ocam_ref, oland_ref, damp_ref, part_ref, jac_ref, cam_hot_ref, land_hot_ref, index_ref, m_ref, fac_ref, damp_tile_ref, select_ref, spots_ref):
    groups = cams // CAM
    row_tiles = cams // n_row // LANES
    tiles = row_tiles + cams // n_col // LANES
    count, obs = ocam_ref.shape
    each = range(count)
    shard = damp_ref.shape[0]

    index_ref[0] = ocam_ref[...]
    index_ref[1] = oland_ref[...]
    rows = jnp.concatenate([ocam_ref[...], oland_ref[...]], axis=0).astype(jnp.float32)
    columns = jnp.transpose(pad_rows(rows, (2 * count + 7) // 8 * 8)).astype(jnp.int32)
    key = (ocam_ref[...] * LM + oland_ref[...]).astype(jnp.int16)
    lanes = lax.broadcasted_iota(jnp.int32, (obs, LANES), 1).astype(jnp.int16)
    cam_columns = [columns[:, k : k + 1] for k in each]
    land_columns = [columns[:, count + k : count + k + 1] for k in each]
    for k in each:
        land_hot_ref[k] = onehot(land_columns[k].astype(jnp.int16), lanes)

    lj = [[land_ref[i, k : k + 1, :] for i in range(6)] for k in each]
    e0 = [resid_ref[k, 0:1, :] for k in each]
    e1 = [resid_ref[k, 1:2, :] for k in each]
    sums = []
    for k in each:

        def outer(i, j):
            return lj[k][i] * lj[k][j] + lj[k][3 + i] * lj[k][3 + j]

        entries = [outer(0, 0), outer(0, 1), outer(0, 2), outer(1, 1), outer(1, 2), outer(2, 2)]
        entries += [lj[k][b] * e0[k] + lj[k][3 + b] * e1[k] for b in range(3)]
        sums.append(dot3(stack_rows(entries, 16), land_hot_ref[k], NN))
    alike = []
    for k in each:
        for r in range(2):
            jac_ref[k, r, 0:8, :] = cam_ref[9 * r : 9 * r + 8, k, :]
            jac_ref[k, r, 8:16, :] = pad_rows(cam_ref[9 * r + 8 : 9 * r + 9, k, :], 8)
        j0, j1 = jac_ref[k, 0], jac_ref[k, 1]
        coupled = [j0[:8] * lj[k][b] + j1[:8] * lj[k][3 + b] for b in range(3)]
        coupled.append(stack_rows([j0[8:9] * lj[k][b] + j1[8:9] * lj[k][3 + b] for b in range(3)], 8))
        same = onehot((cam_columns[k] * LM + land_columns[k]).astype(jnp.int16), key[k : k + 1, :])
        alike.append(dot3(jnp.concatenate(coupled, axis=0), same, NN))
    total = [jnp.concatenate([sums[k][i : i + 1] for k in each], axis=0) for i in range(9)]
    factor = cholesky_three(
        total[0] + DAMPING, total[1], total[2], total[3] + DAMPING, total[4], total[5] + DAMPING
    )
    land_rows = list(factor) + list(lower_solve(factor, total[6], total[7], total[8]))
    for k in each:
        cam_hot_ref[k] = onehot(cam_columns[k].astype(jnp.int16), lanes)
    ms, ws = [], []
    for k in each:
        land_values = stack_rows([row[k : k + 1] for row in land_rows], 16)
        fac_ref[k] = land_values
        at_obs = row_list(take_lanes(land_values, oland_ref[k : k + 1, :]), 9)
        m0 = lower_solve(at_obs, lj[k][0], lj[k][1], lj[k][2])
        m1 = lower_solve(at_obs, lj[k][3], lj[k][4], lj[k][5])
        m_ref[k] = stack_rows(m0 + m1, 8)
        ms.append((at_obs, m0, m1))
        w0 = m0[0] * at_obs[6] + m0[1] * at_obs[7] + m0[2] * at_obs[8] - e0[k]
        w1 = m1[0] * at_obs[6] + m1[1] * at_obs[7] + m1[2] * at_obs[8] - e1[k]
        ws.append((w0, w1))
    both = []
    for k in each:
        j0, j1 = jac_ref[k, 0], jac_ref[k, 1]
        at_obs, m0, m1 = ms[k]
        squares = []
        for jr0, jr1, products in (
            (j0[:8], j1[:8], [alike[k][8 * b : 8 * b + 8] for b in range(3)]),
            (j0[8:9], j1[8:9], [alike[k][24 + b : 25 + b] for b in range(3)]),
        ):
            solved = lower_solve(at_obs, *products)
            squares.append(sum((jr0 * m0[b] + jr1 * m1[b]) * solved[b] for b in range(3)))
        diag = j0 * j0 + j1 * j1 - jnp.concatenate([squares[0], pad_rows(squares[1], 8)], axis=0)
        rhs = j0 * ws[k][0] + j1 * ws[k][1]
        both.append(dot3(jnp.concatenate([rhs, diag], axis=0), cam_hot_ref[k], NN))

    own_tile, own_lane = own_place(n_row, n_col, cams)
    spread = jnp.where(param_mask(shard), damp_ref[...].reshape(1, shard), 0.0)
    select = shard_select(shard, own_lane)
    select_ref[...] = select
    damp_tile = dot3(spread, select, NN)
    damp_tile_ref[...] = damp_tile
    spots = [place(pairs_ref, k, n_row, n_col, groups) for k in each]
    for k in each:
        for i in range(4):
            spots_ref[i, k] = spots[k][i]
    write_parts(part_ref.at[0], row_tiles, spots, [x[:16] for x in both])
    write_parts(part_ref.at[1], row_tiles, spots, [x[16:] for x in both], (own_tile, damp_tile))


def half_product(p_ref, row_tiles, tiles, spots, jac_ref, land_hot_ref, index_ref, m_ref):
    each = range(jac_ref.shape[0])
    lower = lane_ids(16) < CAM
    u, m, y_land = [], [], []
    for k in each:
        t_first, h_first, t_second, h_second = spots[k]
        p_first = to_first(load_tile(p_ref, tiles, t_first), h_first)
        p_second = to_second(load_tile(p_ref, tiles, row_tiles + t_second), h_second)
        at_obs = take_lanes(jnp.where(lower, p_first, p_second), index_ref[0, k : k + 1, :])
        u.append([jnp.sum(jac_ref[k, r] * at_obs, axis=0, keepdims=True) for r in range(2)])
    for k in each:
        m.append([m_ref[k, i : i + 1, :] for i in range(6)])
        y = [m[k][b] * u[k][0] + m[k][3 + b] * u[k][1] for b in range(3)]
        y_land.append(dot3(stack_rows(y, 16), land_hot_ref[k], NN)[:8])
    return u, m, y_land


def reduced_rows(u, m, y_land, index_ref):
    out = []
    for k in range(len(u)):
        y = row_list(take_lanes(y_land[k], index_ref[1, k : k + 1, :]), 3)
        out.append([u[k][r] - (m[k][3 * r] * y[0] + m[k][3 * r + 1] * y[1] + m[k][3 * r + 2] * y[2]) for r in range(2)])
    return out


def back_solve(fac_ref, k, rows):
    factor = row_list(fac_ref[k], 9)
    return upper_solve(factor, *rows), factor


def total_sum(x):
    return jnp.sum(jnp.sum(x, axis=0, keepdims=True), axis=1, keepdims=True)


def own_lanes(own_lane, shard_cams):
    ids = lane_ids(16)
    return (ids >= own_lane) & (ids < own_lane + shard_cams)


def in_lanes(values):
    ids = lane_ids(1)
    row = jnp.zeros((1, LANES), jnp.float32)
    for lane, value in enumerate(values):
        row = jnp.where(ids == lane, value, row)
    return row


def energy_sum(u, v):
    return total_sum(sum(u[k][r] * v[k][r] for k in range(len(u)) for r in range(2)))


def add_up(refs):
    total = refs[0][...]
    for ref in refs[1:]:
        total = total + ref[...]
    return total


def first_kernel(n_row, n_col, cams, pieces, spots_ref, jac_ref, cam_hot_ref, land_hot_ref, index_ref, m_ref, fac_ref, damp_tile_ref, *refs):
    part_ref, back_ref, right_ref, precond_ref, p_ref = refs[pieces:]
    row_tiles = cams // n_row // LANES
    tiles = row_tiles + cams // n_col // LANES
    each = range(jac_ref.shape[0])
    sums = add_up(refs[:pieces])
    right, precond = sums[0], 1.0 / sums[1]
    right_ref[...] = right
    precond_ref[...] = precond
    p_ref[...] = right * precond
    spots = read_spots(spots_ref)
    u, m, y_land = half_product(p_ref, row_tiles, tiles, spots, jac_ref, land_hot_ref, index_ref, m_ref)
    v = reduced_rows(u, m, y_land, index_ref)
    images = [dot3(jac_ref[k, 0] * v[k][0] + jac_ref[k, 1] * v[k][1], cam_hot_ref[k], NN) for k in each]
    own_tile, own_lane = own_place(n_row, n_col, cams)
    own = load_tile(p_ref, tiles, own_tile)
    damped = own * damp_tile_ref[...]
    mask = own_lanes(own_lane, cams // (n_row * n_col))
    norm_now = total_sum(jnp.where(mask, own * load_tile(right_ref, tiles, own_tile), 0.0))
    energy = energy_sum(u, v) + total_sum(own * damped)
    for k in each:
        solved, factor = back_solve(fac_ref, k, row_list(y_land[k], 3))
        from_t = upper_solve(factor, factor[6], factor[7], factor[8])
        for b in range(3):
            back_ref[0, b, k : k + 1, :] = from_t[b]
            back_ref[1, b, k : k + 1, :] = solved[b]
    write_parts(part_ref.at[0], row_tiles, spots, images, (own_tile, damped), in_lanes([norm_now, energy]))


def second_kernel(n_row, n_col, cams, pieces, spots_ref, jac_ref, land_hot_ref, index_ref, m_ref, fac_ref, damp_tile_ref, select_ref, right_ref, precond_ref, *refs):
    sums_ref, known_ref, cam_ref, solved_ref, p_ref, scratch_ref = refs[pieces:]
    row_tiles = cams // n_row // LANES
    tiles = row_tiles + cams // n_col // LANES
    each = range(jac_ref.shape[0])
    shard = cam_ref.shape[1]
    image = add_up(refs[:pieces])[0]
    sums = image[tiles + tiles // 8, tiles % 8 : tiles % 8 + 1]
    norm_now, energy_now = sums[:, 0:1], sums[:, 1:2]
    alpha = norm_now / energy_now
    for i, value in enumerate((1.0 / norm_now, energy_now, alpha)):
        known_ref[i : i + 1, :] = jnp.broadcast_to(value, (1, LANES))
    right, precond = right_ref[...], precond_ref[...]
    residual = right - alpha * image
    p_ref[...] = precond * residual
    scratch_ref[0] = right * precond
    scratch_ref[1] = residual
    scratch_ref[2] = image
    spots = read_spots(spots_ref)
    u, m, y_land = half_product(p_ref, row_tiles, tiles, spots, jac_ref, land_hot_ref, index_ref, m_ref)
    v = reduced_rows(u, m, y_land, index_ref)

    own_tile, own_lane = own_place(n_row, n_col, cams)
    own = load_tile(p_ref, tiles, own_tile)
    own_start, own_residual, own_image = [load_tile(scratch_ref.at[i], tiles, own_tile) for i in range(3)]
    flat = dot3(jnp.concatenate([own_start, own], axis=0), select_ref[...], NT)
    params = param_mask(shard)
    for i in range(2):
        cam_ref[i : i + 1, :] = jnp.sum(jnp.where(params, flat[16 * i : 16 * i + 16], 0.0), axis=0, keepdims=True)
    mask = own_lanes(own_lane, cams // (n_row * n_col))
    norm_next = total_sum(jnp.where(mask, own * own_residual, 0.0))
    cross = total_sum(jnp.where(mask, own * own_image, 0.0))
    energy = energy_sum(u, v) + total_sum(own * own * damp_tile_ref[...])
    sums_ref[...] = jnp.broadcast_to(in_lanes([energy, norm_next, cross])[None], sums_ref.shape)
    for k in each:
        solved, _ = back_solve(fac_ref, k, row_list(y_land[k], 3))
        for b in range(3):
            solved_ref[b, k : k + 1, :] = solved[b]


def last_kernel(sums_ref, known_ref, cam_ref, back_ref, solved_ref, cam_out_ref, land_out_ref):
    sums = jnp.sum(sums_ref[...], axis=0)
    energy, norm_next, cross = [jnp.broadcast_to(sums[:, i : i + 1], (1, LANES)) for i in range(3)]
    inverse_now, energy_now, alpha = [known_ref[i : i + 1, :] for i in range(3)]
    beta = norm_next * inverse_now
    slope = norm_next / (energy + beta * (2.0 * cross + beta * energy_now))
    first = alpha + slope * beta
    shard = cam_ref.shape[1]
    repeats = (shard + LANES - 1) // LANES
    first_wide, slope_wide = [jnp.concatenate([x] * repeats, axis=1)[:, :shard] for x in (first, slope)]
    cam_step = first_wide * cam_ref[0:1, :] + slope_wide * cam_ref[1:2, :]
    cam_out_ref[...] = cam_step.reshape(cam_out_ref.shape)
    land_out_ref[...] = -(back_ref[0] + first[None] * back_ref[1] + slope[None] * solved_ref[...])


def column_tiles(parts, row_tiles, col_tiles, pairs):
    tiles = row_tiles + pairs

    def row(part, i):
        return part[tiles + i // 8, i % 8 : i % 8 + 1]

    halves = []
    for part in parts:
        for i in range(pairs):
            t = row_tiles + i
            value = jnp.concatenate([part[t], row(part, t), jnp.zeros((7, LANES), jnp.float32)], axis=0)
            halves.append((row(part, tiles + 1 + i), value))
    folded = []
    for group in range(2 * col_tiles):
        total = sum(jnp.where(ids == float(group), value, 0.0) for ids, value in halves)
        folded.append(total + pltpu.roll(total, CAM, 1))
    lower = lane_ids(16) < CAM
    return [jnp.where(lower, folded[2 * t], folded[2 * t + 1]) for t in range(col_tiles)]


def core_kernel(n_row, n_col, cams, radix, pairs, *refs):
    part_refs, out_refs, (whole_ref, ninth_ref) = refs[:radix], refs[radix:-2], refs[-2:]
    row_tiles = cams // n_row // LANES
    col_tiles = cams // n_col // LANES
    tiles = row_tiles + pairs
    low = n_row // radix
    row, col = lax.axis_index("row"), lax.axis_index("col")
    for v in range(whole_ref.shape[0]):
        parts = [ref[v] for ref in part_refs]
        sums = sum(part[tiles + tiles // 8, tiles % 8 : tiles % 8 + 1] for part in parts)
        whole_ref[v] = jnp.zeros(whole_ref.shape[1:], jnp.float32)
        ninth_ref[v] = jnp.zeros(ninth_ref.shape[1:], jnp.float32)
        for column, sources in ((col, parts[:1]), (col ^ 1, parts[1:])):
            for i, total in enumerate(column_tiles(sources, row_tiles, col_tiles, pairs)):
                whole_ref[v, column * col_tiles + i] = total[:8]
                ninth_ref[v, pl.ds(column * col_tiles + i, 1), :] = total[8:9]
        for digit, part in enumerate(parts):
            start = (row ^ (digit * low)) * row_tiles
            for i in range(row_tiles):
                whole_ref[v, start + i] += part[i]
                ninth_ref[v, pl.ds(start + i, 1), :] += part[tiles + i // 8, i % 8 : i % 8 + 1]
        for core, out_ref in zip((col % 2, 1 - col % 2), out_refs):
            places = [(2 * y + 1 - core) * col_tiles + i for y in range(n_col // 2) for i in range(col_tiles)]
            places += [(col // 2 * 2 + core) * col_tiles + i for i in range(col_tiles)]
            places += [row // low * (low * row_tiles) + i for i in range(low * row_tiles)]
            for i, t in enumerate(places):
                out_ref[v, i] = whole_ref[v, t]
            write_ninths(out_ref.at[v], len(places), [ninth_ref[v, pl.ds(t, 1), :] for t in places], sums)


def spread_kernel(n_row, n_col, cams, radix, masks, mine_ref, other_ref, *refs):
    out_refs, total_ref = refs[:-1], refs[-1]
    row_tiles = cams // n_row // LANES
    col_tiles = cams // n_col // LANES
    tiles = row_tiles + col_tiles
    low = n_row // radix
    col_sent = n_col // 2 * col_tiles
    sent = col_sent + col_tiles + low * row_tiles
    row, col = lax.axis_index("row") % low, lax.axis_index("col") // 2
    for v in range(total_ref.shape[0]):
        total = mine_ref[v] + other_ref[v]
        total_ref[v] = total
        sums = total[sent + sent // 8, sent % 8 : sent % 8 + 1]
        for mask, out_ref in zip(masks, out_refs):
            row_start = col_sent + col_tiles + (row ^ (mask // n_col)) * row_tiles
            col_start = (col ^ (mask % n_col // 2)) * col_tiles if mask else col_sent
            places = [row_start + i for i in range(row_tiles)] + [col_start + i for i in range(col_tiles)]
            for i, t in enumerate(places):
                out_ref[v, i] = total_ref[v, t]
            ninths = [total_ref[v, sent + t // 8, pl.ds(t % 8, 1), :] for t in places]
            write_ninths(out_ref.at[v], tiles, ninths, sums)


def exchange(x, masks, n_dev):
    return [lax.ppermute(x, AXES, [(i, i ^ mask) for i in range(n_dev)]) for mask in masks]


def in_vmem(x):
    return pltpu.with_memory_space_constraint(x, pltpu.VMEM)


def per_device(n_row, n_col, cam_jac, land_jac, resid, obs_cam, obs_land, pairs, cam_damp):
    f32 = jnp.float32
    count, _, obs = cam_jac.shape
    shard = cam_damp.shape[0]
    n_dev = n_row * n_col
    cams = shard * n_dev // 9
    row_tiles = cams // n_row // LANES
    col_tiles = cams // n_col // LANES
    tiles = row_tiles + col_tiles
    vmem = pl.BlockSpec(memory_space=pltpu.VMEM)
    smem = pl.BlockSpec(memory_space=pltpu.SMEM)

    def shape(*dims):
        return pltpu.VMEM(dims, f32)

    radix = min(n_row, 4)
    pair_tiles = (count + 1) // 2
    part_tiles = packed(row_tiles + pair_tiles, pair_tiles)
    low = n_row // radix
    sent = n_col // 2 * col_tiles + col_tiles + low * row_tiles
    lead = [digit * low * n_col + 1 for digit in range(1, radix)]
    middle = [x * n_col + y * 2 for x in range(low) for y in range(n_col // 2)]
    middle = middle[:1] + [mask + 1 for mask in middle[:0:-1]]

    def call(kernel, operands, out_shape, scratch=(), whole=(n_row, n_col, cams), specs=None, out_specs=None):
        return pl.pallas_call(
            functools.partial(kernel, *whole),
            out_shape=out_shape,
            in_specs=specs or [vmem] * len(operands),
            out_specs=out_specs or jax.tree.map(lambda _: vmem, out_shape),
            scratch_shapes=scratch,
        )(*operands)

    def all_reduce(part):
        vectors = part.shape[0]
        pieces = [part] + exchange(part, lead, n_dev)
        mine, other = call(
            core_kernel,
            tuple(map(in_vmem, pieces)),
            (shape(vectors, packed(sent), 8, LANES),) * 2,
            (pltpu.VMEM((vectors, cams // LANES, 8, LANES), f32), pltpu.VMEM((vectors, cams // LANES, LANES), f32)),
            (n_row, n_col, cams, radix, pair_tiles),
        )
        (other,) = exchange(other, [1], n_dev)
        to_send = call(
            spread_kernel,
            (in_vmem(mine), in_vmem(other)),
            (shape(vectors, packed(tiles), 8, LANES),) * len(middle),
            (pltpu.VMEM((vectors, packed(sent), 8, LANES), f32),),
            (n_row, n_col, cams, radix, tuple(middle)),
        )
        got = [to_send[0]] + [exchange(x, [mask], n_dev)[0] for x, mask in zip(to_send[1:], middle[1:])]
        return tuple(map(in_vmem, got))

    hot = pltpu.VMEM((count, obs, LANES), jnp.bfloat16)
    part, jac, cam_hot, land_hot, index, m, fac, damp_tile, select, spots = call(
        build_kernel,
        (
            pairs.T,
            jnp.transpose(cam_jac, (1, 0, 2)),
            jnp.transpose(land_jac, (1, 0, 2)),
            resid,
            obs_cam,
            obs_land,
            cam_damp,
        ),
        (
            shape(2, part_tiles, 8, LANES),
            shape(count, 2, 16, obs),
            hot,
            hot,
            pltpu.VMEM((2, count, obs), jnp.int32),
            shape(count, 8, obs),
            shape(count, 16, LM),
            shape(16, LANES),
            pltpu.VMEM((shard, LANES), jnp.bfloat16),
            pltpu.SMEM((4, count), jnp.int32),
        ),
        specs=[smem] + [vmem] * 6,
        out_specs=(vmem,) * 9 + (smem,),
    )
    sums = all_reduce(part)
    jac, cam_hot, land_hot, index, m, fac, damp_tile, select = map(
        in_vmem, (jac, cam_hot, land_hot, index, m, fac, damp_tile, select)
    )
    spots = pltpu.with_memory_space_constraint(spots, pltpu.SMEM)
    pieces = len(middle)
    vector = pltpu.VMEM((packed(tiles), 8, LANES), f32)
    part, back, right, precond = call(
        first_kernel,
        (spots, jac, cam_hot, land_hot, index, m, fac, damp_tile, *sums),
        (shape(1, part_tiles, 8, LANES), shape(2, 3, count, LM), vector, vector),
        (vector,),
        (n_row, n_col, cams, pieces),
        specs=[smem] + [vmem] * (7 + pieces),
    )
    image = all_reduce(part)
    partial, known, cam_flat, solved = call(
        second_kernel,
        (spots, jac, land_hot, index, m, fac, damp_tile, select, in_vmem(right), in_vmem(precond), *image),
        (shape(n_dev, 1, LANES), shape(8, LANES), shape(2, shard), shape(3, count, LM)),
        (vector, pltpu.VMEM((3, packed(tiles), 8, LANES), f32)),
        (n_row, n_col, cams, pieces),
        specs=[smem] + [vmem] * (9 + pieces),
    )
    gathered = lax.all_to_all(partial, AXES, 0, 0, tiled=True)
    cam_step, land_step = call(
        last_kernel,
        tuple(map(in_vmem, (gathered, known, cam_flat, back, solved))),
        (jax.ShapeDtypeStruct((shard,), f32), jax.ShapeDtypeStruct((3, count, LM), f32)),
        whole=(),
    )
    return cam_step, jnp.transpose(land_step, (1, 0, 2))


def solution(mesh):
    n_row, n_col = mesh.shape["row"], mesh.shape["col"]
    both = P(AXES)
    in_specs = (P(AXES, None, None),) * 3 + (P(AXES, None),) * 3 + (both,)
    out_specs = (both, P(AXES, None, None))
    return jax.shard_map(
        functools.partial(per_device, n_row, n_col),
        mesh=mesh,
        in_specs=in_specs,
        out_specs=out_specs,
        check_vma=False,
    )
```

```python
import functools

import jax
import jax.numpy as jnp
from jax import lax
from jax.experimental import pallas as pl
from jax.experimental.pallas import tpu as pltpu
from jax.sharding import PartitionSpec as P

CAM = 64
LM = 128
LANES = 128
AXES = ("row", "col")
DAMPING = 1.0

NN = (((1,), (0,)), ((), ()))
NT = (((1,), (1,)), ((), ()))


def split3(x):
    hi = x.astype(jnp.bfloat16)
    rest = x - hi.astype(jnp.float32)
    mid = rest.astype(jnp.bfloat16)
    low = (rest - mid.astype(jnp.float32)).astype(jnp.bfloat16)
    return jnp.concatenate([hi, mid, low], axis=0)


def dot3(x, exact, dims):
    n = x.shape[0]
    y = lax.dot_general(split3(x), exact, dims, preferred_element_type=jnp.float32)
    return (y[2 * n :] + y[n : 2 * n]) + y[:n]


def onehot(index_column, lanes):
    return jnp.where(index_column == lanes, jnp.bfloat16(1), jnp.bfloat16(0))


def take_lanes(x, index_row):
    pieces = []
    for start in range(0, index_row.shape[1], LANES):
        index = jnp.broadcast_to(index_row[:, start : start + LANES], x.shape)
        pieces.append(jnp.take_along_axis(x, index, axis=1, mode="promise_in_bounds"))
    return jnp.concatenate(pieces, axis=1)


def pad_rows(x, rows):
    if x.shape[0] == rows:
        return x
    return jnp.concatenate([x, jnp.zeros((rows - x.shape[0], x.shape[1]), x.dtype)], axis=0)


def stack_rows(rows, total):
    rows = list(rows)
    if len(rows) == total:
        return jnp.concatenate(rows, axis=0)
    rows.append(jnp.zeros((total - len(rows), rows[0].shape[1]), jnp.float32))
    return jnp.concatenate(rows, axis=0)


def cholesky_three(v00, v01, v02, v11, v12, v22):
    inv_first = 1.0 / jnp.sqrt(v00)
    low_one = v01 * inv_first
    low_two = v02 * inv_first
    inv_second = 1.0 / jnp.sqrt(v11 - low_one * low_one)
    low_three = (v12 - low_two * low_one) * inv_second
    inv_third = 1.0 / jnp.sqrt(v22 - low_two * low_two - low_three * low_three)
    return (inv_first, low_one, low_two, inv_second, low_three, inv_third)


def lower_solve(factor, first, second, third):
    out_one = first * factor[0]
    out_two = (second - factor[1] * out_one) * factor[3]
    out_three = (third - factor[2] * out_one - factor[4] * out_two) * factor[5]
    return (out_one, out_two, out_three)


def upper_solve(factor, first, second, third):
    out_three = third * factor[5]
    out_two = (second - factor[4] * out_three) * factor[3]
    out_one = (first - factor[1] * out_two - factor[2] * out_three) * factor[0]
    return (out_one, out_two, out_three)


def row_list(x, count):
    return [x[i : i + 1] for i in range(count)]


def lane_ids(rows):
    return lax.broadcasted_iota(jnp.int32, (rows, LANES), 1)


def to_first(x, half):
    return pltpu.roll(x, half * CAM, 1)


def to_second(x, half):
    return pltpu.roll(x, (1 - half) * CAM, 1)


def packed(tiles, more=0):
    return tiles + (tiles + more) // 8 + 1


def load_tile(ref, tiles, t):
    ninth = ref[tiles + t // 8, pl.ds(t % 8, 1), :]
    return jnp.concatenate([ref[t], ninth, jnp.zeros((7, LANES), jnp.float32)], axis=0)


def write_ninths(ref, tiles, rows, sums=None, more=()):
    rows = list(rows) + [jnp.zeros((1, LANES), jnp.float32) if sums is None else sums] + list(more)
    for start in range(0, len(rows), 8):
        ref[tiles + start // 8] = stack_rows(rows[start : start + 8], 8)


def shard_select(shard, lane_offset):
    entry = lax.broadcasted_iota(jnp.int32, (shard, LANES), 0)
    start = 9 * (lax.broadcasted_iota(jnp.int32, (shard, LANES), 1) - lane_offset)
    inside = (entry >= start) & (entry < start + 9)
    return jnp.where(inside, 1.0, 0.0).astype(jnp.bfloat16)


def param_mask(shard):
    entry = lax.broadcasted_iota(jnp.int32, (16, shard), 1).astype(jnp.float32)
    camera = jnp.floor((entry + 0.5) * (1.0 / 9.0))
    param = entry - 9.0 * camera
    return param == lax.broadcasted_iota(jnp.int32, (16, shard), 0).astype(jnp.float32)


def place(pairs_ref, k, n_row, n_col, groups):
    first = pairs_ref[0, k] - lax.axis_index("row") * (groups // n_row)
    second = pairs_ref[1, k] - lax.axis_index("col") * (groups // n_col)
    return first // 2, first % 2, second // 2, second % 2


def read_spots(spots_ref):
    return [[spots_ref[i, k] for i in range(4)] for k in range(spots_ref.shape[1])]


def write_parts(ref, row_tiles, spots, values, extra=None, sums=None):
    lower = lane_ids(values[0].shape[0]) < CAM
    firsts = [to_first(jnp.where(lower, v, 0.0), spot[1]) for v, spot in zip(values, spots)]
    tiles = []
    for t in range(row_tiles):
        items = [(spot[0] == t, v) for v, spot in zip(firsts, spots)]
        if extra is not None:
            items.append((extra[0] == t, extra[1]))
        tiles.append(sum(jnp.where(here, v, 0.0) for here, v in items))
    groups = []
    left = lane_ids(1) < CAM
    for k in range(0, len(values), 2):
        other = min(k + 1, len(values) - 1)
        second = values[other] if other > k else jnp.zeros_like(values[k])
        tiles.append(jnp.where(lower, pltpu.roll(values[k], CAM, 1), second))
        ids = [2 * spots[i][2] + spots[i][3] for i in (k, other)]
        groups.append(jnp.where(left, ids[0], ids[1]).astype(jnp.float32))
    for t, tile in enumerate(tiles):
        ref[t] = tile[:8]
    write_ninths(ref, len(tiles), [tile[8:9] for tile in tiles], sums, groups)


def own_place(n_row, n_col, cams):
    shard_cams = cams // (n_row * n_col)
    start = lax.axis_index("col") * shard_cams
    return start // LANES, start % LANES


def build_kernel(n_row, n_col, cams, pairs_ref, cam_ref, land_ref, resid_ref, ocam_ref, oland_ref, damp_ref, part_ref, jac_ref, cam_hot_ref, land_hot_ref, index_ref, m_ref, fac_ref, damp_tile_ref, select_ref, spots_ref):
    groups = cams // CAM
    row_tiles = cams // n_row // LANES
    tiles = row_tiles + cams // n_col // LANES
    count, obs = ocam_ref.shape
    each = range(count)
    shard = damp_ref.shape[0]

    index_ref[0] = ocam_ref[...]
    index_ref[1] = oland_ref[...]
    rows = jnp.concatenate([ocam_ref[...], oland_ref[...]], axis=0).astype(jnp.float32)
    columns = jnp.transpose(pad_rows(rows, (2 * count + 7) // 8 * 8)).astype(jnp.int32)
    key = (ocam_ref[...] * LM + oland_ref[...]).astype(jnp.int16)
    lanes = lax.broadcasted_iota(jnp.int32, (obs, LANES), 1).astype(jnp.int16)
    cam_columns = [columns[:, k : k + 1] for k in each]
    land_columns = [columns[:, count + k : count + k + 1] for k in each]
    for k in each:
        land_hot_ref[k] = onehot(land_columns[k].astype(jnp.int16), lanes)

    lj = [[land_ref[i, k : k + 1, :] for i in range(6)] for k in each]
    e0 = [resid_ref[k, 0:1, :] for k in each]
    e1 = [resid_ref[k, 1:2, :] for k in each]
    sums = []
    for k in each:

        def outer(i, j):
            return lj[k][i] * lj[k][j] + lj[k][3 + i] * lj[k][3 + j]

        entries = [outer(0, 0), outer(0, 1), outer(0, 2), outer(1, 1), outer(1, 2), outer(2, 2)]
        entries += [lj[k][b] * e0[k] + lj[k][3 + b] * e1[k] for b in range(3)]
        sums.append(dot3(stack_rows(entries, 16), land_hot_ref[k], NN))
    alike = []
    for k in each:
        for r in range(2):
            jac_ref[k, r, 0:8, :] = cam_ref[9 * r : 9 * r + 8, k, :]
            jac_ref[k, r, 8:16, :] = pad_rows(cam_ref[9 * r + 8 : 9 * r + 9, k, :], 8)
        j0, j1 = jac_ref[k, 0], jac_ref[k, 1]
        coupled = [j0[:8] * lj[k][b] + j1[:8] * lj[k][3 + b] for b in range(3)]
        coupled.append(stack_rows([j0[8:9] * lj[k][b] + j1[8:9] * lj[k][3 + b] for b in range(3)], 8))
        same = onehot((cam_columns[k] * LM + land_columns[k]).astype(jnp.int16), key[k : k + 1, :])
        alike.append(dot3(jnp.concatenate(coupled, axis=0), same, NN))
    total = [jnp.concatenate([sums[k][i : i + 1] for k in each], axis=0) for i in range(9)]
    factor = cholesky_three(
        total[0] + DAMPING, total[1], total[2], total[3] + DAMPING, total[4], total[5] + DAMPING
    )
    land_rows = list(factor) + list(lower_solve(factor, total[6], total[7], total[8]))
    for k in each:
        cam_hot_ref[k] = onehot(cam_columns[k].astype(jnp.int16), lanes)
    ms, ws = [], []
    for k in each:
        land_values = stack_rows([row[k : k + 1] for row in land_rows], 16)
        fac_ref[k] = land_values
        at_obs = row_list(take_lanes(land_values, oland_ref[k : k + 1, :]), 9)
        m0 = lower_solve(at_obs, lj[k][0], lj[k][1], lj[k][2])
        m1 = lower_solve(at_obs, lj[k][3], lj[k][4], lj[k][5])
        m_ref[k] = stack_rows(m0 + m1, 8)
        ms.append((at_obs, m0, m1))
        w0 = m0[0] * at_obs[6] + m0[1] * at_obs[7] + m0[2] * at_obs[8] - e0[k]
        w1 = m1[0] * at_obs[6] + m1[1] * at_obs[7] + m1[2] * at_obs[8] - e1[k]
        ws.append((w0, w1))
    both = []
    for k in each:
        j0, j1 = jac_ref[k, 0], jac_ref[k, 1]
        at_obs, m0, m1 = ms[k]
        squares = []
        for jr0, jr1, products in (
            (j0[:8], j1[:8], [alike[k][8 * b : 8 * b + 8] for b in range(3)]),
            (j0[8:9], j1[8:9], [alike[k][24 + b : 25 + b] for b in range(3)]),
        ):
            solved = lower_solve(at_obs, *products)
            squares.append(sum((jr0 * m0[b] + jr1 * m1[b]) * solved[b] for b in range(3)))
        diag = j0 * j0 + j1 * j1 - jnp.concatenate([squares[0], pad_rows(squares[1], 8)], axis=0)
        rhs = j0 * ws[k][0] + j1 * ws[k][1]
        both.append(dot3(jnp.concatenate([rhs, diag], axis=0), cam_hot_ref[k], NN))

    own_tile, own_lane = own_place(n_row, n_col, cams)
    spread = jnp.where(param_mask(shard), damp_ref[...].reshape(1, shard), 0.0)
    select = shard_select(shard, own_lane)
    select_ref[...] = select
    damp_tile = dot3(spread, select, NN)
    damp_tile_ref[...] = damp_tile
    spots = [place(pairs_ref, k, n_row, n_col, groups) for k in each]
    for k in each:
        for i in range(4):
            spots_ref[i, k] = spots[k][i]
    write_parts(part_ref.at[0], row_tiles, spots, [x[:16] for x in both])
    write_parts(part_ref.at[1], row_tiles, spots, [x[16:] for x in both], (own_tile, damp_tile))


def half_product(p_ref, row_tiles, tiles, spots, jac_ref, land_hot_ref, index_ref, m_ref):
    each = range(jac_ref.shape[0])
    lower = lane_ids(16) < CAM
    u, m, y_land = [], [], []
    for k in each:
        t_first, h_first, t_second, h_second = spots[k]
        p_first = to_first(load_tile(p_ref, tiles, t_first), h_first)
        p_second = to_second(load_tile(p_ref, tiles, row_tiles + t_second), h_second)
        at_obs = take_lanes(jnp.where(lower, p_first, p_second), index_ref[0, k : k + 1, :])
        u.append([jnp.sum(jac_ref[k, r] * at_obs, axis=0, keepdims=True) for r in range(2)])
    for k in each:
        m.append([m_ref[k, i : i + 1, :] for i in range(6)])
        y = [m[k][b] * u[k][0] + m[k][3 + b] * u[k][1] for b in range(3)]
        y_land.append(dot3(stack_rows(y, 16), land_hot_ref[k], NN)[:8])
    return u, m, y_land


def reduced_rows(u, m, y_land, index_ref):
    out = []
    for k in range(len(u)):
        y = row_list(take_lanes(y_land[k], index_ref[1, k : k + 1, :]), 3)
        out.append([u[k][r] - (m[k][3 * r] * y[0] + m[k][3 * r + 1] * y[1] + m[k][3 * r + 2] * y[2]) for r in range(2)])
    return out


def back_solve(fac_ref, k, rows):
    factor = row_list(fac_ref[k], 9)
    return upper_solve(factor, *rows), factor


def total_sum(x):
    return jnp.sum(jnp.sum(x, axis=0, keepdims=True), axis=1, keepdims=True)


def own_lanes(own_lane, shard_cams):
    ids = lane_ids(16)
    return (ids >= own_lane) & (ids < own_lane + shard_cams)


def in_lanes(values):
    ids = lane_ids(1)
    row = jnp.zeros((1, LANES), jnp.float32)
    for lane, value in enumerate(values):
        row = jnp.where(ids == lane, value, row)
    return row


def energy_sum(u, v):
    return total_sum(sum(u[k][r] * v[k][r] for k in range(len(u)) for r in range(2)))


def add_up(refs):
    total = refs[0][...]
    for ref in refs[1:]:
        total = total + ref[...]
    return total


def first_kernel(n_row, n_col, cams, pieces, spots_ref, jac_ref, cam_hot_ref, land_hot_ref, index_ref, m_ref, fac_ref, damp_tile_ref, *refs):
    part_ref, back_ref, right_ref, precond_ref, p_ref = refs[pieces:]
    row_tiles = cams // n_row // LANES
    tiles = row_tiles + cams // n_col // LANES
    each = range(jac_ref.shape[0])
    sums = add_up(refs[:pieces])
    right, precond = sums[0], 1.0 / sums[1]
    right_ref[...] = right
    precond_ref[...] = precond
    p_ref[...] = right * precond
    spots = read_spots(spots_ref)
    u, m, y_land = half_product(p_ref, row_tiles, tiles, spots, jac_ref, land_hot_ref, index_ref, m_ref)
    v = reduced_rows(u, m, y_land, index_ref)
    images = [dot3(jac_ref[k, 0] * v[k][0] + jac_ref[k, 1] * v[k][1], cam_hot_ref[k], NN) for k in each]
    own_tile, own_lane = own_place(n_row, n_col, cams)
    own = load_tile(p_ref, tiles, own_tile)
    damped = own * damp_tile_ref[...]
    mask = own_lanes(own_lane, cams // (n_row * n_col))
    norm_now = total_sum(jnp.where(mask, own * load_tile(right_ref, tiles, own_tile), 0.0))
    energy = energy_sum(u, v) + total_sum(own * damped)
    for k in each:
        solved, factor = back_solve(fac_ref, k, row_list(y_land[k], 3))
        from_t = upper_solve(factor, factor[6], factor[7], factor[8])
        for b in range(3):
            back_ref[0, b, k : k + 1, :] = from_t[b]
            back_ref[1, b, k : k + 1, :] = solved[b]
    write_parts(part_ref.at[0], row_tiles, spots, images, (own_tile, damped), in_lanes([norm_now, energy]))


def second_kernel(n_row, n_col, cams, pieces, spots_ref, jac_ref, land_hot_ref, index_ref, m_ref, fac_ref, damp_tile_ref, select_ref, right_ref, precond_ref, *refs):
    sums_ref, known_ref, cam_ref, solved_ref, p_ref, scratch_ref = refs[pieces:]
    row_tiles = cams // n_row // LANES
    tiles = row_tiles + cams // n_col // LANES
    each = range(jac_ref.shape[0])
    shard = cam_ref.shape[1]
    image = add_up(refs[:pieces])[0]
    sums = image[tiles + tiles // 8, tiles % 8 : tiles % 8 + 1]
    norm_now, energy_now = sums[:, 0:1], sums[:, 1:2]
    alpha = norm_now / energy_now
    for i, value in enumerate((1.0 / norm_now, energy_now, alpha)):
        known_ref[i : i + 1, :] = jnp.broadcast_to(value, (1, LANES))
    right, precond = right_ref[...], precond_ref[...]
    residual = right - alpha * image
    p_ref[...] = precond * residual
    scratch_ref[0] = right * precond
    scratch_ref[1] = residual
    scratch_ref[2] = image
    spots = read_spots(spots_ref)
    u, m, y_land = half_product(p_ref, row_tiles, tiles, spots, jac_ref, land_hot_ref, index_ref, m_ref)

    own_tile, own_lane = own_place(n_row, n_col, cams)
    own = load_tile(p_ref, tiles, own_tile)
    own_start, own_residual, own_image = [load_tile(scratch_ref.at[i], tiles, own_tile) for i in range(3)]
    flat = dot3(jnp.concatenate([own_start, own], axis=0), select_ref[...], NT)
    params = param_mask(shard)
    for i in range(2):
        cam_ref[i : i + 1, :] = jnp.sum(jnp.where(params, flat[16 * i : 16 * i + 16], 0.0), axis=0, keepdims=True)
    mask = own_lanes(own_lane, cams // (n_row * n_col))
    norm_next = total_sum(jnp.where(mask, own * own_residual, 0.0))
    cross = total_sum(jnp.where(mask, own * own_image, 0.0))
    energy = energy_sum(u, u) - total_sum(sum(y[:3] * y[:3] for y in y_land)) + total_sum(own * own * damp_tile_ref[...])
    sums_ref[...] = jnp.broadcast_to(in_lanes([energy, norm_next, cross])[None], sums_ref.shape)
    for k in each:
        solved, _ = back_solve(fac_ref, k, row_list(y_land[k], 3))
        for b in range(3):
            solved_ref[b, k : k + 1, :] = solved[b]


def last_kernel(sums_ref, known_ref, cam_ref, back_ref, solved_ref, cam_out_ref, land_out_ref):
    sums = jnp.sum(sums_ref[...], axis=0)
    energy, norm_next, cross = [jnp.broadcast_to(sums[:, i : i + 1], (1, LANES)) for i in range(3)]
    inverse_now, energy_now, alpha = [known_ref[i : i + 1, :] for i in range(3)]
    beta = norm_next * inverse_now
    slope = norm_next / (energy + beta * (2.0 * cross + beta * energy_now))
    first = alpha + slope * beta
    shard = cam_ref.shape[1]
    repeats = (shard + LANES - 1) // LANES
    first_wide, slope_wide = [jnp.concatenate([x] * repeats, axis=1)[:, :shard] for x in (first, slope)]
    cam_step = first_wide * cam_ref[0:1, :] + slope_wide * cam_ref[1:2, :]
    cam_out_ref[...] = cam_step.reshape(cam_out_ref.shape)
    land_out_ref[...] = -(back_ref[0] + first[None] * back_ref[1] + slope[None] * solved_ref[...])


def column_tiles(parts, row_tiles, col_tiles, pairs):
    tiles = row_tiles + pairs

    def row(part, i):
        return part[tiles + i // 8, i % 8 : i % 8 + 1]

    halves = []
    for part in parts:
        for i in range(pairs):
            t = row_tiles + i
            value = jnp.concatenate([part[t], row(part, t), jnp.zeros((7, LANES), jnp.float32)], axis=0)
            halves.append((row(part, tiles + 1 + i), value))
    folded = []
    for group in range(2 * col_tiles):
        total = sum(jnp.where(ids == float(group), value, 0.0) for ids, value in halves)
        folded.append(total + pltpu.roll(total, CAM, 1))
    lower = lane_ids(16) < CAM
    return [jnp.where(lower, folded[2 * t], folded[2 * t + 1]) for t in range(col_tiles)]


def kept_tiles(n_col, row_tiles, col_tiles, middle):
    ys = sorted({mask % n_col // 2 for mask in middle})
    rows = sorted({mask // n_col for mask in middle})
    return ys, rows, (len(ys) + 1) * col_tiles + len(rows) * row_tiles


def core_kernel(n_row, n_col, cams, lead, middle, pairs, *refs):
    part_refs, out_refs, (whole_ref, ninth_ref) = refs[: len(lead)], refs[len(lead) : -2], refs[-2:]
    row_tiles = cams // n_row // LANES
    col_tiles = cams // n_col // LANES
    tiles = row_tiles + pairs
    row, col = lax.axis_index("row"), lax.axis_index("col")
    ys, rows, sent = kept_tiles(n_col, row_tiles, col_tiles, middle)
    for v in range(whole_ref.shape[0]):
        parts = [ref[v] for ref in part_refs]
        sums = sum(part[tiles + tiles // 8, tiles % 8 : tiles % 8 + 1] for part in parts)
        whole_ref[v] = jnp.zeros(whole_ref.shape[1:], jnp.float32)
        ninth_ref[v] = jnp.zeros(ninth_ref.shape[1:], jnp.float32)
        by_column, by_row = {}, {}
        for mask, part in zip(lead, parts):
            by_column.setdefault(mask % n_col, []).append(part)
            by_row.setdefault(mask // n_col, []).append(part)
        for bits, sources in by_column.items():
            for i, total in enumerate(column_tiles(sources, row_tiles, col_tiles, pairs)):
                whole_ref[v, (col ^ bits) * col_tiles + i] = total[:8]
                ninth_ref[v, pl.ds((col ^ bits) * col_tiles + i, 1), :] = total[8:9]
        for bits, sources in by_row.items():
            total = sum(sources)
            start = (row ^ bits) * row_tiles
            for i in range(row_tiles):
                whole_ref[v, start + i] += total[i]
                ninth_ref[v, pl.ds(start + i, 1), :] += total[tiles + i // 8, i % 8 : i % 8 + 1]
        for core, out_ref in zip((col % 2, 1 - col % 2), out_refs):
            columns = [(col // 2 ^ y) * 2 + 1 - core for y in ys] + [col // 2 * 2 + core]
            places = [column * col_tiles + i for column in columns for i in range(col_tiles)]
            places += [(row ^ bits) * row_tiles + i for bits in rows for i in range(row_tiles)]
            for i, t in enumerate(places):
                out_ref[v, i] = whole_ref[v, t]
            write_ninths(out_ref.at[v], sent, [ninth_ref[v, pl.ds(t, 1), :] for t in places], sums)


def spread_kernel(n_row, n_col, cams, middle, mine_ref, other_ref, *out_refs):
    row_tiles = cams // n_row // LANES
    col_tiles = cams // n_col // LANES
    tiles = row_tiles + col_tiles
    ys, rows, sent = kept_tiles(n_col, row_tiles, col_tiles, middle)
    for v in range(mine_ref.shape[0]):
        total = mine_ref[v] + other_ref[v]

        def ninth(t):
            return total[sent + t // 8, t % 8 : t % 8 + 1]

        for mask, out_ref in zip(middle, out_refs):
            row_start = (len(ys) + 1) * col_tiles + rows.index(mask // n_col) * row_tiles
            col_start = (ys.index(mask % n_col // 2) if mask else len(ys)) * col_tiles
            places = [row_start + i for i in range(row_tiles)] + [col_start + i for i in range(col_tiles)]
            for i, t in enumerate(places):
                out_ref[v, i] = total[t]
            write_ninths(out_ref.at[v], tiles, [ninth(t) for t in places], ninth(sent))


def exchange(x, masks, n_dev):
    return [lax.ppermute(x, AXES, [(i, i ^ mask) for i in range(n_dev)]) for mask in masks]


def in_vmem(x):
    return pltpu.with_memory_space_constraint(x, pltpu.VMEM)


def per_device(n_row, n_col, cam_jac, land_jac, resid, obs_cam, obs_land, pairs, cam_damp):
    f32 = jnp.float32
    count, _, obs = cam_jac.shape
    shard = cam_damp.shape[0]
    n_dev = n_row * n_col
    cams = shard * n_dev // 9
    row_tiles = cams // n_row // LANES
    col_tiles = cams // n_col // LANES
    tiles = row_tiles + col_tiles
    vmem = pl.BlockSpec(memory_space=pltpu.VMEM)
    smem = pl.BlockSpec(memory_space=pltpu.SMEM)

    def shape(*dims):
        return pltpu.VMEM(dims, f32)

    pair_tiles = (count + 1) // 2
    part_tiles = packed(row_tiles + pair_tiles, pair_tiles)
    low = n_row // 4
    over_z = [0] + [z * low * n_col + 1 for z in range(1, 4)]
    over_xy = [x * n_col + y * 2 for x in range(low) for y in range(n_col // 2)]
    over_xy = [0] + [mask + 1 for mask in over_xy[1:]]

    def call(kernel, operands, out_shape, scratch=(), whole=(n_row, n_col, cams), specs=None, out_specs=None):
        return pl.pallas_call(
            functools.partial(kernel, *whole),
            out_shape=out_shape,
            in_specs=specs or [vmem] * len(operands),
            out_specs=out_specs or jax.tree.map(lambda _: vmem, out_shape),
            scratch_shapes=scratch,
        )(*operands)

    def all_reduce(part, lead, middle):
        vectors = part.shape[0]
        sent = kept_tiles(n_col, row_tiles, col_tiles, middle)[2]
        mine, other = call(
            core_kernel,
            tuple(map(in_vmem, [part] + exchange(part, lead[1:], n_dev))),
            (shape(vectors, packed(sent), 8, LANES),) * 2,
            (pltpu.VMEM((vectors, cams // LANES, 8, LANES), f32), pltpu.VMEM((vectors, cams // LANES, LANES), f32)),
            (n_row, n_col, cams, tuple(lead), tuple(middle), pair_tiles),
        )
        (other,) = exchange(other, [1], n_dev)
        to_send = call(
            spread_kernel,
            (in_vmem(mine), in_vmem(other)),
            (shape(vectors, packed(tiles), 8, LANES),) * len(middle),
            (),
            (n_row, n_col, cams, tuple(middle)),
        )
        got = [to_send[0]] + [exchange(x, [mask], n_dev)[0] for x, mask in zip(to_send[1:], middle[1:])]
        return tuple(map(in_vmem, got))

    hot = pltpu.VMEM((count, obs, LANES), jnp.bfloat16)
    part, jac, cam_hot, land_hot, index, m, fac, damp_tile, select, spots = call(
        build_kernel,
        (
            pairs.T,
            jnp.transpose(cam_jac, (1, 0, 2)),
            jnp.transpose(land_jac, (1, 0, 2)),
            resid,
            obs_cam,
            obs_land,
            cam_damp,
        ),
        (
            shape(2, part_tiles, 8, LANES),
            shape(count, 2, 16, obs),
            hot,
            hot,
            pltpu.VMEM((2, count, obs), jnp.int32),
            shape(count, 8, obs),
            shape(count, 16, LM),
            shape(16, LANES),
            pltpu.VMEM((shard, LANES), jnp.bfloat16),
            pltpu.SMEM((4, count), jnp.int32),
        ),
        specs=[smem] + [vmem] * 6,
        out_specs=(vmem,) * 9 + (smem,),
    )
    sums = all_reduce(part, over_z, over_xy[:1] + over_xy[:0:-1])
    jac, cam_hot, land_hot, index, m, fac, damp_tile, select = map(
        in_vmem, (jac, cam_hot, land_hot, index, m, fac, damp_tile, select)
    )
    spots = pltpu.with_memory_space_constraint(spots, pltpu.SMEM)
    vector = pltpu.VMEM((packed(tiles), 8, LANES), f32)
    part, back, right, precond = call(
        first_kernel,
        (spots, jac, cam_hot, land_hot, index, m, fac, damp_tile, *sums),
        (shape(1, part_tiles, 8, LANES), shape(2, 3, count, LM), vector, vector),
        (vector,),
        (n_row, n_col, cams, len(sums)),
        specs=[smem] + [vmem] * (7 + len(sums)),
    )
    image = all_reduce(part, over_z, over_xy[:1] + over_xy[:0:-1])
    partial, known, cam_flat, solved = call(
        second_kernel,
        (spots, jac, land_hot, index, m, fac, damp_tile, select, in_vmem(right), in_vmem(precond), *image),
        (shape(n_dev, 1, LANES), shape(8, LANES), shape(2, shard), shape(3, count, LM)),
        (vector, pltpu.VMEM((3, packed(tiles), 8, LANES), f32)),
        (n_row, n_col, cams, len(image)),
        specs=[smem] + [vmem] * (9 + len(image)),
    )
    gathered = lax.all_to_all(partial, AXES, 0, 0, tiled=True)
    cam_step, land_step = call(
        last_kernel,
        tuple(map(in_vmem, (gathered, known, cam_flat, back, solved))),
        (jax.ShapeDtypeStruct((shard,), f32), jax.ShapeDtypeStruct((3, count, LM), f32)),
        whole=(),
    )
    return cam_step, jnp.transpose(land_step, (1, 0, 2))


def solution(mesh):
    n_row, n_col = mesh.shape["row"], mesh.shape["col"]
    both = P(AXES)
    in_specs = (P(AXES, None, None),) * 3 + (P(AXES, None),) * 3 + (both,)
    out_specs = (both, P(AXES, None, None))
    return jax.shard_map(
        functools.partial(per_device, n_row, n_col),
        mesh=mesh,
        in_specs=in_specs,
        out_specs=out_specs,
        check_vma=False,
    )
```

```python
import functools

import jax
import jax.numpy as jnp
from jax import lax
from jax.experimental import pallas as pl
from jax.experimental.pallas import tpu as pltpu
from jax.sharding import PartitionSpec as P

CAM = 64
LM = 128
LANES = 128
AXES = ("row", "col")
DAMPING = 1.0

NN = (((1,), (0,)), ((), ()))
NT = (((1,), (1,)), ((), ()))


def split3(x):
    hi = x.astype(jnp.bfloat16)
    rest = x - hi.astype(jnp.float32)
    mid = rest.astype(jnp.bfloat16)
    low = (rest - mid.astype(jnp.float32)).astype(jnp.bfloat16)
    return jnp.concatenate([hi, mid, low], axis=0)


def dot3(x, exact, dims):
    n = x.shape[0]
    y = lax.dot_general(split3(x), exact, dims, preferred_element_type=jnp.float32)
    return (y[2 * n :] + y[n : 2 * n]) + y[:n]


def onehot(index_column, lanes):
    return jnp.where(index_column == lanes, jnp.bfloat16(1), jnp.bfloat16(0))


def take_lanes(x, index_row):
    pieces = []
    for start in range(0, index_row.shape[1], LANES):
        index = jnp.broadcast_to(index_row[:, start : start + LANES], x.shape)
        pieces.append(jnp.take_along_axis(x, index, axis=1, mode="promise_in_bounds"))
    return jnp.concatenate(pieces, axis=1)


def pad_rows(x, rows):
    if x.shape[0] == rows:
        return x
    return jnp.concatenate([x, jnp.zeros((rows - x.shape[0], x.shape[1]), x.dtype)], axis=0)


def stack_rows(rows, total):
    rows = list(rows)
    if len(rows) == total:
        return jnp.concatenate(rows, axis=0)
    rows.append(jnp.zeros((total - len(rows), rows[0].shape[1]), jnp.float32))
    return jnp.concatenate(rows, axis=0)


def cholesky_three(v00, v01, v02, v11, v12, v22):
    inv_first = 1.0 / jnp.sqrt(v00)
    low_one = v01 * inv_first
    low_two = v02 * inv_first
    inv_second = 1.0 / jnp.sqrt(v11 - low_one * low_one)
    low_three = (v12 - low_two * low_one) * inv_second
    inv_third = 1.0 / jnp.sqrt(v22 - low_two * low_two - low_three * low_three)
    return (inv_first, low_one, low_two, inv_second, low_three, inv_third)


def lower_solve(factor, first, second, third):
    out_one = first * factor[0]
    out_two = (second - factor[1] * out_one) * factor[3]
    out_three = (third - factor[2] * out_one - factor[4] * out_two) * factor[5]
    return (out_one, out_two, out_three)


def upper_solve(factor, first, second, third):
    out_three = third * factor[5]
    out_two = (second - factor[4] * out_three) * factor[3]
    out_one = (first - factor[1] * out_two - factor[2] * out_three) * factor[0]
    return (out_one, out_two, out_three)


def row_list(x, count):
    return [x[i : i + 1] for i in range(count)]


def lane_ids(rows):
    return lax.broadcasted_iota(jnp.int32, (rows, LANES), 1)


def to_first(x, half):
    return pltpu.roll(x, half * CAM, 1)


def to_second(x, half):
    return pltpu.roll(x, (1 - half) * CAM, 1)


def packed(tiles, more=0):
    return tiles + (tiles + more) // 8 + 1


def load_tile(ref, tiles, t):
    here = lax.broadcasted_iota(jnp.int32, (8, LANES), 0) == t % 8
    ninth = jnp.sum(jnp.where(here, ref[tiles + t // 8], 0.0), axis=0, keepdims=True)
    return jnp.concatenate([ref[t], ninth, jnp.zeros((7, LANES), jnp.float32)], axis=0)


def write_ninths(ref, tiles, rows, sums=None, more=()):
    rows = list(rows) + [jnp.zeros((1, LANES), jnp.float32) if sums is None else sums] + list(more)
    for start in range(0, len(rows), 8):
        ref[tiles + start // 8] = stack_rows(rows[start : start + 8], 8)


def shard_select(shard, lane_offset):
    entry = lax.broadcasted_iota(jnp.int32, (shard, LANES), 0)
    start = 9 * (lax.broadcasted_iota(jnp.int32, (shard, LANES), 1) - lane_offset)
    inside = (entry >= start) & (entry < start + 9)
    return jnp.where(inside, 1.0, 0.0).astype(jnp.bfloat16)


def param_mask(shard):
    entry = lax.broadcasted_iota(jnp.int32, (16, shard), 1).astype(jnp.float32)
    camera = jnp.floor((entry + 0.5) * (1.0 / 9.0))
    param = entry - 9.0 * camera
    return param == lax.broadcasted_iota(jnp.int32, (16, shard), 0).astype(jnp.float32)


def place(pairs_ref, k, n_row, n_col, groups):
    first = pairs_ref[0, k] - lax.axis_index("row") * (groups // n_row)
    second = pairs_ref[1, k] - lax.axis_index("col") * (groups // n_col)
    return first // 2, first % 2, second // 2, second % 2


def read_spots(spots_ref):
    return [[spots_ref[i, k] for i in range(4)] for k in range(spots_ref.shape[1])]


def write_parts(ref, row_tiles, spots, values, extra=None, sums=None):
    lower = lane_ids(values[0].shape[0]) < CAM
    firsts = [to_first(jnp.where(lower, v, 0.0), spot[1]) for v, spot in zip(values, spots)]
    tiles = []
    for t in range(row_tiles):
        items = [(spot[0] == t, v) for v, spot in zip(firsts, spots)]
        if extra is not None:
            items.append((extra[0] == t, extra[1]))
        tiles.append(sum(jnp.where(here, v, 0.0) for here, v in items))
    groups = []
    left = lane_ids(1) < CAM
    for k in range(0, len(values), 2):
        other = min(k + 1, len(values) - 1)
        second = values[other] if other > k else jnp.zeros_like(values[k])
        tiles.append(jnp.where(lower, pltpu.roll(values[k], CAM, 1), second))
        ids = [2 * spots[i][2] + spots[i][3] for i in (k, other)]
        groups.append(jnp.where(left, ids[0], ids[1]).astype(jnp.float32))
    for t, tile in enumerate(tiles):
        ref[t] = tile[:8]
    write_ninths(ref, len(tiles), [tile[8:9] for tile in tiles], sums, groups)


def own_place(n_row, n_col, cams):
    shard_cams = cams // (n_row * n_col)
    start = lax.axis_index("col") * shard_cams
    return start // LANES, start % LANES


def build_kernel(n_row, n_col, cams, pairs_ref, cam_ref, land_ref, resid_ref, ocam_ref, oland_ref, damp_ref, part_ref, jac_ref, cam_hot_ref, land_hot_ref, index_ref, m_ref, fac_ref, damp_tile_ref, select_ref, spots_ref):
    groups = cams // CAM
    row_tiles = cams // n_row // LANES
    tiles = row_tiles + cams // n_col // LANES
    count, obs = ocam_ref.shape
    each = range(count)
    shard = damp_ref.shape[0]

    index_ref[0] = ocam_ref[...]
    index_ref[1] = oland_ref[...]
    rows = jnp.concatenate([ocam_ref[...], oland_ref[...]], axis=0).astype(jnp.float32)
    columns = jnp.transpose(pad_rows(rows, (2 * count + 7) // 8 * 8)).astype(jnp.int32)
    key = (ocam_ref[...] * LM + oland_ref[...]).astype(jnp.int16)
    lanes = lax.broadcasted_iota(jnp.int32, (obs, LANES), 1).astype(jnp.int16)
    cam_columns = [columns[:, k : k + 1] for k in each]
    land_columns = [columns[:, count + k : count + k + 1] for k in each]
    for k in each:
        land_hot_ref[k] = onehot(land_columns[k].astype(jnp.int16), lanes)

    lj = [[land_ref[i, k : k + 1, :] for i in range(6)] for k in each]
    e0 = [resid_ref[k, 0:1, :] for k in each]
    e1 = [resid_ref[k, 1:2, :] for k in each]
    sums = []
    for k in each:

        def outer(i, j):
            return lj[k][i] * lj[k][j] + lj[k][3 + i] * lj[k][3 + j]

        entries = [outer(0, 0), outer(0, 1), outer(0, 2), outer(1, 1), outer(1, 2), outer(2, 2)]
        entries += [lj[k][b] * e0[k] + lj[k][3 + b] * e1[k] for b in range(3)]
        sums.append(dot3(stack_rows(entries, 16), land_hot_ref[k], NN))
    alike = []
    for k in each:
        for r in range(2):
            jac_ref[k, r, 0:8, :] = cam_ref[9 * r : 9 * r + 8, k, :]
            jac_ref[k, r, 8:16, :] = pad_rows(cam_ref[9 * r + 8 : 9 * r + 9, k, :], 8)
        j0, j1 = jac_ref[k, 0], jac_ref[k, 1]
        coupled = [j0[:8] * lj[k][b] + j1[:8] * lj[k][3 + b] for b in range(3)]
        coupled.append(stack_rows([j0[8:9] * lj[k][b] + j1[8:9] * lj[k][3 + b] for b in range(3)], 8))
        same = onehot((cam_columns[k] * LM + land_columns[k]).astype(jnp.int16), key[k : k + 1, :])
        alike.append(dot3(jnp.concatenate(coupled, axis=0), same, NN))
    total = [jnp.concatenate([sums[k][i : i + 1] for k in each], axis=0) for i in range(9)]
    factor = cholesky_three(
        total[0] + DAMPING, total[1], total[2], total[3] + DAMPING, total[4], total[5] + DAMPING
    )
    land_rows = list(factor) + list(lower_solve(factor, total[6], total[7], total[8]))
    for k in each:
        cam_hot_ref[k] = onehot(cam_columns[k].astype(jnp.int16), lanes)
    ms, ws = [], []
    for k in each:
        land_values = stack_rows([row[k : k + 1] for row in land_rows], 16)
        fac_ref[k] = land_values
        at_obs = row_list(take_lanes(land_values, oland_ref[k : k + 1, :]), 9)
        m0 = lower_solve(at_obs, lj[k][0], lj[k][1], lj[k][2])
        m1 = lower_solve(at_obs, lj[k][3], lj[k][4], lj[k][5])
        m_ref[k] = stack_rows(m0 + m1, 8)
        ms.append((at_obs, m0, m1))
        w0 = m0[0] * at_obs[6] + m0[1] * at_obs[7] + m0[2] * at_obs[8] - e0[k]
        w1 = m1[0] * at_obs[6] + m1[1] * at_obs[7] + m1[2] * at_obs[8] - e1[k]
        ws.append((w0, w1))
    both = []
    for k in each:
        j0, j1 = jac_ref[k, 0], jac_ref[k, 1]
        at_obs, m0, m1 = ms[k]
        squares = []
        for jr0, jr1, products in (
            (j0[:8], j1[:8], [alike[k][8 * b : 8 * b + 8] for b in range(3)]),
            (j0[8:9], j1[8:9], [alike[k][24 + b : 25 + b] for b in range(3)]),
        ):
            solved = lower_solve(at_obs, *products)
            squares.append(sum((jr0 * m0[b] + jr1 * m1[b]) * solved[b] for b in range(3)))
        diag = j0 * j0 + j1 * j1 - jnp.concatenate([squares[0], pad_rows(squares[1], 8)], axis=0)
        rhs = j0 * ws[k][0] + j1 * ws[k][1]
        both.append(dot3(jnp.concatenate([rhs, diag], axis=0), cam_hot_ref[k], NN))

    own_tile, own_lane = own_place(n_row, n_col, cams)
    spread = jnp.where(param_mask(shard), damp_ref[...].reshape(1, shard), 0.0)
    select = shard_select(shard, own_lane)
    select_ref[...] = select
    damp_tile = dot3(spread, select, NN)
    damp_tile_ref[...] = damp_tile
    spots = [place(pairs_ref, k, n_row, n_col, groups) for k in each]
    for k in each:
        for i in range(4):
            spots_ref[i, k] = spots[k][i]
    write_parts(part_ref.at[0], row_tiles, spots, [x[:16] for x in both])
    write_parts(part_ref.at[1], row_tiles, spots, [x[16:] for x in both], (own_tile, damp_tile))


def half_product(p_ref, row_tiles, tiles, spots, jac_ref, land_hot_ref, index_ref, m_ref):
    each = range(jac_ref.shape[0])
    lower = lane_ids(16) < CAM
    u, m, y_land = [], [], []
    for k in each:
        t_first, h_first, t_second, h_second = spots[k]
        p_first = to_first(load_tile(p_ref, tiles, t_first), h_first)
        p_second = to_second(load_tile(p_ref, tiles, row_tiles + t_second), h_second)
        at_obs = take_lanes(jnp.where(lower, p_first, p_second), index_ref[0, k : k + 1, :])
        u.append([jnp.sum(jac_ref[k, r] * at_obs, axis=0, keepdims=True) for r in range(2)])
    for k in each:
        m.append([m_ref[k, i : i + 1, :] for i in range(6)])
        y = [m[k][b] * u[k][0] + m[k][3 + b] * u[k][1] for b in range(3)]
        y_land.append(dot3(stack_rows(y, 16), land_hot_ref[k], NN)[:8])
    return u, m, y_land


def reduced_rows(u, m, y_land, index_ref):
    out = []
    for k in range(len(u)):
        y = row_list(take_lanes(y_land[k], index_ref[1, k : k + 1, :]), 3)
        out.append([u[k][r] - (m[k][3 * r] * y[0] + m[k][3 * r + 1] * y[1] + m[k][3 * r + 2] * y[2]) for r in range(2)])
    return out


def back_solve(fac_ref, k, rows):
    factor = row_list(fac_ref[k], 9)
    return upper_solve(factor, *rows), factor


def total_sum(x):
    return jnp.sum(jnp.sum(x, axis=0, keepdims=True), axis=1, keepdims=True)


def own_lanes(own_lane, shard_cams):
    ids = lane_ids(16)
    return (ids >= own_lane) & (ids < own_lane + shard_cams)


def in_lanes(values):
    ids = lane_ids(1)
    row = jnp.zeros((1, LANES), jnp.float32)
    for lane, value in enumerate(values):
        row = jnp.where(ids == lane, value, row)
    return row


def energy_sum(u, v):
    return total_sum(sum(u[k][r] * v[k][r] for k in range(len(u)) for r in range(2)))


def add_up(refs):
    total = refs[0][...]
    for ref in refs[1:]:
        total = total + ref[...]
    return total


def first_kernel(n_row, n_col, cams, pieces, spots_ref, jac_ref, cam_hot_ref, land_hot_ref, index_ref, m_ref, fac_ref, damp_tile_ref, *refs):
    part_ref, back_ref, right_ref, precond_ref, p_ref = refs[pieces:]
    row_tiles = cams // n_row // LANES
    tiles = row_tiles + cams // n_col // LANES
    each = range(jac_ref.shape[0])
    sums = add_up(refs[:pieces])
    right, precond = sums[0], 1.0 / sums[1]
    right_ref[...] = right
    precond_ref[...] = precond
    p_ref[...] = right * precond
    spots = read_spots(spots_ref)
    u, m, y_land = half_product(p_ref, row_tiles, tiles, spots, jac_ref, land_hot_ref, index_ref, m_ref)
    v = reduced_rows(u, m, y_land, index_ref)
    images = [dot3(jac_ref[k, 0] * v[k][0] + jac_ref[k, 1] * v[k][1], cam_hot_ref[k], NN) for k in each]
    own_tile, own_lane = own_place(n_row, n_col, cams)
    own = load_tile(p_ref, tiles, own_tile)
    damped = own * damp_tile_ref[...]
    mask = own_lanes(own_lane, cams // (n_row * n_col))
    norm_now = total_sum(jnp.where(mask, own * load_tile(right_ref, tiles, own_tile), 0.0))
    energy = energy_sum(u, v) + total_sum(own * damped)
    for k in each:
        solved, factor = back_solve(fac_ref, k, row_list(y_land[k], 3))
        from_t = upper_solve(factor, factor[6], factor[7], factor[8])
        for b in range(3):
            back_ref[0, b, k : k + 1, :] = from_t[b]
            back_ref[1, b, k : k + 1, :] = solved[b]
    write_parts(part_ref.at[0], row_tiles, spots, images, (own_tile, damped), in_lanes([norm_now, energy]))


def second_kernel(n_row, n_col, cams, pieces, spots_ref, jac_ref, land_hot_ref, index_ref, m_ref, fac_ref, damp_tile_ref, select_ref, right_ref, precond_ref, *refs):
    sums_ref, known_ref, cam_ref, solved_ref, p_ref, scratch_ref = refs[pieces:]
    row_tiles = cams // n_row // LANES
    tiles = row_tiles + cams // n_col // LANES
    each = range(jac_ref.shape[0])
    shard = cam_ref.shape[1]
    image = add_up(refs[:pieces])[0]
    sums = image[tiles + tiles // 8, tiles % 8 : tiles % 8 + 1]
    norm_now, energy_now = sums[:, 0:1], sums[:, 1:2]
    alpha = norm_now / energy_now
    for i, value in enumerate((1.0 / norm_now, energy_now, alpha)):
        known_ref[i : i + 1, :] = jnp.broadcast_to(value, (1, LANES))
    right, precond = right_ref[...], precond_ref[...]
    residual = right - alpha * image
    p_ref[...] = precond * residual
    scratch_ref[0] = right * precond
    scratch_ref[1] = residual
    scratch_ref[2] = image
    spots = read_spots(spots_ref)
    u, m, y_land = half_product(p_ref, row_tiles, tiles, spots, jac_ref, land_hot_ref, index_ref, m_ref)

    own_tile, own_lane = own_place(n_row, n_col, cams)
    own = load_tile(p_ref, tiles, own_tile)
    own_start, own_residual, own_image = [load_tile(scratch_ref.at[i], tiles, own_tile) for i in range(3)]
    flat = dot3(jnp.concatenate([own_start, own], axis=0), select_ref[...], NT)
    params = param_mask(shard)
    for i in range(2):
        cam_ref[i : i + 1, :] = jnp.sum(jnp.where(params, flat[16 * i : 16 * i + 16], 0.0), axis=0, keepdims=True)
    mask = own_lanes(own_lane, cams // (n_row * n_col))
    norm_next = total_sum(jnp.where(mask, own * own_residual, 0.0))
    cross = total_sum(jnp.where(mask, own * own_image, 0.0))
    energy = energy_sum(u, u) - total_sum(sum(y[:3] * y[:3] for y in y_land)) + total_sum(own * own * damp_tile_ref[...])
    sums_ref[...] = jnp.broadcast_to(in_lanes([energy, norm_next, cross])[None], sums_ref.shape)
    for k in each:
        solved, _ = back_solve(fac_ref, k, row_list(y_land[k], 3))
        for b in range(3):
            solved_ref[b, k : k + 1, :] = solved[b]


def last_kernel(sums_ref, known_ref, cam_ref, back_ref, solved_ref, cam_out_ref, land_out_ref):
    sums = jnp.sum(sums_ref[...], axis=0)
    energy, norm_next, cross = [jnp.broadcast_to(sums[:, i : i + 1], (1, LANES)) for i in range(3)]
    inverse_now, energy_now, alpha = [known_ref[i : i + 1, :] for i in range(3)]
    beta = norm_next * inverse_now
    slope = norm_next / (energy + beta * (2.0 * cross + beta * energy_now))
    first = alpha + slope * beta
    shard = cam_ref.shape[1]
    repeats = (shard + LANES - 1) // LANES
    first_wide, slope_wide = [jnp.concatenate([x] * repeats, axis=1)[:, :shard] for x in (first, slope)]
    cam_step = first_wide * cam_ref[0:1, :] + slope_wide * cam_ref[1:2, :]
    cam_out_ref[...] = cam_step.reshape(cam_out_ref.shape)
    land_out_ref[...] = -(back_ref[0] + first[None] * back_ref[1] + slope[None] * solved_ref[...])


def column_tiles(parts, row_tiles, col_tiles, pairs):
    tiles = row_tiles + pairs

    def row(part, i):
        return part[tiles + i // 8, i % 8 : i % 8 + 1]

    halves = [(row(part, tiles + 1 + i), part[row_tiles + i]) for part in parts for i in range(pairs)]
    ids = jnp.concatenate([group for group, _ in halves], axis=0)
    rows = jnp.concatenate([row(part, row_tiles + i) for part in parts for i in range(pairs)], axis=0)
    folded, ninths = [], []
    for group in range(2 * col_tiles):
        total = sum(jnp.where(group_row == float(group), value, 0.0) for group_row, value in halves)
        ninth = jnp.sum(jnp.where(ids == float(group), rows, 0.0), axis=0, keepdims=True)
        folded.append(total + pltpu.roll(total, CAM, 1))
        ninths.append(ninth + pltpu.roll(ninth, CAM, 1))
    lower = lane_ids(8) < CAM
    return [
        (jnp.where(lower, folded[2 * t], folded[2 * t + 1]), jnp.where(lower[:1], ninths[2 * t], ninths[2 * t + 1]))
        for t in range(col_tiles)
    ]


def kept_tiles(n_col, row_tiles, col_tiles, middle):
    ys = sorted({mask % n_col // 2 for mask in middle})
    rows = sorted({mask // n_col for mask in middle})
    return ys, rows, (len(ys) + 1) * col_tiles + len(rows) * row_tiles


def core_kernel(n_row, n_col, cams, lead, middle, pairs, *refs):
    part_refs, out_refs, (whole_ref, ninth_ref) = refs[: len(lead)], refs[len(lead) : -2], refs[-2:]
    row_tiles = cams // n_row // LANES
    col_tiles = cams // n_col // LANES
    tiles = row_tiles + pairs
    row, col = lax.axis_index("row"), lax.axis_index("col")
    ys, rows, sent = kept_tiles(n_col, row_tiles, col_tiles, middle)
    for v in range(whole_ref.shape[0]):
        parts = [ref[v] for ref in part_refs]
        sums = sum(part[tiles + tiles // 8, tiles % 8 : tiles % 8 + 1] for part in parts)
        whole_ref[v] = jnp.zeros(whole_ref.shape[1:], jnp.float32)
        ninth_ref[v] = jnp.zeros(ninth_ref.shape[1:], jnp.float32)
        by_column, by_row = {}, {}
        for mask, part in zip(lead, parts):
            by_column.setdefault(mask % n_col, []).append(part)
            by_row.setdefault(mask // n_col, []).append(part)
        for bits, sources in by_column.items():
            totals = column_tiles(sources, row_tiles, col_tiles, pairs)
            start = (col ^ bits) * col_tiles
            for i, total in enumerate(totals):
                whole_ref[v, start + i] = total[0]
            ninth_ref[v, pl.ds(start, col_tiles), :] = jnp.concatenate([total[1] for total in totals], axis=0)
        for bits, sources in by_row.items():
            total = sum(sources)
            start = (row ^ bits) * row_tiles
            for i in range(row_tiles):
                whole_ref[v, start + i] += total[i]
                ninth_ref[v, pl.ds(start + i, 1), :] += total[tiles + i // 8, i % 8 : i % 8 + 1]
        for core, out_ref in zip((col % 2, 1 - col % 2), out_refs):
            columns = [(col // 2 ^ y) * 2 + 1 - core for y in ys] + [col // 2 * 2 + core]
            runs = [(column * col_tiles, col_tiles) for column in columns]
            runs += [((row ^ bits) * row_tiles, row_tiles) for bits in rows]
            for i in range(sent, packed(sent)):
                out_ref[v, i] = jnp.zeros((8, LANES), jnp.float32)
            place = 0
            for start, length in runs:
                for i in range(length):
                    out_ref[v, place + i] = whole_ref[v, start + i]
                step = length if place % 8 + length <= 8 else 1
                for i in range(0, length, step):
                    at = place + i
                    out_ref[v, sent + at // 8, at % 8 : at % 8 + step, :] = ninth_ref[v, pl.ds(start + i, step), :]
                place += length
            out_ref[v, sent + sent // 8, sent % 8 : sent % 8 + 1, :] = sums


def spread_kernel(n_row, n_col, cams, middle, mine_ref, other_ref, *out_refs):
    row_tiles = cams // n_row // LANES
    col_tiles = cams // n_col // LANES
    tiles = row_tiles + col_tiles
    ys, rows, sent = kept_tiles(n_col, row_tiles, col_tiles, middle)
    for v in range(mine_ref.shape[0]):
        total = mine_ref[v] + other_ref[v]

        def ninth(t):
            return total[sent + t // 8, t % 8 : t % 8 + 1]

        for mask, out_ref in zip(middle, out_refs):
            row_start = (len(ys) + 1) * col_tiles + rows.index(mask // n_col) * row_tiles
            col_start = (ys.index(mask % n_col // 2) if mask else len(ys)) * col_tiles
            places = [row_start + i for i in range(row_tiles)] + [col_start + i for i in range(col_tiles)]
            for i, t in enumerate(places):
                out_ref[v, i] = total[t]
            write_ninths(out_ref.at[v], tiles, [ninth(t) for t in places], ninth(sent))


def exchange(x, masks, n_dev):
    return [lax.ppermute(x, AXES, [(i, i ^ mask) for i in range(n_dev)]) for mask in masks]


def in_vmem(x):
    return pltpu.with_memory_space_constraint(x, pltpu.VMEM)


def per_device(n_row, n_col, cam_jac, land_jac, resid, obs_cam, obs_land, pairs, cam_damp):
    f32 = jnp.float32
    count, _, obs = cam_jac.shape
    shard = cam_damp.shape[0]
    n_dev = n_row * n_col
    cams = shard * n_dev // 9
    row_tiles = cams // n_row // LANES
    col_tiles = cams // n_col // LANES
    tiles = row_tiles + col_tiles
    vmem = pl.BlockSpec(memory_space=pltpu.VMEM)
    smem = pl.BlockSpec(memory_space=pltpu.SMEM)

    def shape(*dims):
        return pltpu.VMEM(dims, f32)

    pair_tiles = (count + 1) // 2
    part_tiles = packed(row_tiles + pair_tiles, pair_tiles)
    low = n_row // 4
    over_z = [0] + [z * low * n_col + 1 for z in range(1, 4)]
    over_xy = [x * n_col + y * 2 for x in range(low) for y in range(n_col // 2)]
    over_xy = [0] + [mask + 1 for mask in over_xy[1:]]

    def call(kernel, operands, out_shape, scratch=(), whole=(n_row, n_col, cams), specs=None, out_specs=None):
        return pl.pallas_call(
            functools.partial(kernel, *whole),
            out_shape=out_shape,
            in_specs=specs or [vmem] * len(operands),
            out_specs=out_specs or jax.tree.map(lambda _: vmem, out_shape),
            scratch_shapes=scratch,
        )(*operands)

    def all_reduce(part, lead, middle):
        vectors = part.shape[0]
        sent = kept_tiles(n_col, row_tiles, col_tiles, middle)[2]
        mine, other = call(
            core_kernel,
            tuple(map(in_vmem, [part] + exchange(part, lead[1:], n_dev))),
            (shape(vectors, packed(sent), 8, LANES),) * 2,
            (pltpu.VMEM((vectors, cams // LANES, 8, LANES), f32), pltpu.VMEM((vectors, cams // LANES + 8, LANES), f32)),
            (n_row, n_col, cams, tuple(lead), tuple(middle), pair_tiles),
        )
        (other,) = exchange(other, [1], n_dev)
        to_send = call(
            spread_kernel,
            (in_vmem(mine), in_vmem(other)),
            (shape(vectors, packed(tiles), 8, LANES),) * len(middle),
            (),
            (n_row, n_col, cams, tuple(middle)),
        )
        got = [to_send[0]] + [exchange(x, [mask], n_dev)[0] for x, mask in zip(to_send[1:], middle[1:])]
        return tuple(map(in_vmem, got))

    hot = pltpu.VMEM((count, obs, LANES), jnp.bfloat16)
    part, jac, cam_hot, land_hot, index, m, fac, damp_tile, select, spots = call(
        build_kernel,
        (
            pairs.T,
            jnp.transpose(cam_jac, (1, 0, 2)),
            jnp.transpose(land_jac, (1, 0, 2)),
            resid,
            obs_cam,
            obs_land,
            cam_damp,
        ),
        (
            shape(2, part_tiles, 8, LANES),
            shape(count, 2, 16, obs),
            hot,
            hot,
            pltpu.VMEM((2, count, obs), jnp.int32),
            shape(count, 8, obs),
            shape(count, 16, LM),
            shape(16, LANES),
            pltpu.VMEM((shard, LANES), jnp.bfloat16),
            pltpu.SMEM((4, count), jnp.int32),
        ),
        specs=[smem] + [vmem] * 6,
        out_specs=(vmem,) * 9 + (smem,),
    )
    sums = all_reduce(part, over_z, over_xy[:1] + over_xy[:0:-1])
    jac, cam_hot, land_hot, index, m, fac, damp_tile, select = map(
        in_vmem, (jac, cam_hot, land_hot, index, m, fac, damp_tile, select)
    )
    spots = pltpu.with_memory_space_constraint(spots, pltpu.SMEM)
    vector = pltpu.VMEM((packed(tiles), 8, LANES), f32)
    part, back, right, precond = call(
        first_kernel,
        (spots, jac, cam_hot, land_hot, index, m, fac, damp_tile, *sums),
        (shape(1, part_tiles, 8, LANES), shape(2, 3, count, LM), vector, vector),
        (vector,),
        (n_row, n_col, cams, len(sums)),
        specs=[smem] + [vmem] * (7 + len(sums)),
    )
    image = all_reduce(part, over_z, over_xy[:1] + over_xy[:0:-1])
    partial, known, cam_flat, solved = call(
        second_kernel,
        (spots, jac, land_hot, index, m, fac, damp_tile, select, in_vmem(right), in_vmem(precond), *image),
        (shape(n_dev, 1, LANES), shape(8, LANES), shape(2, shard), shape(3, count, LM)),
        (vector, pltpu.VMEM((3, packed(tiles), 8, LANES), f32)),
        (n_row, n_col, cams, len(image)),
        specs=[smem] + [vmem] * (9 + len(image)),
    )
    gathered = lax.all_to_all(partial, AXES, 0, 0, tiled=True)
    cam_step, land_step = call(
        last_kernel,
        tuple(map(in_vmem, (gathered, known, cam_flat, back, solved))),
        (jax.ShapeDtypeStruct((shard,), f32), jax.ShapeDtypeStruct((3, count, LM), f32)),
        whole=(),
    )
    return cam_step, jnp.transpose(land_step, (1, 0, 2))


def solution(mesh):
    n_row, n_col = mesh.shape["row"], mesh.shape["col"]
    both = P(AXES)
    in_specs = (P(AXES, None, None),) * 3 + (P(AXES, None),) * 3 + (both,)
    out_specs = (both, P(AXES, None, None))
    return jax.shard_map(
        functools.partial(per_device, n_row, n_col),
        mesh=mesh,
        in_specs=in_specs,
        out_specs=out_specs,
        check_vma=False,
    )
```

```python
import functools

import jax
import jax.numpy as jnp
from jax import lax
from jax.experimental import pallas as pl
from jax.experimental.pallas import tpu as pltpu
from jax.sharding import PartitionSpec as P

CAM = 64
LM = 128
LANES = 128
AXES = ("row", "col")
DAMPING = 1.0

NN = (((1,), (0,)), ((), ()))
NT = (((1,), (1,)), ((), ()))


def split3(x):
    hi = x.astype(jnp.bfloat16)
    rest = x - hi.astype(jnp.float32)
    mid = rest.astype(jnp.bfloat16)
    low = (rest - mid.astype(jnp.float32)).astype(jnp.bfloat16)
    return jnp.concatenate([hi, mid, low], axis=0)


def dot3(x, exact, dims):
    n = x.shape[0]
    y = lax.dot_general(split3(x), exact, dims, preferred_element_type=jnp.float32)
    return (y[2 * n :] + y[n : 2 * n]) + y[:n]


def onehot(index_column, lanes):
    return jnp.where(index_column == lanes, jnp.bfloat16(1), jnp.bfloat16(0))


def take_lanes(x, index_row):
    pieces = []
    for start in range(0, index_row.shape[1], LANES):
        index = jnp.broadcast_to(index_row[:, start : start + LANES], x.shape)
        pieces.append(jnp.take_along_axis(x, index, axis=1, mode="promise_in_bounds"))
    return jnp.concatenate(pieces, axis=1)


def pad_rows(x, rows):
    if x.shape[0] == rows:
        return x
    return jnp.concatenate([x, jnp.zeros((rows - x.shape[0], x.shape[1]), x.dtype)], axis=0)


def stack_rows(rows, total):
    rows = list(rows)
    if len(rows) == total:
        return jnp.concatenate(rows, axis=0)
    rows.append(jnp.zeros((total - len(rows), rows[0].shape[1]), jnp.float32))
    return jnp.concatenate(rows, axis=0)


def cholesky_three(v00, v01, v02, v11, v12, v22):
    inv_first = 1.0 / jnp.sqrt(v00)
    low_one = v01 * inv_first
    low_two = v02 * inv_first
    inv_second = 1.0 / jnp.sqrt(v11 - low_one * low_one)
    low_three = (v12 - low_two * low_one) * inv_second
    inv_third = 1.0 / jnp.sqrt(v22 - low_two * low_two - low_three * low_three)
    return (inv_first, low_one, low_two, inv_second, low_three, inv_third)


def lower_solve(factor, first, second, third):
    out_one = first * factor[0]
    out_two = (second - factor[1] * out_one) * factor[3]
    out_three = (third - factor[2] * out_one - factor[4] * out_two) * factor[5]
    return (out_one, out_two, out_three)


def upper_solve(factor, first, second, third):
    out_three = third * factor[5]
    out_two = (second - factor[4] * out_three) * factor[3]
    out_one = (first - factor[1] * out_two - factor[2] * out_three) * factor[0]
    return (out_one, out_two, out_three)


def row_list(x, count):
    return [x[i : i + 1] for i in range(count)]


def lane_ids(rows):
    return lax.broadcasted_iota(jnp.int32, (rows, LANES), 1)


def to_first(x, half):
    return pltpu.roll(x, half * CAM, 1)


def to_second(x, half):
    return pltpu.roll(x, (1 - half) * CAM, 1)


def packed(tiles, more=0):
    return tiles + (tiles + more) // 8 + 1


def load_tile(ref, tiles, t):
    here = lax.broadcasted_iota(jnp.int32, (8, LANES), 0) == t % 8
    ninth = jnp.sum(jnp.where(here, ref[tiles + t // 8], 0.0), axis=0, keepdims=True)
    return jnp.concatenate([ref[t], ninth, jnp.zeros((7, LANES), jnp.float32)], axis=0)


def write_ninths(ref, tiles, rows, sums=None, more=()):
    rows = list(rows) + [jnp.zeros((1, LANES), jnp.float32) if sums is None else sums] + list(more)
    for start in range(0, len(rows), 8):
        ref[tiles + start // 8] = stack_rows(rows[start : start + 8], 8)


def shard_select(shard, lane_offset):
    entry = lax.broadcasted_iota(jnp.int32, (shard, LANES), 0)
    start = 9 * (lax.broadcasted_iota(jnp.int32, (shard, LANES), 1) - lane_offset)
    inside = (entry >= start) & (entry < start + 9)
    return jnp.where(inside, 1.0, 0.0).astype(jnp.bfloat16)


def param_mask(shard):
    entry = lax.broadcasted_iota(jnp.int32, (16, shard), 1).astype(jnp.float32)
    camera = jnp.floor((entry + 0.5) * (1.0 / 9.0))
    param = entry - 9.0 * camera
    return param == lax.broadcasted_iota(jnp.int32, (16, shard), 0).astype(jnp.float32)


def place(pairs_ref, k, n_row, n_col, groups):
    first = pairs_ref[0, k] - lax.axis_index("row") * (groups // n_row)
    second = pairs_ref[1, k] - lax.axis_index("col") * (groups // n_col)
    return first // 2, first % 2, second // 2, second % 2


def read_spots(spots_ref):
    return [[spots_ref[i, k] for i in range(4)] for k in range(spots_ref.shape[1])]


def write_parts(ref, row_tiles, spots, values, extra=None, sums=None):
    lower = lane_ids(values[0].shape[0]) < CAM
    firsts = [to_first(jnp.where(lower, v, 0.0), spot[1]) for v, spot in zip(values, spots)]
    tiles = []
    for t in range(row_tiles):
        items = [(spot[0] == t, v) for v, spot in zip(firsts, spots)]
        if extra is not None:
            items.append((extra[0] == t, extra[1]))
        tiles.append(sum(jnp.where(here, v, 0.0) for here, v in items))
    groups = []
    left = lane_ids(1) < CAM
    for k in range(0, len(values), 2):
        other = min(k + 1, len(values) - 1)
        second = values[other] if other > k else jnp.zeros_like(values[k])
        tiles.append(jnp.where(lower, pltpu.roll(values[k], CAM, 1), second))
        ids = [2 * spots[i][2] + spots[i][3] for i in (k, other)]
        groups.append(jnp.where(left, ids[0], ids[1]).astype(jnp.float32))
    for t, tile in enumerate(tiles):
        ref[t] = tile[:8]
    write_ninths(ref, len(tiles), [tile[8:9] for tile in tiles], sums, groups)


def own_place(n_row, n_col, cams):
    shard_cams = cams // (n_row * n_col)
    start = lax.axis_index("col") * shard_cams
    return start // LANES, start % LANES


def build_kernel(n_row, n_col, cams, pairs_ref, cam_ref, land_ref, resid_ref, ocam_ref, oland_ref, damp_ref, part_ref, jac_ref, cam_hot_ref, land_hot_ref, index_ref, m_ref, fac_ref, damp_tile_ref, select_ref, spots_ref):
    groups = cams // CAM
    row_tiles = cams // n_row // LANES
    tiles = row_tiles + cams // n_col // LANES
    count, obs = ocam_ref.shape
    each = range(count)
    shard = damp_ref.shape[0]

    index_ref[0] = ocam_ref[...]
    index_ref[1] = oland_ref[...]
    rows = jnp.concatenate([ocam_ref[...], oland_ref[...]], axis=0).astype(jnp.float32)
    columns = jnp.transpose(pad_rows(rows, (2 * count + 7) // 8 * 8)).astype(jnp.int32)
    key = (ocam_ref[...] * LM + oland_ref[...]).astype(jnp.int16)
    lanes = lax.broadcasted_iota(jnp.int32, (obs, LANES), 1).astype(jnp.int16)
    cam_columns = [columns[:, k : k + 1] for k in each]
    land_columns = [columns[:, count + k : count + k + 1] for k in each]
    for k in each:
        land_hot_ref[k] = onehot(land_columns[k].astype(jnp.int16), lanes)

    lj = [[land_ref[i, k : k + 1, :] for i in range(6)] for k in each]
    e0 = [resid_ref[k, 0:1, :] for k in each]
    e1 = [resid_ref[k, 1:2, :] for k in each]
    sums = []
    for k in each:

        def outer(i, j):
            return lj[k][i] * lj[k][j] + lj[k][3 + i] * lj[k][3 + j]

        entries = [outer(0, 0), outer(0, 1), outer(0, 2), outer(1, 1), outer(1, 2), outer(2, 2)]
        entries += [lj[k][b] * e0[k] + lj[k][3 + b] * e1[k] for b in range(3)]
        sums.append(dot3(stack_rows(entries, 16), land_hot_ref[k], NN))
    alike = []
    for k in each:
        for r in range(2):
            jac_ref[k, r, 0:8, :] = cam_ref[9 * r : 9 * r + 8, k, :]
            jac_ref[k, r, 8:16, :] = pad_rows(cam_ref[9 * r + 8 : 9 * r + 9, k, :], 8)
        j0, j1 = jac_ref[k, 0], jac_ref[k, 1]
        coupled = [j0[:8] * lj[k][b] + j1[:8] * lj[k][3 + b] for b in range(3)]
        coupled.append(stack_rows([j0[8:9] * lj[k][b] + j1[8:9] * lj[k][3 + b] for b in range(3)], 8))
        same = onehot((cam_columns[k] * LM + land_columns[k]).astype(jnp.int16), key[k : k + 1, :])
        alike.append(dot3(jnp.concatenate(coupled, axis=0), same, NN))
    total = [jnp.concatenate([sums[k][i : i + 1] for k in each], axis=0) for i in range(9)]
    factor = cholesky_three(
        total[0] + DAMPING, total[1], total[2], total[3] + DAMPING, total[4], total[5] + DAMPING
    )
    land_rows = list(factor) + list(lower_solve(factor, total[6], total[7], total[8]))
    for k in each:
        cam_hot_ref[k] = onehot(cam_columns[k].astype(jnp.int16), lanes)
    ms, ws = [], []
    for k in each:
        land_values = stack_rows([row[k : k + 1] for row in land_rows], 16)
        fac_ref[k] = land_values
        at_obs = row_list(take_lanes(land_values, oland_ref[k : k + 1, :]), 9)
        m0 = lower_solve(at_obs, lj[k][0], lj[k][1], lj[k][2])
        m1 = lower_solve(at_obs, lj[k][3], lj[k][4], lj[k][5])
        m_ref[k] = stack_rows(m0 + m1, 8)
        ms.append((at_obs, m0, m1))
        w0 = m0[0] * at_obs[6] + m0[1] * at_obs[7] + m0[2] * at_obs[8] - e0[k]
        w1 = m1[0] * at_obs[6] + m1[1] * at_obs[7] + m1[2] * at_obs[8] - e1[k]
        ws.append((w0, w1))
    both = []
    for k in each:
        j0, j1 = jac_ref[k, 0], jac_ref[k, 1]
        at_obs, m0, m1 = ms[k]
        squares = []
        for jr0, jr1, products in (
            (j0[:8], j1[:8], [alike[k][8 * b : 8 * b + 8] for b in range(3)]),
            (j0[8:9], j1[8:9], [alike[k][24 + b : 25 + b] for b in range(3)]),
        ):
            solved = lower_solve(at_obs, *products)
            squares.append(sum((jr0 * m0[b] + jr1 * m1[b]) * solved[b] for b in range(3)))
        diag = j0 * j0 + j1 * j1 - jnp.concatenate([squares[0], pad_rows(squares[1], 8)], axis=0)
        rhs = j0 * ws[k][0] + j1 * ws[k][1]
        both.append(dot3(jnp.concatenate([rhs, diag], axis=0), cam_hot_ref[k], NN))

    own_tile, own_lane = own_place(n_row, n_col, cams)
    spread = jnp.where(param_mask(shard), damp_ref[...].reshape(1, shard), 0.0)
    select = shard_select(shard, own_lane)
    select_ref[...] = select
    damp_tile = dot3(spread, select, NN)
    damp_tile_ref[...] = damp_tile
    spots = [place(pairs_ref, k, n_row, n_col, groups) for k in each]
    for k in each:
        for i in range(4):
            spots_ref[i, k] = spots[k][i]
    write_parts(part_ref.at[0], row_tiles, spots, [x[:16] for x in both])
    write_parts(part_ref.at[1], row_tiles, spots, [x[16:] for x in both], (own_tile, damp_tile))


def half_product(p_ref, row_tiles, tiles, spots, jac_ref, land_hot_ref, index_ref, m_ref):
    each = range(jac_ref.shape[0])
    lower = lane_ids(16) < CAM
    u, m, y_land = [], [], []
    for k in each:
        t_first, h_first, t_second, h_second = spots[k]
        p_first = to_first(load_tile(p_ref, tiles, t_first), h_first)
        p_second = to_second(load_tile(p_ref, tiles, row_tiles + t_second), h_second)
        at_obs = take_lanes(jnp.where(lower, p_first, p_second), index_ref[0, k : k + 1, :])
        u.append([jnp.sum(jac_ref[k, r] * at_obs, axis=0, keepdims=True) for r in range(2)])
    for k in each:
        m.append([m_ref[k, i : i + 1, :] for i in range(6)])
        y = [m[k][b] * u[k][0] + m[k][3 + b] * u[k][1] for b in range(3)]
        y_land.append(dot3(stack_rows(y, 16), land_hot_ref[k], NN)[:8])
    return u, m, y_land


def reduced_rows(u, m, y_land, index_ref):
    out = []
    for k in range(len(u)):
        y = row_list(take_lanes(y_land[k], index_ref[1, k : k + 1, :]), 3)
        out.append([u[k][r] - (m[k][3 * r] * y[0] + m[k][3 * r + 1] * y[1] + m[k][3 * r + 2] * y[2]) for r in range(2)])
    return out


def back_solve(fac_ref, k, rows):
    factor = row_list(fac_ref[k], 9)
    return upper_solve(factor, *rows), factor


def total_sum(x):
    return jnp.sum(jnp.sum(x, axis=0, keepdims=True), axis=1, keepdims=True)


def own_lanes(own_lane, shard_cams):
    ids = lane_ids(16)
    return (ids >= own_lane) & (ids < own_lane + shard_cams)


def in_lanes(values):
    ids = lane_ids(1)
    row = jnp.zeros((1, LANES), jnp.float32)
    for lane, value in enumerate(values):
        row = jnp.where(ids == lane, value, row)
    return row


def energy_sum(u, v):
    return total_sum(sum(u[k][r] * v[k][r] for k in range(len(u)) for r in range(2)))


def widen(x, n_row, n_col, row_tiles, col_tiles, mask):
    low, ratio = n_row // 4, col_tiles // row_tiles
    row, col = lax.axis_index("row"), lax.axis_index("col")
    place = shared_row(low, ratio, col, (row ^ (mask // n_col)) % low)
    held = 2 * row_tiles
    vectors = []
    for v in range(x.shape[0]):

        def ninth(t):
            return x[v, held + t // 8, t % 8 : t % 8 + 1]

        tiles = [x[v, i] for i in range(row_tiles)]
        rows = [ninth(i) for i in range(row_tiles)]
        for j in range(ratio):
            for i in range(row_tiles, held):
                tiles.append(jnp.where(place == j, x[v, i], 0.0))
                rows.append(jnp.where(place == j, ninth(i), 0.0))
        rows.append(ninth(held))
        tiles += [stack_rows(rows[start : start + 8], 8) for start in range(0, len(rows), 8)]
        vectors.append(jnp.stack(tiles))
    return jnp.stack(vectors)


def add_up(refs, n_row, n_col, cams, middle):
    row_tiles = cams // n_row // LANES
    col_tiles = cams // n_col // LANES
    total = refs[0][...]
    for mask, ref in zip(middle[1:], refs[1:]):
        piece = ref[...]
        if is_short(n_row, n_col, row_tiles, col_tiles, mask):
            piece = widen(piece, n_row, n_col, row_tiles, col_tiles, mask)
        total = total + piece
    return total


def first_kernel(n_row, n_col, cams, middle, spots_ref, jac_ref, cam_hot_ref, land_hot_ref, index_ref, m_ref, fac_ref, damp_tile_ref, *refs):
    part_ref, back_ref, right_ref, precond_ref, p_ref = refs[len(middle) :]
    row_tiles = cams // n_row // LANES
    tiles = row_tiles + cams // n_col // LANES
    each = range(jac_ref.shape[0])
    sums = add_up(refs[: len(middle)], n_row, n_col, cams, middle)
    right, precond = sums[0], 1.0 / sums[1]
    right_ref[...] = right
    precond_ref[...] = precond
    p_ref[...] = right * precond
    spots = read_spots(spots_ref)
    u, m, y_land = half_product(p_ref, row_tiles, tiles, spots, jac_ref, land_hot_ref, index_ref, m_ref)
    v = reduced_rows(u, m, y_land, index_ref)
    images = [dot3(jac_ref[k, 0] * v[k][0] + jac_ref[k, 1] * v[k][1], cam_hot_ref[k], NN) for k in each]
    own_tile, own_lane = own_place(n_row, n_col, cams)
    own = load_tile(p_ref, tiles, own_tile)
    damped = own * damp_tile_ref[...]
    mask = own_lanes(own_lane, cams // (n_row * n_col))
    norm_now = total_sum(jnp.where(mask, own * load_tile(right_ref, tiles, own_tile), 0.0))
    energy = energy_sum(u, v) + total_sum(own * damped)
    for k in each:
        solved, factor = back_solve(fac_ref, k, row_list(y_land[k], 3))
        from_t = upper_solve(factor, factor[6], factor[7], factor[8])
        for b in range(3):
            back_ref[0, b, k : k + 1, :] = from_t[b]
            back_ref[1, b, k : k + 1, :] = solved[b]
    write_parts(part_ref.at[0], row_tiles, spots, images, (own_tile, damped), in_lanes([norm_now, energy]))


def second_kernel(n_row, n_col, cams, middle, spots_ref, jac_ref, land_hot_ref, index_ref, m_ref, fac_ref, damp_tile_ref, select_ref, right_ref, precond_ref, *refs):
    sums_ref, known_ref, cam_ref, solved_ref, p_ref, scratch_ref = refs[len(middle) :]
    row_tiles = cams // n_row // LANES
    tiles = row_tiles + cams // n_col // LANES
    each = range(jac_ref.shape[0])
    shard = cam_ref.shape[1]
    image = add_up(refs[: len(middle)], n_row, n_col, cams, middle)[0]
    sums = image[tiles + tiles // 8, tiles % 8 : tiles % 8 + 1]
    norm_now, energy_now = sums[:, 0:1], sums[:, 1:2]
    alpha = norm_now / energy_now
    for i, value in enumerate((1.0 / norm_now, energy_now, alpha)):
        known_ref[i : i + 1, :] = jnp.broadcast_to(value, (1, LANES))
    right, precond = right_ref[...], precond_ref[...]
    residual = right - alpha * image
    p_ref[...] = precond * residual
    scratch_ref[0] = right * precond
    scratch_ref[1] = residual
    scratch_ref[2] = image
    spots = read_spots(spots_ref)
    u, m, y_land = half_product(p_ref, row_tiles, tiles, spots, jac_ref, land_hot_ref, index_ref, m_ref)

    own_tile, own_lane = own_place(n_row, n_col, cams)
    own = load_tile(p_ref, tiles, own_tile)
    own_start, own_residual, own_image = [load_tile(scratch_ref.at[i], tiles, own_tile) for i in range(3)]
    flat = dot3(jnp.concatenate([own_start, own], axis=0), select_ref[...], NT)
    params = param_mask(shard)
    for i in range(2):
        cam_ref[i : i + 1, :] = jnp.sum(jnp.where(params, flat[16 * i : 16 * i + 16], 0.0), axis=0, keepdims=True)
    mask = own_lanes(own_lane, cams // (n_row * n_col))
    norm_next = total_sum(jnp.where(mask, own * own_residual, 0.0))
    cross = total_sum(jnp.where(mask, own * own_image, 0.0))
    energy = energy_sum(u, u) - total_sum(sum(y[:3] * y[:3] for y in y_land)) + total_sum(own * own * damp_tile_ref[...])
    sums_ref[...] = jnp.broadcast_to(in_lanes([energy, norm_next, cross])[None], sums_ref.shape)
    for k in each:
        solved, _ = back_solve(fac_ref, k, row_list(y_land[k], 3))
        for b in range(3):
            solved_ref[b, k : k + 1, :] = solved[b]


def last_kernel(sums_ref, known_ref, cam_ref, back_ref, solved_ref, cam_out_ref, land_out_ref):
    sums = jnp.sum(sums_ref[...], axis=0)
    energy, norm_next, cross = [jnp.broadcast_to(sums[:, i : i + 1], (1, LANES)) for i in range(3)]
    inverse_now, energy_now, alpha = [known_ref[i : i + 1, :] for i in range(3)]
    beta = norm_next * inverse_now
    slope = norm_next / (energy + beta * (2.0 * cross + beta * energy_now))
    first = alpha + slope * beta
    shard = cam_ref.shape[1]
    repeats = (shard + LANES - 1) // LANES
    first_wide, slope_wide = [jnp.concatenate([x] * repeats, axis=1)[:, :shard] for x in (first, slope)]
    cam_step = first_wide * cam_ref[0:1, :] + slope_wide * cam_ref[1:2, :]
    cam_out_ref[...] = cam_step.reshape(cam_out_ref.shape)
    land_out_ref[...] = -(back_ref[0] + first[None] * back_ref[1] + slope[None] * solved_ref[...])


def column_tiles(parts, row_tiles, col_tiles, pairs):
    tiles = row_tiles + pairs

    def row(part, i):
        return part[tiles + i // 8, i % 8 : i % 8 + 1]

    halves = [(row(part, tiles + 1 + i), part[row_tiles + i]) for part in parts for i in range(pairs)]
    ids = jnp.concatenate([group for group, _ in halves], axis=0)
    rows = jnp.concatenate([row(part, row_tiles + i) for part in parts for i in range(pairs)], axis=0)
    folded, ninths = [], []
    for group in range(2 * col_tiles):
        total = sum(jnp.where(group_row == float(group), value, 0.0) for group_row, value in halves)
        ninth = jnp.sum(jnp.where(ids == float(group), rows, 0.0), axis=0, keepdims=True)
        folded.append(total + pltpu.roll(total, CAM, 1))
        ninths.append(ninth + pltpu.roll(ninth, CAM, 1))
    lower = lane_ids(8) < CAM
    return [
        (jnp.where(lower, folded[2 * t], folded[2 * t + 1]), jnp.where(lower[:1], ninths[2 * t], ninths[2 * t + 1]))
        for t in range(col_tiles)
    ]


def kept_tiles(n_col, row_tiles, col_tiles, middle):
    ys = sorted({mask % n_col // 2 for mask in middle})
    rows = sorted({mask // n_col for mask in middle})
    return ys, rows, (len(ys) + 1) * col_tiles + len(rows) * row_tiles


def core_kernel(n_row, n_col, cams, lead, middle, pairs, *refs):
    part_refs, out_refs, (whole_ref, ninth_ref) = refs[: len(lead)], refs[len(lead) : -2], refs[-2:]
    row_tiles = cams // n_row // LANES
    col_tiles = cams // n_col // LANES
    tiles = row_tiles + pairs
    row, col = lax.axis_index("row"), lax.axis_index("col")
    ys, rows, sent = kept_tiles(n_col, row_tiles, col_tiles, middle)
    for v in range(whole_ref.shape[0]):
        parts = [ref[v] for ref in part_refs]
        sums = sum(part[tiles + tiles // 8, tiles % 8 : tiles % 8 + 1] for part in parts)
        whole_ref[v] = jnp.zeros(whole_ref.shape[1:], jnp.float32)
        ninth_ref[v] = jnp.zeros(ninth_ref.shape[1:], jnp.float32)
        by_column, by_row = {}, {}
        for mask, part in zip(lead, parts):
            by_column.setdefault(mask % n_col, []).append(part)
            by_row.setdefault(mask // n_col, []).append(part)
        for bits, sources in by_column.items():
            totals = column_tiles(sources, row_tiles, col_tiles, pairs)
            start = (col ^ bits) * col_tiles
            for i, total in enumerate(totals):
                whole_ref[v, start + i] = total[0]
            ninth_ref[v, pl.ds(start, col_tiles), :] = jnp.concatenate([total[1] for total in totals], axis=0)
        for bits, sources in by_row.items():
            total = sum(sources)
            start = (row ^ bits) * row_tiles
            for i in range(row_tiles):
                whole_ref[v, start + i] += total[i]
                ninth_ref[v, pl.ds(start + i, 1), :] += total[tiles + i // 8, i % 8 : i % 8 + 1]
        for core, out_ref in zip((col % 2, 1 - col % 2), out_refs):
            columns = [(col // 2 ^ y) * 2 + 1 - core for y in ys] + [col // 2 * 2 + core]
            runs = [(column * col_tiles, col_tiles) for column in columns]
            runs += [((row ^ bits) * row_tiles, row_tiles) for bits in rows]
            for i in range(sent, packed(sent)):
                out_ref[v, i] = jnp.zeros((8, LANES), jnp.float32)
            place = 0
            for start, length in runs:
                for i in range(length):
                    out_ref[v, place + i] = whole_ref[v, start + i]
                step = length if place % 8 + length <= 8 else 1
                for i in range(0, length, step):
                    at = place + i
                    out_ref[v, sent + at // 8, at % 8 : at % 8 + step, :] = ninth_ref[v, pl.ds(start + i, step), :]
                place += length
            out_ref[v, sent + sent // 8, sent % 8 : sent % 8 + 1, :] = sums


def is_short(n_row, n_col, row_tiles, col_tiles, mask):
    return mask % n_col > 1 and col_tiles % row_tiles == 0 and col_tiles // row_tiles <= n_row // 4


def shared_row(low, ratio, column, digit):
    return (digit + low * ratio * column - ratio * column) % low


def spread_kernel(n_row, n_col, cams, middle, mine_ref, other_ref, *out_refs):
    row_tiles = cams // n_row // LANES
    col_tiles = cams // n_col // LANES
    tiles = row_tiles + col_tiles
    ys, rows, sent = kept_tiles(n_col, row_tiles, col_tiles, middle)
    low, ratio = n_row // 4, col_tiles // row_tiles
    row, col = lax.axis_index("row"), lax.axis_index("col")
    for v in range(mine_ref.shape[0]):
        total = mine_ref[v] + other_ref[v]

        def ninth(t):
            return total[sent + t // 8, t % 8 : t % 8 + 1]

        for mask, out_ref in zip(middle, out_refs):
            row_start = (len(ys) + 1) * col_tiles + rows.index(mask // n_col) * row_tiles
            col_start = (ys.index(mask % n_col // 2) if mask else len(ys)) * col_tiles
            places = [row_start + i for i in range(row_tiles)] + [col_start + i for i in range(col_tiles)]
            if not is_short(n_row, n_col, row_tiles, col_tiles, mask):
                for i, t in enumerate(places):
                    out_ref[v, i] = total[t]
                write_ninths(out_ref.at[v], tiles, [ninth(t) for t in places], ninth(sent))
                continue
            column = (col // 2 ^ (mask % n_col // 2)) * 2 + 1 - col % 2
            place = shared_row(low, ratio, column, row % low)
            ninths = []
            for i in range(2 * row_tiles):
                if i < row_tiles:
                    value, last = total[row_start + i], ninth(row_start + i)
                else:
                    starts = [col_start + j * row_tiles + i - row_tiles for j in range(ratio)]
                    value = sum(jnp.where(place == j, total[t], 0.0) for j, t in enumerate(starts))
                    last = sum(jnp.where(place == j, ninth(t), 0.0) for j, t in enumerate(starts))
                out_ref[v, i] = value
                ninths.append(last)
            write_ninths(out_ref.at[v], 2 * row_tiles, ninths, ninth(sent))


def exchange(x, masks, n_dev):
    return [lax.ppermute(x, AXES, [(i, i ^ mask) for i in range(n_dev)]) for mask in masks]


def in_vmem(x):
    return pltpu.with_memory_space_constraint(x, pltpu.VMEM)


def per_device(n_row, n_col, cam_jac, land_jac, resid, obs_cam, obs_land, pairs, cam_damp):
    f32 = jnp.float32
    count, _, obs = cam_jac.shape
    shard = cam_damp.shape[0]
    n_dev = n_row * n_col
    cams = shard * n_dev // 9
    row_tiles = cams // n_row // LANES
    col_tiles = cams // n_col // LANES
    tiles = row_tiles + col_tiles
    vmem = pl.BlockSpec(memory_space=pltpu.VMEM)
    smem = pl.BlockSpec(memory_space=pltpu.SMEM)

    def shape(*dims):
        return pltpu.VMEM(dims, f32)

    pair_tiles = (count + 1) // 2
    part_tiles = packed(row_tiles + pair_tiles, pair_tiles)
    low = n_row // 4
    over_z = [0] + [z * low * n_col + 1 for z in range(1, 4)]
    over_xy = [x * n_col + y * 2 for x in range(low) for y in range(n_col // 2)]
    over_xy = [0] + [mask + 1 for mask in over_xy[:0:-1]]

    def call(kernel, operands, out_shape, scratch=(), whole=(n_row, n_col, cams), specs=None, out_specs=None):
        return pl.pallas_call(
            functools.partial(kernel, *whole),
            out_shape=out_shape,
            in_specs=specs or [vmem] * len(operands),
            out_specs=out_specs or jax.tree.map(lambda _: vmem, out_shape),
            scratch_shapes=scratch,
        )(*operands)

    def all_reduce(part, lead, middle):
        vectors = part.shape[0]
        sent = kept_tiles(n_col, row_tiles, col_tiles, middle)[2]
        mine, other = call(
            core_kernel,
            tuple(map(in_vmem, [part] + exchange(part, lead[1:], n_dev))),
            (shape(vectors, packed(sent), 8, LANES),) * 2,
            (pltpu.VMEM((vectors, cams // LANES, 8, LANES), f32), pltpu.VMEM((vectors, cams // LANES + 8, LANES), f32)),
            (n_row, n_col, cams, tuple(lead), tuple(middle), pair_tiles),
        )
        (other,) = exchange(other, [1], n_dev)
        to_send = call(
            spread_kernel,
            (in_vmem(mine), in_vmem(other)),
            tuple(
                shape(vectors, packed(2 * row_tiles if is_short(n_row, n_col, row_tiles, col_tiles, mask) else tiles), 8, LANES)
                for mask in middle
            ),
            (),
            (n_row, n_col, cams, tuple(middle)),
        )
        got = [to_send[0]] + [exchange(x, [mask], n_dev)[0] for x, mask in zip(to_send[1:], middle[1:])]
        return tuple(map(in_vmem, got))

    hot = pltpu.VMEM((count, obs, LANES), jnp.bfloat16)
    part, jac, cam_hot, land_hot, index, m, fac, damp_tile, select, spots = call(
        build_kernel,
        (
            pairs.T,
            jnp.transpose(cam_jac, (1, 0, 2)),
            jnp.transpose(land_jac, (1, 0, 2)),
            resid,
            obs_cam,
            obs_land,
            cam_damp,
        ),
        (
            shape(2, part_tiles, 8, LANES),
            shape(count, 2, 16, obs),
            hot,
            hot,
            pltpu.VMEM((2, count, obs), jnp.int32),
            shape(count, 8, obs),
            shape(count, 16, LM),
            shape(16, LANES),
            pltpu.VMEM((shard, LANES), jnp.bfloat16),
            pltpu.SMEM((4, count), jnp.int32),
        ),
        specs=[smem] + [vmem] * 6,
        out_specs=(vmem,) * 9 + (smem,),
    )
    sums = all_reduce(part, over_z, over_xy)
    jac, cam_hot, land_hot, index, m, fac, damp_tile, select = map(
        in_vmem, (jac, cam_hot, land_hot, index, m, fac, damp_tile, select)
    )
    spots = pltpu.with_memory_space_constraint(spots, pltpu.SMEM)
    vector = pltpu.VMEM((packed(tiles), 8, LANES), f32)
    part, back, right, precond = call(
        first_kernel,
        (spots, jac, cam_hot, land_hot, index, m, fac, damp_tile, *sums),
        (shape(1, part_tiles, 8, LANES), shape(2, 3, count, LM), vector, vector),
        (vector,),
        (n_row, n_col, cams, tuple(over_xy)),
        specs=[smem] + [vmem] * (7 + len(sums)),
    )
    image = all_reduce(part, over_z, over_xy)
    partial, known, cam_flat, solved = call(
        second_kernel,
        (spots, jac, land_hot, index, m, fac, damp_tile, select, in_vmem(right), in_vmem(precond), *image),
        (shape(n_dev, 1, LANES), shape(8, LANES), shape(2, shard), shape(3, count, LM)),
        (vector, pltpu.VMEM((3, packed(tiles), 8, LANES), f32)),
        (n_row, n_col, cams, tuple(over_xy)),
        specs=[smem] + [vmem] * (9 + len(image)),
    )
    gathered = lax.all_to_all(partial, AXES, 0, 0, tiled=True)
    cam_step, land_step = call(
        last_kernel,
        tuple(map(in_vmem, (gathered, known, cam_flat, back, solved))),
        (jax.ShapeDtypeStruct((shard,), f32), jax.ShapeDtypeStruct((3, count, LM), f32)),
        whole=(),
    )
    return cam_step, jnp.transpose(land_step, (1, 0, 2))


def solution(mesh):
    n_row, n_col = mesh.shape["row"], mesh.shape["col"]
    both = P(AXES)
    in_specs = (P(AXES, None, None),) * 3 + (P(AXES, None),) * 3 + (both,)
    out_specs = (both, P(AXES, None, None))
    return jax.shard_map(
        functools.partial(per_device, n_row, n_col),
        mesh=mesh,
        in_specs=in_specs,
        out_specs=out_specs,
        check_vma=False,
    )
```
